32 devices in a mesh: det: 8 (over z, core), band: 4 (over y, x).
Axes of the slice: x: 2, y: 2, z: 4, core: 2. Of those that a mesh axis runs over, the one named last changes fastest.
Arguments:
- scan_lines: float32 [256, 4096], P(('det', 'band')), may hold values from -6 to 6
- response: float32 [256, 4096], P(('det', 'band')), may hold values from 0.02 to 1
- cycle_offset: int32 [256, 4096], P(('det', 'band')), may hold values from 0 to 255
- column: int32 [256, 4096], P(('det', 'band')), may hold values from 0 to 2047
- order_slot: int32 [256], replicated, may hold values from 0 to 255, each once
- legendre: float32 [256, 1024, 1024], P('det', 'band'), may hold values from -0.046875 to 0.046875
Outputs:
- harmonics: float32 [2, 256, 1024], P(None, 'det', 'band')
- sky_map: float32 [1024, 2048], P(('band', 'det'))
The draws below stay inside these ranges and needn't reach their ends.
Inputs may be any that keep to these rules, and one draw needn't show every extreme that they name: `order_slot`: each of the orders 0 to 255 stands in exactly one slot.
All inputs are finite; a program needn't handle non-finite values.
Results may differ from the reference program's by a relative error of at most 0.000073.
Values sent between devices are 32-bit elements; how exact they have to be, the bound alone decides.
No kernel may reach another device: no remote copies, remote signals or barrier semaphores. Data moves between devices by JAX's collectives and lax.ppermute only.
A program may use at most 128 MiB of HBM per device.

```python
import math
import jax
import jax.numpy as jnp
import numpy as np
from jax import lax

S = 4096
NRING = 1024
NPHI = 2048
MMAX = 256
LMAX = 1024
DET_DEV = 8
DETS = 256
RB = 256
N_BAND = 4


def with_ends(entries, own_key, smallest, top_value):
    longest = entries.shape.index(max(entries.shape))
    spots = []
    for shift in (0, 1):
        where = [jax.random.randint(jax.random.fold_in(own_key, axis), (), 0, length) for axis, length in enumerate(entries.shape)]
        where[longest] = (where[longest] + shift) % entries.shape[longest]
        spots.append(tuple(where))
    return entries.at[spots[0]].set(smallest).at[spots[1]].set(top_value)


def shard_levels(stream_key, shape, shards, smallest, high):
    def one(dim, parts):
        heights = jax.random.uniform(jax.random.fold_in(jax.random.fold_in(stream_key, 6), dim), (parts,), jnp.float32, smallest / len(shards), high / len(shards))
        return jnp.repeat(jnp.exp(heights), shape[dim] // parts).reshape((-1,) + (1,) * (len(shape) - dim - 1))

    level = one(*shards[0])
    for cut in shards[1:]:
        level = level * one(*cut)
    return level


def rank_bounds(count, slope):
    portions = [(1 << 20) // math.isqrt(rank ** slope) + 1 for rank in range(1, count + 1)]
    spread = 1 + sum(portions) // (1 << 30)
    return np.cumsum(np.array([max(1, weight // spread) for weight in portions]))


def ranked(own_key, extent, number_of, skew):
    listing = rank_bounds(number_of, skew)
    lot = jax.random.randint(jax.random.fold_in(own_key, 1), extent, 0, int(listing[number_of - 1]))
    grade = jnp.searchsorted(jnp.asarray(listing, jnp.int32), lot, side="right")
    return jax.random.permutation(jax.random.fold_in(own_key, 2), number_of)[grade].astype(jnp.int32)


def noise(stream_key, shape, scale, limit, split=(), kind=jnp.bfloat16):
    factor_of = shard_levels(stream_key, shape, split, -0.22, 0.18) if split else 1.0
    drawn = jax.random.normal(stream_key, shape, jnp.float32) * scale * factor_of
    return jnp.minimum(jnp.maximum(drawn, -limit), limit).astype(kind)


def setup_inputs(seed: int = 0) -> dict:
    seeds = jax.random.split(jax.random.key(seed), 7)
    scan_lines = noise(seeds[0], (DETS, S), 1.0, 6.0, ((0, 32),), jnp.float32)
    response = jnp.clip(jnp.exp(math.log(1.0) - 3.912023 * jax.random.uniform(seeds[1], (DETS, S), jnp.float32) ** shard_levels(seeds[1], (DETS, S), ((0, 32),), -0.2, 0.2)), 0.02, 1.0)
    cycle_offset = with_ends(jax.random.randint(seeds[2], (DETS, S), 0, RB), jax.random.fold_in(seeds[2], 1), 0, RB - 1).astype(jnp.int32)
    column = with_ends(ranked(seeds[3], (DETS, S), NPHI, 2), jax.random.fold_in(seeds[3], 3), 0, NPHI - 1).astype(jnp.int32)
    order_slot = jax.random.permutation(seeds[4], MMAX).astype(jnp.int32)
    legendre = noise(seeds[5], (MMAX, NRING, LMAX), (16 * NRING) ** -0.5, 0.046875, ((0, 8), (1, 4)), jnp.float32)
    return {"scan_lines": scan_lines, "response": response, "cycle_offset": cycle_offset, "column": column, "order_slot": order_slot, "legendre": legendre}


def reference(scan_lines, response, cycle_offset, column, order_slot, legendre):
    spectrum = jnp.fft.fft(scan_lines, axis=1) * response
    filtered = jnp.real(jnp.fft.ifft(spectrum, axis=1)).astype(jnp.float32)
    line_count = scan_lines.shape[0]
    band_cycles = NRING // N_BAND
    line_band = (jnp.arange(line_count, dtype=jnp.int32) // DET_DEV) % N_BAND
    cycle_index = line_band[:, None] * band_cycles + cycle_offset
    flat_index = (cycle_index * NPHI + column).reshape(-1)
    summed = jnp.zeros((NRING * NPHI,), jnp.float32).at[flat_index].add(filtered.reshape(-1))
    counts = jnp.zeros((NRING * NPHI,), jnp.float32).at[flat_index].add(1.0)
    sky_map = (summed / jnp.maximum(counts, 1.0)).reshape(NRING, NPHI)
    pixel_index = jnp.arange(NPHI, dtype=jnp.int32)[:, None]
    phases = (2.0 * jnp.pi / NPHI) * ((pixel_index * order_slot[None, :]) % NPHI).astype(jnp.float32)
    cycle_real = jnp.dot(sky_map, jnp.cos(phases), precision=lax.Precision.HIGHEST, preferred_element_type=jnp.float32)
    cycle_imag = -jnp.dot(sky_map, jnp.sin(phases), precision=lax.Precision.HIGHEST, preferred_element_type=jnp.float32)
    cycle_modes = jnp.stack([cycle_real, cycle_imag])
    degree_index = jnp.arange(LMAX, dtype=jnp.int32)
    keep_mask = (degree_index[None, :] >= order_slot[:, None]).astype(jnp.float32)
    harmonics = jnp.einsum("crs,srl->csl", cycle_modes, legendre, precision=lax.Precision.HIGHEST) * keep_mask[None]
    return harmonics, sky_map
```

```python
import functools

import jax
import jax.numpy as jnp
import numpy as np
from jax import lax
from jax.experimental import pallas as pl
from jax.experimental.pallas import tpu as pltpu
from jax.sharding import PartitionSpec as P

NPHI = 2048
LANES = 128
SUB = 8
WINDOWS = 2
ROW = 256

precise = lax.Precision.HIGHEST
NT = (((1,), (1,)), ((), ()))


def filter_tables(length):
    outer = length // LANES
    k1 = np.arange(outer)[:, None]
    n2 = np.arange(LANES)[None, :]
    turn = 2.0 * np.pi * ((k1 * n2) % length) / length
    twiddle = np.stack([np.cos(turn), np.sin(turn)])[:, :, None, :]
    a = np.arange(LANES)
    angle = 2.0 * np.pi * (np.outer(a, a) % LANES) / LANES
    c, s = np.cos(angle), np.sin(angle)
    forward = np.block([[c, -s], [s, c]])
    back = np.block([[c, s], [-s, c]])
    return (
        twiddle.astype(np.float32),
        forward.astype(np.float32),
        back.astype(np.float32),
    )


def mode_tables(count):
    half = NPHI // 2
    p = np.arange(half)[:, None]
    out = []
    for parity in (0, 1):
        m = 2 * np.arange(count // 2)[None, :] + parity
        angle = 2.0 * np.pi * ((p * m) % NPHI) / NPHI
        out.append(np.concatenate([np.cos(angle), -np.sin(angle)], axis=1))
    table = np.stack(out).astype(np.float32)
    high = table.astype(jnp.bfloat16)
    low = (table - high.astype(np.float32)).astype(jnp.bfloat16)
    return high, low


def small_fft(re, im, sign):
    count = len(re)
    if count == 1:
        return re, im
    even_re, even_im = small_fft(re[0::2], None if im is None else im[0::2], sign)
    odd_re, odd_im = small_fft(re[1::2], None if im is None else im[1::2], sign)
    half = count // 2
    out_re, out_im = [None] * count, [None] * count
    for k in range(half):
        wr = float(np.cos(2 * np.pi * k / count))
        wi = float(sign * np.sin(2 * np.pi * k / count))
        er, ei, orr, oi = even_re[k], even_im and even_im[k], odd_re[k], odd_im and odd_im[k]
        if k == 0:
            tr, ti = orr, oi
        elif 4 * k == count:
            tr = None if oi is None else -wi * oi
            ti = wi * orr
        elif oi is None:
            tr, ti = wr * orr, wi * orr
        else:
            tr, ti = wr * orr - wi * oi, wr * oi + wi * orr
        out_re[k] = er if tr is None else er + tr
        out_re[k + half] = er if tr is None else er - tr
        if ti is None:
            out_im[k] = out_im[k + half] = ei
        else:
            out_im[k] = ti if ei is None else ei + ti
            out_im[k + half] = -ti if ei is None else ei - ti
    if all(x is None for x in out_im):
        return out_re, None
    out_im = [jnp.zeros_like(out_re[0]) if x is None else x for x in out_im]
    return out_re, out_im


def partner(x, axis, distance):
    size = x.shape[axis]
    if 2 * distance == size:
        return pltpu.roll(x, distance, axis=axis)
    index = lax.broadcasted_iota(jnp.int32, x.shape, axis)
    upper = (index & distance) != 0
    return jnp.where(
        upper,
        pltpu.roll(x, distance, axis=axis),
        pltpu.roll(x, size - distance, axis=axis),
    )


def rank_bit(bit, tile_bits):
    shape = (SUB, LANES)
    if bit < tile_bits + 3:
        return (lax.broadcasted_iota(jnp.int32, shape, 0) & (1 << (bit - tile_bits))) != 0
    return (lax.broadcasted_iota(jnp.int32, shape, 1) & (1 << (bit - tile_bits - 3))) != 0


def sort_inner(key_ref, val_ref, level, tile_bits, total_bits, group):
    tiles = key_ref.shape[0]

    def body(g, carry):
        part = pl.ds(g * group, group)
        key, val = key_ref[part], val_ref[part]
        for bit in range(level - 1, tile_bits - 1, -1):
            if bit < tile_bits + 3:
                axis, distance = 1, 1 << (bit - tile_bits)
            else:
                axis, distance = 2, 1 << (bit - tile_bits - 3)
            want_max = rank_bit(bit, tile_bits)
            if level < total_bits:
                want_max = jnp.logical_xor(want_max, rank_bit(level, tile_bits))
            sign = jnp.where(want_max, -1.0, 1.0)[None]
            key_p, val_p = partner(key, axis, distance), partner(val, axis, distance)
            swap = (key - key_p) * sign > 0.0
            key = jnp.where(swap, key_p, key)
            val = jnp.where(swap, val_p, val)
        key_ref[part] = key
        val_ref[part] = val
        return carry

    lax.fori_loop(0, tiles // group, body, 0)


def exchange(keys, vals, a, b, down):
    swap = keys[a] > keys[b]
    if down is True:
        swap = keys[a] < keys[b]
    elif down is not False:
        swap = jnp.logical_xor(swap, down)
    keys[a], keys[b] = jnp.where(swap, keys[b], keys[a]), jnp.where(swap, keys[a], keys[b])
    vals[a], vals[b] = jnp.where(swap, vals[b], vals[a]), jnp.where(swap, vals[a], vals[b])


def sort_across(key_ref, val_ref, level, tile_bits, total_bits):
    tiles = key_ref.shape[0]
    top = min(level, tile_bits)
    bits = list(range(top - 1, -1, -1))
    passes = [bits[:-3], bits[-3:]] if len(bits) > 3 else [bits]
    for chosen in passes:
        low, span = min(chosen), len(chosen)
        members = 1 << span
        stride = 1 << low

        def run(base, static_base):
            keys = [key_ref[base + i * stride] for i in range(members)]
            vals = [val_ref[base + i * stride] for i in range(members)]
            for bit in chosen:
                step = 1 << (bit - low)
                for i in range(members):
                    if i & step:
                        continue
                    if level >= total_bits:
                        down = False
                    elif level < tile_bits:
                        down = ((static_base + i * stride) >> level) & 1 == 1
                    else:
                        down = rank_bit(level, tile_bits)
                    exchange(keys, vals, i, i + step, down)
            for i in range(members):
                key_ref[base + i * stride] = keys[i]
                val_ref[base + i * stride] = vals[i]

        def base_of(g):
            return (g // stride) * (members * stride) + g % stride

        groups = tiles // members
        if level < tile_bits:
            for g in range(groups):
                run(base_of(g), base_of(g))
        else:
            for g in range(groups):
                run(base_of(g), None)


def sort_kernel(
    scan_ref, resp_ref, cycle_ref, column_ref, twiddle_ref, forward_ref, back_ref,
    filtered_ref, send_ref, flag_ref,
    key_ref, val_ref, spec_ref, key_rows, val_rows,
    *, buckets, span, rows, windows,
):
    lines, length = scan_ref.shape
    outer = length // LANES
    re, im = small_fft([scan_ref[:, n * LANES:(n + 1) * LANES] for n in range(outer)], None, -1)
    for k in range(outer):
        c, s = twiddle_ref[0, k], twiddle_ref[1, k]
        here = pl.ds(k * lines, lines)
        spec_ref[here, :LANES] = re[k] * c + im[k] * s
        spec_ref[here, LANES:] = im[k] * c - re[k] * s
    spec = jnp.dot(spec_ref[...], forward_ref[...], precision=precise, preferred_element_type=jnp.float32)
    resp = resp_ref[...] * (1.0 / length)
    spec = spec * jnp.concatenate([resp, resp], axis=1)
    spec_ref[...] = jnp.dot(spec, back_ref[...], precision=precise, preferred_element_type=jnp.float32)
    re, im = [], []
    for k in range(outer):
        c, s = twiddle_ref[0, k], twiddle_ref[1, k]
        here = pl.ds(k * lines, lines)
        ur, ui = spec_ref[here, :LANES], spec_ref[here, LANES:]
        re.append(ur * c - ui * s)
        im.append(ui * c + ur * s)
    out, _ = small_fft(re, im, 1)
    for n in range(outer):
        cols = slice(n * LANES, (n + 1) * LANES)
        filtered_ref[:, cols] = out[n]
        val_ref[n] = out[n]
        key_ref[n] = (cycle_ref[:, cols] * NPHI + column_ref[:, cols]).astype(jnp.float32)
    tiles = outer
    tile_bits = tiles.bit_length() - 1
    total_bits = tile_bits + 10
    for level in range(1, total_bits + 1):
        if level > tile_bits:
            sort_inner(key_ref, val_ref, level, tile_bits, total_bits, min(16, tiles))
        sort_across(key_ref, val_ref, level, tile_bits, total_bits)
    keys = key_ref[...]
    last = jnp.max(jnp.max(keys, axis=0), axis=0, keepdims=True)
    first = jnp.min(jnp.min(keys, axis=0), axis=0, keepdims=True)
    row_len = tiles * SUB
    key_rows[:LANES, :] = keys.reshape(row_len, LANES).T
    val_rows[:LANES, :] = val_ref[...].reshape(row_len, LANES).T
    reach = key_rows.shape[0] - LANES
    key_rows[LANES:, :] = jnp.full((reach, row_len), 2.0 * buckets * span, jnp.float32)
    val_rows[LANES:, :] = jnp.zeros((reach, row_len), jnp.float32)
    over = jnp.int32(0)
    for b in range(buckets):
        begin = jnp.sum((last < float(b * span)).astype(jnp.float32)).astype(jnp.int32)
        end = jnp.sum((first < float((b + 1) * span)).astype(jnp.float32)).astype(jnp.int32)
        over = over + (end - begin > rows).astype(jnp.int32)
        begin = jnp.minimum(begin, LANES)
        aligned = pl.multiple_of((begin // SUB) * SUB, SUB)
        back = lax.rem(reach - (begin - aligned), reach)
        here = pl.ds(aligned, reach)
        dest, w = divmod(b, windows)
        taken = pltpu.roll(key_rows[here, :], back, axis=0)[:rows]
        send_ref[dest, w * rows:(w + 1) * rows, :] = taken - float(b * span)
        at = (windows + w) * rows
        send_ref[dest, at:at + rows, :] = pltpu.roll(val_rows[here, :], back, axis=0)[:rows]
    flag_ref[0, 0] = over


def filter_and_sort(scan, resp, cycle, column, det_count, band_cycles):
    lines, length = scan.shape
    tiles = length // LANES
    windows = WINDOWS
    buckets = det_count * windows
    span = band_cycles * NPHI // buckets
    row_len = tiles * SUB
    rows = LANES // buckets + 2
    reach = (rows + 2 * SUB - 2) // SUB * SUB
    twiddle, forward, back = filter_tables(length)
    resp_rows = resp.reshape(lines, LANES, tiles).transpose(2, 0, 1).reshape(tiles * lines, LANES)
    body = functools.partial(sort_kernel, buckets=buckets, span=span, rows=rows, windows=windows)
    vmem = pl.BlockSpec(memory_space=pltpu.VMEM)
    return pl.pallas_call(
        body,
        out_shape=(
            jax.ShapeDtypeStruct((lines, length), jnp.float32),
            jax.ShapeDtypeStruct((det_count, 2 * windows * rows, row_len), jnp.float32),
            jax.ShapeDtypeStruct((1, 1), jnp.int32),
        ),
        in_specs=[vmem] * 7,
        out_specs=(vmem, vmem, pl.BlockSpec(memory_space=pltpu.SMEM)),
        scratch_shapes=[
            pltpu.VMEM((tiles, SUB, LANES), jnp.float32),
            pltpu.VMEM((tiles, SUB, LANES), jnp.float32),
            pltpu.VMEM((tiles * lines, 2 * LANES), jnp.float32),
            pltpu.VMEM((LANES + reach, row_len), jnp.float32),
            pltpu.VMEM((LANES + reach, row_len), jnp.float32),
        ],
        compiler_params=pltpu.CompilerParams(vmem_limit_bytes=24 * 1024 * 1024),
        name="filter_sort",
    )(scan, resp_rows, cycle, column, jnp.asarray(twiddle), jnp.asarray(forward), jnp.asarray(back))


def split2(x):
    high = x.astype(jnp.bfloat16)
    low = (x - high.astype(jnp.float32)).astype(jnp.bfloat16)
    return high, low


def bin_kernel(recv_ref, pick_ref, table_hi, table_lo, map_ref, send_ref, *, windows, rows, window_cycles):
    sources = recv_ref.shape[0]
    row_len = recv_ref.shape[2]
    parts = NPHI // ROW
    area = parts * window_cycles
    for w in range(windows):
        def body(e, acc):
            left, right = [], []
            a_iota = lax.broadcasted_iota(jnp.int32, (area, row_len), 0)
            b_iota = lax.broadcasted_iota(jnp.int32, (ROW, row_len), 0)
            for r in range(rows):
                q = recv_ref[e, w * rows + r:w * rows + r + 1, :].astype(jnp.int32)
                v = recv_ref[e, (windows + w) * rows + r:(windows + w) * rows + r + 1, :]
                high, low = split2(v)
                cycle = q >> 11
                inside = (q >= 0) & (cycle < window_cycles)
                a = jnp.where(inside, ((q >> 8) & (parts - 1)) * window_cycles + cycle, -1)
                hit_a = a_iota == a
                zero = jnp.zeros((), jnp.float32)
                left.append(jnp.concatenate([
                    jnp.where(hit_a, high.astype(jnp.float32), zero).astype(jnp.bfloat16),
                    jnp.where(hit_a, low.astype(jnp.float32), zero).astype(jnp.bfloat16),
                    jnp.where(hit_a, 1.0, zero).astype(jnp.bfloat16),
                ], axis=0))
                right.append(jnp.where(b_iota == (q & (ROW - 1)), 1.0, zero).astype(jnp.bfloat16))
            return acc + lax.dot_general(
                jnp.concatenate(left, axis=1), jnp.concatenate(right, axis=1), NT,
                preferred_element_type=jnp.float32,
            )

        acc = lax.fori_loop(0, sources, body, jnp.zeros((3 * area, ROW), jnp.float32))
        sky = (acc[:area] + acc[area:2 * area]) / jnp.maximum(acc[2 * area:], 1.0)
        for c8 in range(parts):
            map_ref[w * window_cycles:(w + 1) * window_cycles, c8 * ROW:(c8 + 1) * ROW] = (
                sky[c8 * window_cycles:(c8 + 1) * window_cycles]
            )
    cycles = map_ref.shape[0]
    half = NPHI // 2
    modes = []
    for parity in (0, 1):
        a, b = map_ref[:, :half], map_ref[:, half:]
        high, low = split2(a + b if parity == 0 else a - b)
        first = jnp.dot(jnp.concatenate([high, low], axis=0), table_hi[parity], preferred_element_type=jnp.float32)
        second = jnp.dot(high, table_lo[parity], preferred_element_type=jnp.float32)
        modes.append(first[:cycles] + first[cycles:] + second)
    modes = jnp.concatenate(modes, axis=1)
    count = modes.shape[1]
    width = pick_ref.shape[1]
    high = modes.astype(jnp.bfloat16)
    rest = modes - high.astype(jnp.float32)
    middle = rest.astype(jnp.bfloat16)
    low = (rest - middle.astype(jnp.float32)).astype(jnp.bfloat16)
    pieces = jnp.concatenate([high, middle, low], axis=0)
    choose = (lax.broadcasted_iota(jnp.int32, (count, width), 0) == pick_ref[...])
    choose = jnp.where(choose, 1.0, 0.0).astype(jnp.bfloat16)
    moved = jnp.dot(pieces, choose, preferred_element_type=jnp.float32)
    moved = moved[:cycles] + moved[cycles:2 * cycles] + moved[2 * cycles:]
    owners, group_rows, lanes = send_ref.shape
    groups = cycles // group_rows
    lane_group = lax.broadcasted_iota(jnp.int32, (group_rows, lanes), 1) // (lanes // groups)
    for d in range(owners):
        block = moved[:, d * lanes:(d + 1) * lanes]
        out = block[:group_rows]
        for h in range(1, groups):
            out = jnp.where(lane_group == h, block[h * group_rows:(h + 1) * group_rows], out)
        send_ref[d] = out


def bin_and_modes(recv, order_slot, band_cycles):
    sources, lines, row_len = recv.shape
    windows = WINDOWS
    rows = lines // (2 * windows)
    cycles = band_cycles // sources
    count = order_slot.shape[0]
    slots = count // sources
    groups = LANES // (2 * slots)
    high, low = mode_tables(count)
    m = order_slot.reshape(sources, 1, 1, slots)
    part = jnp.arange(2, dtype=jnp.int32).reshape(1, 1, 2, 1)
    pick = (m & 1) * count + part * (count // 2) + (m >> 1)
    pick = jnp.broadcast_to(pick, (sources, groups, 2, slots)).reshape(1, sources * LANES)
    vmem = pl.BlockSpec(memory_space=pltpu.VMEM)
    return pl.pallas_call(
        functools.partial(bin_kernel, windows=windows, rows=rows, window_cycles=cycles // windows),
        out_shape=(
            jax.ShapeDtypeStruct((cycles, NPHI), jnp.float32),
            jax.ShapeDtypeStruct((sources, cycles // groups, LANES), jnp.float32),
        ),
        in_specs=[vmem] * 4,
        out_specs=(vmem, vmem),
        compiler_params=pltpu.CompilerParams(vmem_limit_bytes=40 * 1024 * 1024),
        name="bin_modes",
    )(recv, pick, jnp.asarray(high), jnp.asarray(low))


def legendre_kernel(order_ref, recv_ref, leg_ref, out_ref, modes_ref, *, per_step):
    slots = out_ref.shape[1] // 2
    sources, group_rows, lanes = recv_ref.shape
    groups = lanes // (2 * slots)
    band_cycles, degrees = leg_ref.shape[1:]
    step = pl.program_id(0)

    @pl.when(step == 0)
    def _():
        for e in range(sources):
            block = recv_ref[e]
            for h in range(groups):
                at = (e * groups + h) * group_rows
                turned = block if h == 0 else pltpu.roll(block, lanes - h * 2 * slots, axis=1)
                modes_ref[at:at + group_rows, :] = turned

    chunk = 32
    for i in range(per_step):
        slot = step * per_step + i

        def body(n, acc):
            here = pl.ds(pl.multiple_of(n * chunk, chunk), chunk)
            turned = pltpu.roll(modes_ref[here, :], lanes - slot, axis=1)
            leg = leg_ref[i, here, :]
            real, imag = acc
            for r in range(0, chunk, SUB):
                block = leg[r:r + SUB]
                real = real + block * turned[r:r + SUB, 0:1]
                imag = imag + block * turned[r:r + SUB, slots:slots + 1]
            return real, imag

        zero = jnp.zeros((SUB, degrees), jnp.float32)
        sums = lax.fori_loop(0, band_cycles // chunk, body, (zero, zero))
        keep = lax.broadcasted_iota(jnp.int32, (1, degrees), 1) >= order_ref[slot]
        owners, _, width = out_ref.shape
        for c in range(2):
            line = jnp.where(keep, jnp.sum(sums[c], axis=0, keepdims=True), 0.0)
            for d in range(owners):
                out_ref[d, pl.ds(c * slots + slot, 1), :] = line[:, d * width:(d + 1) * width]


def legendre_sums(recv, local_orders, legendre, owners):
    slots, band_cycles, degrees = legendre.shape
    per_step = 2
    vmem = pl.BlockSpec(memory_space=pltpu.VMEM)
    return pl.pallas_call(
        functools.partial(legendre_kernel, per_step=per_step),
        grid=(slots // per_step,),
        out_shape=jax.ShapeDtypeStruct((owners, 2 * slots, degrees // owners), jnp.float32),
        in_specs=[
            pl.BlockSpec(memory_space=pltpu.SMEM),
            vmem,
            pl.BlockSpec((per_step, band_cycles, degrees), lambda s: (s, 0, 0)),
        ],
        out_specs=vmem,
        scratch_shapes=[pltpu.VMEM((band_cycles, LANES), jnp.float32)],
        compiler_params=pltpu.CompilerParams(vmem_limit_bytes=24 * 1024 * 1024),
        name="legendre_sums",
    )(local_orders, recv, legendre)


def dense_path(filtered, cycle_offset, column, order_slot, legendre):
    band_cycles = legendre.shape[1]
    flat_index = (cycle_offset * NPHI + column).reshape(-1)
    empty = jnp.zeros((band_cycles * NPHI,), jnp.float32)
    partial_value = empty.at[flat_index].add(filtered.reshape(-1)).reshape(band_cycles, NPHI)
    counts = empty.at[flat_index].add(1.0).reshape(band_cycles, NPHI)
    summed = lax.psum_scatter(partial_value, "det", scatter_dimension=0, tiled=True)
    hit_total = lax.psum_scatter(counts, "det", scatter_dimension=0, tiled=True)
    sky_map = summed / jnp.maximum(hit_total, 1.0)
    pixel_index = jnp.arange(NPHI, dtype=jnp.int32)[:, None]
    phases = 2.0 * jnp.pi / NPHI * (pixel_index * order_slot[None, :] % NPHI).astype(jnp.float32)
    cycle_modes = jnp.stack([
        jnp.dot(sky_map, jnp.cos(phases), precision=precise),
        -jnp.dot(sky_map, jnp.sin(phases), precision=precise),
    ])
    slot_count, _, degrees = legendre.shape
    local_orders = lax.dynamic_slice_in_dim(order_slot, lax.axis_index("det") * slot_count, slot_count, 0)
    keep = jnp.arange(degrees, dtype=jnp.int32)[None, :] >= local_orders[:, None]
    terms = jnp.einsum(
        "crs,srl->csl",
        lax.all_to_all(cycle_modes, "det", split_axis=2, concat_axis=1, tiled=True),
        legendre,
        precision=precise,
    ) * keep.astype(jnp.float32)[None]
    return lax.psum_scatter(terms, "band", scatter_dimension=2, tiled=True), sky_map


def local(scan_lines, response, cycle_offset, column, order_slot, legendre, *, det_count, band_count):
    slots, band_cycles, degrees = legendre.shape
    filtered, send, flag = filter_and_sort(
        scan_lines, response, cycle_offset, column, det_count, band_cycles
    )
    crowded = lax.pmax(flag[0, 0], ("det", "band"))
    recv = lax.all_to_all(send, "det", split_axis=0, concat_axis=0, tiled=True)
    sky_map, modes = bin_and_modes(recv, order_slot, band_cycles)
    modes = lax.all_to_all(modes, "det", split_axis=0, concat_axis=0, tiled=True)
    local_orders = lax.dynamic_slice_in_dim(order_slot, lax.axis_index("det") * slots, slots, 0)
    terms = legendre_sums(modes, local_orders, legendre, band_count)
    terms = lax.all_to_all(terms, "band", split_axis=0, concat_axis=0, tiled=True)
    harmonics = jnp.sum(terms, axis=0).reshape(2, slots, degrees // band_count)
    return lax.cond(
        crowded > 0,
        lambda: dense_path(filtered, cycle_offset, column, order_slot, legendre),
        lambda: (harmonics, sky_map),
    )


def solution(mesh):
    sizes = dict(mesh.shape)
    return jax.shard_map(
        functools.partial(local, det_count=sizes["det"], band_count=sizes["band"]),
        mesh=mesh,
        in_specs=(
            P(("det", "band"), None),
            P(("det", "band"), None),
            P(("det", "band"), None),
            P(("det", "band"), None),
            P(),
            P("det", "band", None),
        ),
        out_specs=(P(None, "det", "band"), P(("band", "det"), None)),
        check_vma=False,
    )
```

```python
import functools

import jax
import jax.numpy as jnp
import numpy as np
from jax import lax
from jax.experimental import pallas as pl
from jax.experimental.pallas import tpu as pltpu
from jax.sharding import PartitionSpec as P

NPHI = 2048
LANES = 128
SUB = 8
WINDOWS = 2
ROW = 256

precise = lax.Precision.HIGHEST
NT = (((1,), (1,)), ((), ()))


def filter_tables(length):
    outer = length // LANES
    k1 = np.arange(outer)[:, None]
    n2 = np.arange(LANES)[None, :]
    turn = 2.0 * np.pi * ((k1 * n2) % length) / length
    twiddle = np.stack([np.cos(turn), np.sin(turn)])[:, :, None, :]
    a = np.arange(LANES)
    angle = 2.0 * np.pi * (np.outer(a, a) % LANES) / LANES
    c, s = np.cos(angle), np.sin(angle)
    forward = np.block([[c, -s], [s, c]])
    back = np.block([[c, s], [-s, c]])
    return (
        twiddle.astype(np.float32),
        forward.astype(np.float32),
        back.astype(np.float32),
    )


def mode_tables(count):
    half = NPHI // 2
    p = np.arange(half)[:, None]
    out = []
    for parity in (0, 1):
        m = 2 * np.arange(count // 2)[None, :] + parity
        angle = 2.0 * np.pi * ((p * m) % NPHI) / NPHI
        out.append(np.concatenate([np.cos(angle), -np.sin(angle)], axis=1))
    table = np.stack(out).astype(np.float32)
    high = table.astype(jnp.bfloat16)
    low = (table - high.astype(np.float32)).astype(jnp.bfloat16)
    return high, low


def small_fft(re, im, sign):
    count = len(re)
    if count == 1:
        return re, im
    even_re, even_im = small_fft(re[0::2], None if im is None else im[0::2], sign)
    odd_re, odd_im = small_fft(re[1::2], None if im is None else im[1::2], sign)
    half = count // 2
    out_re, out_im = [None] * count, [None] * count
    for k in range(half):
        wr = float(np.cos(2 * np.pi * k / count))
        wi = float(sign * np.sin(2 * np.pi * k / count))
        er, ei, orr, oi = even_re[k], even_im and even_im[k], odd_re[k], odd_im and odd_im[k]
        if k == 0:
            tr, ti = orr, oi
        elif 4 * k == count:
            tr = None if oi is None else -wi * oi
            ti = wi * orr
        elif oi is None:
            tr, ti = wr * orr, wi * orr
        else:
            tr, ti = wr * orr - wi * oi, wr * oi + wi * orr
        out_re[k] = er if tr is None else er + tr
        out_re[k + half] = er if tr is None else er - tr
        if ti is None:
            out_im[k] = out_im[k + half] = ei
        else:
            out_im[k] = ti if ei is None else ei + ti
            out_im[k + half] = -ti if ei is None else ei - ti
    if all(x is None for x in out_im):
        return out_re, None
    out_im = [jnp.zeros_like(out_re[0]) if x is None else x for x in out_im]
    return out_re, out_im


def partner(x, axis, distance):
    size = x.shape[axis]
    if 2 * distance == size:
        return pltpu.roll(x, distance, axis=axis)
    index = lax.broadcasted_iota(jnp.int32, x.shape, axis)
    upper = (index & distance) != 0
    return jnp.where(
        upper,
        pltpu.roll(x, distance, axis=axis),
        pltpu.roll(x, size - distance, axis=axis),
    )


def rank_bit(bit, tile_bits):
    shape = (SUB, LANES)
    if bit < tile_bits + 3:
        return (lax.broadcasted_iota(jnp.int32, shape, 0) & (1 << (bit - tile_bits))) != 0
    return (lax.broadcasted_iota(jnp.int32, shape, 1) & (1 << (bit - tile_bits - 3))) != 0


def sort_inner(key_ref, val_ref, level, tile_bits, total_bits, group):
    tiles = key_ref.shape[0]

    def body(g, carry):
        part = pl.ds(g * group, group)
        key, val = key_ref[part], val_ref[part]
        for bit in range(level - 1, tile_bits - 1, -1):
            if bit < tile_bits + 3:
                axis, distance = 1, 1 << (bit - tile_bits)
            else:
                axis, distance = 2, 1 << (bit - tile_bits - 3)
            want_max = rank_bit(bit, tile_bits)
            if level < total_bits:
                want_max = jnp.logical_xor(want_max, rank_bit(level, tile_bits))
            sign = jnp.where(want_max, -1.0, 1.0)[None]
            key_p, val_p = partner(key, axis, distance), partner(val, axis, distance)
            swap = (key - key_p) * sign > 0.0
            key = jnp.where(swap, key_p, key)
            val = jnp.where(swap, val_p, val)
        key_ref[part] = key
        val_ref[part] = val
        return carry

    lax.fori_loop(0, tiles // group, body, 0)


def exchange(keys, vals, a, b, down):
    swap = keys[a] > keys[b]
    if down is True:
        swap = keys[a] < keys[b]
    elif down is not False:
        swap = jnp.logical_xor(swap, down)
    keys[a], keys[b] = jnp.where(swap, keys[b], keys[a]), jnp.where(swap, keys[a], keys[b])
    vals[a], vals[b] = jnp.where(swap, vals[b], vals[a]), jnp.where(swap, vals[a], vals[b])


def sort_across(key_ref, val_ref, level, tile_bits, total_bits):
    tiles = key_ref.shape[0]
    top = min(level, tile_bits)
    bits = list(range(top - 1, -1, -1))
    passes = [bits[:-3], bits[-3:]] if len(bits) > 3 else [bits]
    for chosen in passes:
        low, span = min(chosen), len(chosen)
        members = 1 << span
        stride = 1 << low

        def run(base, static_base):
            keys = [key_ref[base + i * stride] for i in range(members)]
            vals = [val_ref[base + i * stride] for i in range(members)]
            for bit in chosen:
                step = 1 << (bit - low)
                for i in range(members):
                    if i & step:
                        continue
                    if level >= total_bits:
                        down = False
                    elif level < tile_bits:
                        down = ((static_base + i * stride) >> level) & 1 == 1
                    else:
                        down = rank_bit(level, tile_bits)
                    exchange(keys, vals, i, i + step, down)
            for i in range(members):
                key_ref[base + i * stride] = keys[i]
                val_ref[base + i * stride] = vals[i]

        def base_of(g):
            return (g // stride) * (members * stride) + g % stride

        groups = tiles // members
        if level < tile_bits:
            for g in range(groups):
                run(base_of(g), base_of(g))
        else:
            for g in range(groups):
                run(base_of(g), None)


def sort_kernel(
    scan_ref, resp_ref, cycle_ref, column_ref, twiddle_ref, forward_ref, back_ref,
    filtered_ref, send_ref,
    key_ref, val_ref, spec_ref, key_rows, val_rows,
    *, buckets, span, rows, windows,
):
    lines, length = scan_ref.shape
    outer = length // LANES
    re, im = small_fft([scan_ref[:, n * LANES:(n + 1) * LANES] for n in range(outer)], None, -1)
    for k in range(outer):
        c, s = twiddle_ref[0, k], twiddle_ref[1, k]
        here = pl.ds(k * lines, lines)
        spec_ref[here, :LANES] = re[k] * c + im[k] * s
        spec_ref[here, LANES:] = im[k] * c - re[k] * s
    spec = jnp.dot(spec_ref[...], forward_ref[...], precision=precise, preferred_element_type=jnp.float32)
    resp = resp_ref[...] * (1.0 / length)
    spec = spec * jnp.concatenate([resp, resp], axis=1)
    spec_ref[...] = jnp.dot(spec, back_ref[...], precision=precise, preferred_element_type=jnp.float32)
    re, im = [], []
    for k in range(outer):
        c, s = twiddle_ref[0, k], twiddle_ref[1, k]
        here = pl.ds(k * lines, lines)
        ur, ui = spec_ref[here, :LANES], spec_ref[here, LANES:]
        re.append(ur * c - ui * s)
        im.append(ui * c + ur * s)
    out, _ = small_fft(re, im, 1)
    for n in range(outer):
        cols = slice(n * LANES, (n + 1) * LANES)
        filtered_ref[:, cols] = out[n]
        val_ref[n] = out[n]
        key_ref[n] = (cycle_ref[:, cols] * NPHI + column_ref[:, cols]).astype(jnp.float32)
    tiles = outer
    tile_bits = tiles.bit_length() - 1
    total_bits = tile_bits + 10
    for level in range(1, total_bits + 1):
        if level > tile_bits:
            sort_inner(key_ref, val_ref, level, tile_bits, total_bits, min(16, tiles))
        sort_across(key_ref, val_ref, level, tile_bits, total_bits)
    keys = key_ref[...]
    last = jnp.max(jnp.max(keys, axis=0), axis=0, keepdims=True)
    first = jnp.min(jnp.min(keys, axis=0), axis=0, keepdims=True)
    row_len = tiles * SUB
    key_rows[:LANES, :] = keys.reshape(row_len, LANES).T
    val_rows[:LANES, :] = val_ref[...].reshape(row_len, LANES).T
    reach = key_rows.shape[0] - LANES
    key_rows[LANES:, :] = jnp.full((reach, row_len), 2.0 * buckets * span, jnp.float32)
    val_rows[LANES:, :] = jnp.zeros((reach, row_len), jnp.float32)
    over = jnp.int32(0)
    for b in range(buckets):
        begin = jnp.sum((last < float(b * span)).astype(jnp.float32)).astype(jnp.int32)
        end = jnp.sum((first < float((b + 1) * span)).astype(jnp.float32)).astype(jnp.int32)
        over = over + (end - begin > rows).astype(jnp.int32)
        begin = jnp.minimum(begin, LANES)
        aligned = pl.multiple_of((begin // SUB) * SUB, SUB)
        back = lax.rem(reach - (begin - aligned), reach)
        here = pl.ds(aligned, reach)
        dest, w = divmod(b, windows)
        taken = pltpu.roll(key_rows[here, :], back, axis=0)[:rows]
        send_ref[dest, w * rows:(w + 1) * rows, :] = taken - float(b * span)
        at = (windows + w) * rows
        send_ref[dest, at:at + rows, :] = pltpu.roll(val_rows[here, :], back, axis=0)[:rows]

    @pl.when(over > 0)
    def _():
        send_ref[...] = jnp.full(send_ref.shape, jnp.nan, jnp.float32)


def filter_and_sort(scan, resp, cycle, column, det_count, band_cycles):
    lines, length = scan.shape
    tiles = length // LANES
    windows = WINDOWS
    buckets = det_count * windows
    span = band_cycles * NPHI // buckets
    row_len = tiles * SUB
    rows = LANES // buckets + 2
    reach = (rows + 2 * SUB - 2) // SUB * SUB
    twiddle, forward, back = filter_tables(length)
    resp_rows = resp.reshape(lines, LANES, tiles).transpose(2, 0, 1).reshape(tiles * lines, LANES)
    body = functools.partial(sort_kernel, buckets=buckets, span=span, rows=rows, windows=windows)
    vmem = pl.BlockSpec(memory_space=pltpu.VMEM)
    return pl.pallas_call(
        body,
        out_shape=(
            jax.ShapeDtypeStruct((lines, length), jnp.float32),
            jax.ShapeDtypeStruct((det_count, 2 * windows * rows, row_len), jnp.float32),
        ),
        in_specs=[vmem] * 7,
        out_specs=(vmem, vmem),
        scratch_shapes=[
            pltpu.VMEM((tiles, SUB, LANES), jnp.float32),
            pltpu.VMEM((tiles, SUB, LANES), jnp.float32),
            pltpu.VMEM((tiles * lines, 2 * LANES), jnp.float32),
            pltpu.VMEM((LANES + reach, row_len), jnp.float32),
            pltpu.VMEM((LANES + reach, row_len), jnp.float32),
        ],
        compiler_params=pltpu.CompilerParams(vmem_limit_bytes=24 * 1024 * 1024),
        name="filter_sort",
    )(scan, resp_rows, cycle, column, jnp.asarray(twiddle), jnp.asarray(forward), jnp.asarray(back))


def split2(x):
    high = x.astype(jnp.bfloat16)
    low = (x - high.astype(jnp.float32)).astype(jnp.bfloat16)
    return high, low


def bin_kernel(recv_ref, pick_ref, table_hi, table_lo, map_ref, send_ref, *, windows, rows, window_cycles):
    sources = recv_ref.shape[0]
    row_len = recv_ref.shape[2]
    parts = NPHI // ROW
    area = parts * window_cycles
    for w in range(windows):
        def body(e, acc):
            left, right = [], []
            a_iota = lax.broadcasted_iota(jnp.int32, (area, row_len), 0)
            b_iota = lax.broadcasted_iota(jnp.int32, (ROW, row_len), 0)
            for r in range(rows):
                q = recv_ref[e, w * rows + r:w * rows + r + 1, :].astype(jnp.int32)
                v = recv_ref[e, (windows + w) * rows + r:(windows + w) * rows + r + 1, :]
                high, low = split2(v)
                cycle = q >> 11
                inside = (q >= 0) & (cycle < window_cycles)
                a = jnp.where(inside, ((q >> 8) & (parts - 1)) * window_cycles + cycle, -1)
                hit_a = a_iota == a
                zero = jnp.zeros((), jnp.float32)
                left.append(jnp.concatenate([
                    jnp.where(hit_a, high.astype(jnp.float32), zero).astype(jnp.bfloat16),
                    jnp.where(hit_a, low.astype(jnp.float32), zero).astype(jnp.bfloat16),
                    jnp.where(hit_a, 1.0, zero).astype(jnp.bfloat16),
                ], axis=0))
                right.append(jnp.where(b_iota == (q & (ROW - 1)), 1.0, zero).astype(jnp.bfloat16))
            return acc + lax.dot_general(
                jnp.concatenate(left, axis=1), jnp.concatenate(right, axis=1), NT,
                preferred_element_type=jnp.float32,
            )

        acc = lax.fori_loop(0, sources, body, jnp.zeros((3 * area, ROW), jnp.float32))
        sky = (acc[:area] + acc[area:2 * area]) / jnp.maximum(acc[2 * area:], 1.0)
        for c8 in range(parts):
            map_ref[w * window_cycles:(w + 1) * window_cycles, c8 * ROW:(c8 + 1) * ROW] = (
                sky[c8 * window_cycles:(c8 + 1) * window_cycles]
            )
    cycles = map_ref.shape[0]
    half = NPHI // 2
    modes = []
    for parity in (0, 1):
        a, b = map_ref[:, :half], map_ref[:, half:]
        high, low = split2(a + b if parity == 0 else a - b)
        first = jnp.dot(jnp.concatenate([high, low], axis=0), table_hi[parity], preferred_element_type=jnp.float32)
        second = jnp.dot(high, table_lo[parity], preferred_element_type=jnp.float32)
        modes.append(first[:cycles] + first[cycles:] + second)
    modes = jnp.concatenate(modes, axis=1)
    count = modes.shape[1]
    width = pick_ref.shape[1]
    high = modes.astype(jnp.bfloat16)
    rest = modes - high.astype(jnp.float32)
    middle = rest.astype(jnp.bfloat16)
    low = (rest - middle.astype(jnp.float32)).astype(jnp.bfloat16)
    pieces = jnp.concatenate([high, middle, low], axis=0)
    choose = (lax.broadcasted_iota(jnp.int32, (count, width), 0) == pick_ref[...])
    choose = jnp.where(choose, 1.0, 0.0).astype(jnp.bfloat16)
    moved = jnp.dot(pieces, choose, preferred_element_type=jnp.float32)
    moved = moved[:cycles] + moved[cycles:2 * cycles] + moved[2 * cycles:]
    owners, group_rows, lanes = send_ref.shape
    groups = cycles // group_rows
    lane_group = lax.broadcasted_iota(jnp.int32, (group_rows, lanes), 1) // (lanes // groups)
    values = recv_ref[:, windows * rows:, :]
    broken = jnp.max(jnp.where(values == values, 0.0, 1.0)) > 0.0
    for d in range(owners):
        block = moved[:, d * lanes:(d + 1) * lanes]
        out = block[:group_rows]
        for h in range(1, groups):
            out = jnp.where(lane_group == h, block[h * group_rows:(h + 1) * group_rows], out)
        send_ref[d] = jnp.where(broken, jnp.nan, out)


def bin_and_modes(recv, order_slot, band_cycles):
    sources, lines, row_len = recv.shape
    windows = WINDOWS
    rows = lines // (2 * windows)
    cycles = band_cycles // sources
    count = order_slot.shape[0]
    slots = count // sources
    groups = LANES // (2 * slots)
    high, low = mode_tables(count)
    m = order_slot.reshape(sources, 1, 1, slots)
    part = jnp.arange(2, dtype=jnp.int32).reshape(1, 1, 2, 1)
    pick = (m & 1) * count + part * (count // 2) + (m >> 1)
    pick = jnp.broadcast_to(pick, (sources, groups, 2, slots)).reshape(1, sources * LANES)
    vmem = pl.BlockSpec(memory_space=pltpu.VMEM)
    return pl.pallas_call(
        functools.partial(bin_kernel, windows=windows, rows=rows, window_cycles=cycles // windows),
        out_shape=(
            jax.ShapeDtypeStruct((cycles, NPHI), jnp.float32),
            jax.ShapeDtypeStruct((sources, cycles // groups, LANES), jnp.float32),
        ),
        in_specs=[vmem] * 4,
        out_specs=(vmem, vmem),
        compiler_params=pltpu.CompilerParams(vmem_limit_bytes=40 * 1024 * 1024),
        name="bin_modes",
    )(recv, pick, jnp.asarray(high), jnp.asarray(low))


def legendre_kernel(recv_ref, table_ref, out_ref, leg_ref, arrived, modes_ref, wide_ref):
    slots, band_cycles, degrees = table_ref.shape

    def load(slot):
        return pltpu.make_async_copy(table_ref.at[slot], leg_ref.at[slot], arrived.at[slot])

    def start(slot, carry):
        load(slot).start()
        return carry

    lax.fori_loop(0, slots, start, 0)
    sources, group_rows, lanes = recv_ref.shape
    groups = lanes // (2 * slots)
    owners, _, width = out_ref.shape
    tiles = degrees // LANES
    for e in range(sources):
        block = recv_ref[e]
        for h in range(groups):
            at = (e * groups + h) * group_rows
            turned = block if h == 0 else pltpu.roll(block, lanes - h * 2 * slots, axis=1)
            modes_ref[at:at + group_rows, :] = turned

    def widen(slot, half):
        turned = pltpu.roll(modes_ref[...], lax.rem(lanes - slot, lanes), axis=1)
        for c in range(2):
            column = turned[:, c * slots:c * slots + 1]
            wide_ref[half, c] = jnp.broadcast_to(column, (band_cycles, lanes))

    widen(0, 0)

    def body(slot, carry):
        half = slot & 1
        load(slot).wait()
        sums = [[jnp.zeros((SUB, LANES), jnp.float32) for _ in range(tiles)] for _ in range(2)]
        for r in range(0, band_cycles, SUB):
            factor = [wide_ref[half, c, r:r + SUB, :] for c in range(2)]
            for t in range(tiles):
                block = leg_ref[slot, r:r + SUB, t * LANES:(t + 1) * LANES]
                for c in range(2):
                    sums[c][t] = sums[c][t] + block * factor[c]
        widen(jnp.minimum(slot + 1, slots - 1), 1 - half)
        per_owner = width // LANES
        for c in range(2):
            lines = [jnp.sum(part, axis=0, keepdims=True) for part in sums[c]]
            for d in range(owners):
                line = jnp.concatenate(lines[d * per_owner:(d + 1) * per_owner], axis=1)
                out_ref[d, pl.ds(c * slots + slot, 1), :] = line
        return carry

    lax.fori_loop(0, slots, body, 0)


def legendre_sums(recv, legendre, owners):
    slots, band_cycles, degrees = legendre.shape
    vmem = pl.BlockSpec(memory_space=pltpu.VMEM)
    return pl.pallas_call(
        legendre_kernel,
        out_shape=jax.ShapeDtypeStruct((owners, 2 * slots, degrees // owners), jnp.float32),
        in_specs=[vmem, pl.BlockSpec(memory_space=pl.ANY)],
        out_specs=vmem,
        scratch_shapes=[
            pltpu.VMEM(legendre.shape, jnp.float32),
            pltpu.SemaphoreType.DMA((slots,)),
            pltpu.VMEM((band_cycles, LANES), jnp.float32),
            pltpu.VMEM((2, 2, band_cycles, LANES), jnp.float32),
        ],
        compiler_params=pltpu.CompilerParams(vmem_limit_bytes=44 * 1024 * 1024),
        name="legendre_sums",
    )(recv, legendre)


def exchange_and_sum(x, axis, count):
    parts = x.reshape(count, x.shape[0] // count, x.shape[1])
    return jnp.sum(lax.all_to_all(parts, axis, split_axis=0, concat_axis=0, tiled=True), axis=0)


def dense_path(filtered, cycle_offset, column, order_slot, legendre, det_count, band_count):
    band_cycles = legendre.shape[1]
    flat_index = (cycle_offset * NPHI + column).reshape(-1)
    empty = jnp.zeros((band_cycles * NPHI,), jnp.float32)
    partial_value = empty.at[flat_index].add(filtered.reshape(-1)).reshape(band_cycles, NPHI)
    counts = empty.at[flat_index].add(1.0).reshape(band_cycles, NPHI)
    summed = exchange_and_sum(partial_value, "det", det_count)
    hit_total = exchange_and_sum(counts, "det", det_count)
    sky_map = summed / jnp.maximum(hit_total, 1.0)
    pixel_index = jnp.arange(NPHI, dtype=jnp.int32)[:, None]
    phases = 2.0 * jnp.pi / NPHI * (pixel_index * order_slot[None, :] % NPHI).astype(jnp.float32)
    cycle_modes = jnp.stack([
        jnp.dot(sky_map, jnp.cos(phases), precision=precise),
        -jnp.dot(sky_map, jnp.sin(phases), precision=precise),
    ])
    slot_count, _, degrees = legendre.shape
    local_orders = lax.dynamic_slice_in_dim(order_slot, lax.axis_index("det") * slot_count, slot_count, 0)
    keep = jnp.arange(degrees, dtype=jnp.int32)[None, :] >= local_orders[:, None]
    terms = jnp.einsum(
        "crs,srl->csl",
        lax.all_to_all(cycle_modes, "det", split_axis=2, concat_axis=1, tiled=True),
        legendre,
        precision=precise,
    ) * keep.astype(jnp.float32)[None]
    harmonics = exchange_and_sum(terms.transpose(2, 0, 1).reshape(degrees, -1), "band", band_count)
    return harmonics.reshape(-1, 2, slot_count).transpose(1, 2, 0), sky_map


def local(scan_lines, response, cycle_offset, column, order_slot, legendre, *, det_count, band_count):
    slots, band_cycles, degrees = legendre.shape
    filtered, send = filter_and_sort(
        scan_lines, response, cycle_offset, column, det_count, band_cycles
    )
    recv = lax.all_to_all(send, "det", split_axis=0, concat_axis=0, tiled=True)
    sky_map, modes = bin_and_modes(recv, order_slot, band_cycles)
    modes = lax.all_to_all(modes, "det", split_axis=0, concat_axis=0, tiled=True)
    terms = legendre_sums(modes, legendre, band_count)
    terms = lax.all_to_all(terms, "band", split_axis=0, concat_axis=0, tiled=True)
    sums = jnp.sum(terms, axis=0)
    crowded = jnp.isnan(sums[0, 0])
    local_orders = lax.dynamic_slice_in_dim(order_slot, lax.axis_index("det") * slots, slots, 0)
    width = degrees // band_count
    degree = lax.axis_index("band") * width + jnp.arange(width, dtype=jnp.int32)
    keep = degree[None, None, :] >= local_orders[None, :, None]
    harmonics = jnp.where(keep, sums.reshape(2, slots, width), 0.0)
    return lax.cond(
        crowded,
        lambda: dense_path(
            filtered, cycle_offset, column, order_slot, legendre, det_count, band_count
        ),
        lambda: (harmonics, sky_map),
    )


def solution(mesh):
    sizes = dict(mesh.shape)
    return jax.shard_map(
        functools.partial(local, det_count=sizes["det"], band_count=sizes["band"]),
        mesh=mesh,
        in_specs=(
            P(("det", "band"), None),
            P(("det", "band"), None),
            P(("det", "band"), None),
            P(("det", "band"), None),
            P(),
            P("det", "band", None),
        ),
        out_specs=(P(None, "det", "band"), P(("band", "det"), None)),
        check_vma=False,
    )
```

```python
import functools

import jax
import jax.numpy as jnp
import numpy as np
from jax import lax
from jax.experimental import pallas as pl
from jax.experimental.pallas import tpu as pltpu
from jax.sharding import PartitionSpec as P

NPHI = 2048
LANES = 128
SUB = 8
WINDOWS = 2
ROW = 256

precise = lax.Precision.HIGHEST
NT = (((1,), (1,)), ((), ()))


def filter_tables(length):
    outer = length // LANES
    k1 = np.arange(outer)[:, None]
    n2 = np.arange(LANES)[None, :]
    turn = 2.0 * np.pi * ((k1 * n2) % length) / length
    twiddle = np.stack([np.cos(turn), np.sin(turn)])[:, :, None, :]
    a = np.arange(LANES)
    angle = 2.0 * np.pi * (np.outer(a, a) % LANES) / LANES
    c, s = np.cos(angle), np.sin(angle)
    forward = np.block([[c, -s], [s, c]])
    back = np.block([[c, s], [-s, c]])
    return (
        twiddle.astype(np.float32),
        forward.astype(np.float32),
        back.astype(np.float32),
    )


def mode_tables(count):
    half = NPHI // 2
    p = np.arange(half)[:, None]
    out = []
    for parity in (0, 1):
        m = 2 * np.arange(count // 2)[None, :] + parity
        angle = 2.0 * np.pi * ((p * m) % NPHI) / NPHI
        out.append(np.concatenate([np.cos(angle), -np.sin(angle)], axis=1))
    table = np.stack(out).astype(np.float32)
    high = table.astype(jnp.bfloat16)
    low = (table - high.astype(np.float32)).astype(jnp.bfloat16)
    return high, low


def small_fft(re, im, sign):
    count = len(re)
    if count == 1:
        return re, im
    even_re, even_im = small_fft(re[0::2], None if im is None else im[0::2], sign)
    odd_re, odd_im = small_fft(re[1::2], None if im is None else im[1::2], sign)
    half = count // 2
    out_re, out_im = [None] * count, [None] * count
    for k in range(half):
        wr = float(np.cos(2 * np.pi * k / count))
        wi = float(sign * np.sin(2 * np.pi * k / count))
        er, ei, orr, oi = even_re[k], even_im and even_im[k], odd_re[k], odd_im and odd_im[k]
        if k == 0:
            tr, ti = orr, oi
        elif 4 * k == count:
            tr = None if oi is None else -wi * oi
            ti = wi * orr
        elif oi is None:
            tr, ti = wr * orr, wi * orr
        else:
            tr, ti = wr * orr - wi * oi, wr * oi + wi * orr
        out_re[k] = er if tr is None else er + tr
        out_re[k + half] = er if tr is None else er - tr
        if ti is None:
            out_im[k] = out_im[k + half] = ei
        else:
            out_im[k] = ti if ei is None else ei + ti
            out_im[k + half] = -ti if ei is None else ei - ti
    if all(x is None for x in out_im):
        return out_re, None
    out_im = [jnp.zeros_like(out_re[0]) if x is None else x for x in out_im]
    return out_re, out_im


def partner(x, axis, distance):
    size = x.shape[axis]
    if 2 * distance == size:
        return pltpu.roll(x, distance, axis=axis)
    index = lax.broadcasted_iota(jnp.int32, x.shape, axis)
    upper = (index & distance) != 0
    return jnp.where(
        upper,
        pltpu.roll(x, distance, axis=axis),
        pltpu.roll(x, size - distance, axis=axis),
    )


def rank_bit(bit, tile_bits):
    shape = (SUB, LANES)
    if bit < tile_bits + 3:
        return (lax.broadcasted_iota(jnp.int32, shape, 0) & (1 << (bit - tile_bits))) != 0
    return (lax.broadcasted_iota(jnp.int32, shape, 1) & (1 << (bit - tile_bits - 3))) != 0


def sort_inner(key_ref, val_ref, level, tile_bits, total_bits, group):
    tiles = key_ref.shape[0]

    def body(g, carry):
        part = pl.ds(g * group, group)
        key, val = key_ref[part], val_ref[part]
        for bit in range(level - 1, tile_bits - 1, -1):
            if bit < tile_bits + 3:
                axis, distance = 1, 1 << (bit - tile_bits)
            else:
                axis, distance = 2, 1 << (bit - tile_bits - 3)
            want_max = rank_bit(bit, tile_bits)
            if level < total_bits:
                want_max = jnp.logical_xor(want_max, rank_bit(level, tile_bits))
            sign = jnp.where(want_max, -1.0, 1.0)[None]
            key_p, val_p = partner(key, axis, distance), partner(val, axis, distance)
            swap = (key - key_p) * sign > 0.0
            key = jnp.where(swap, key_p, key)
            val = jnp.where(swap, val_p, val)
        key_ref[part] = key
        val_ref[part] = val
        return carry

    lax.fori_loop(0, tiles // group, body, 0)


def exchange(keys, vals, a, b, down):
    swap = keys[a] > keys[b]
    if down is True:
        swap = keys[a] < keys[b]
    elif down is not False:
        swap = jnp.logical_xor(swap, down)
    keys[a], keys[b] = jnp.where(swap, keys[b], keys[a]), jnp.where(swap, keys[a], keys[b])
    vals[a], vals[b] = jnp.where(swap, vals[b], vals[a]), jnp.where(swap, vals[a], vals[b])


def sort_across(key_ref, val_ref, level, tile_bits, total_bits):
    tiles = key_ref.shape[0]
    top = min(level, tile_bits)
    bits = list(range(top - 1, -1, -1))
    passes = [bits[:-3], bits[-3:]] if len(bits) > 3 else [bits]
    for chosen in passes:
        low, span = min(chosen), len(chosen)
        members = 1 << span
        stride = 1 << low

        def run(base, static_base):
            keys = [key_ref[base + i * stride] for i in range(members)]
            vals = [val_ref[base + i * stride] for i in range(members)]
            for bit in chosen:
                step = 1 << (bit - low)
                for i in range(members):
                    if i & step:
                        continue
                    if level >= total_bits:
                        down = False
                    elif level < tile_bits:
                        down = ((static_base + i * stride) >> level) & 1 == 1
                    else:
                        down = rank_bit(level, tile_bits)
                    exchange(keys, vals, i, i + step, down)
            for i in range(members):
                key_ref[base + i * stride] = keys[i]
                val_ref[base + i * stride] = vals[i]

        def base_of(g):
            return (g // stride) * (members * stride) + g % stride

        groups = tiles // members
        if level < tile_bits:
            for g in range(groups):
                run(base_of(g), base_of(g))
        else:
            for g in range(groups):
                run(base_of(g), None)


def sort_kernel(
    scan_ref, resp_ref, cycle_ref, column_ref, twiddle_ref, forward_ref, back_ref,
    filtered_ref, send_ref,
    key_ref, val_ref, spec_ref, key_rows, val_rows,
    *, buckets, span, rows, windows,
):
    lines, length = scan_ref.shape
    outer = length // LANES
    re, im = small_fft([scan_ref[:, n * LANES:(n + 1) * LANES] for n in range(outer)], None, -1)
    for k in range(outer):
        c, s = twiddle_ref[0, k], twiddle_ref[1, k]
        here = pl.ds(k * lines, lines)
        spec_ref[here, :LANES] = re[k] * c + im[k] * s
        spec_ref[here, LANES:] = im[k] * c - re[k] * s
    spec = jnp.dot(spec_ref[...], forward_ref[...], precision=precise, preferred_element_type=jnp.float32)
    resp = resp_ref[...] * (1.0 / length)
    spec = spec * jnp.concatenate([resp, resp], axis=1)
    spec_ref[...] = jnp.dot(spec, back_ref[...], precision=precise, preferred_element_type=jnp.float32)
    re, im = [], []
    for k in range(outer):
        c, s = twiddle_ref[0, k], twiddle_ref[1, k]
        here = pl.ds(k * lines, lines)
        ur, ui = spec_ref[here, :LANES], spec_ref[here, LANES:]
        re.append(ur * c - ui * s)
        im.append(ui * c + ur * s)
    out, _ = small_fft(re, im, 1)
    for n in range(outer):
        cols = slice(n * LANES, (n + 1) * LANES)
        filtered_ref[:, cols] = out[n]
        val_ref[n] = out[n]
        key_ref[n] = (cycle_ref[:, cols] * NPHI + column_ref[:, cols]).astype(jnp.float32)
    tiles = outer
    tile_bits = tiles.bit_length() - 1
    total_bits = tile_bits + 10
    for level in range(1, total_bits + 1):
        if level > tile_bits:
            sort_inner(key_ref, val_ref, level, tile_bits, total_bits, min(16, tiles))
        sort_across(key_ref, val_ref, level, tile_bits, total_bits)
    keys = key_ref[...]
    last = jnp.max(jnp.max(keys, axis=0), axis=0, keepdims=True)
    first = jnp.min(jnp.min(keys, axis=0), axis=0, keepdims=True)
    row_len = tiles * SUB
    key_rows[:LANES, :] = keys.reshape(row_len, LANES).T
    val_rows[:LANES, :] = val_ref[...].reshape(row_len, LANES).T
    reach = key_rows.shape[0] - LANES
    key_rows[LANES:, :] = jnp.full((reach, row_len), 2.0 * buckets * span, jnp.float32)
    val_rows[LANES:, :] = jnp.zeros((reach, row_len), jnp.float32)
    over = jnp.int32(0)
    for b in range(buckets):
        begin = jnp.sum((last < float(b * span)).astype(jnp.float32)).astype(jnp.int32)
        end = jnp.sum((first < float((b + 1) * span)).astype(jnp.float32)).astype(jnp.int32)
        over = over + (end - begin > rows).astype(jnp.int32)
        begin = jnp.minimum(begin, LANES)
        aligned = pl.multiple_of((begin // SUB) * SUB, SUB)
        back = lax.rem(reach - (begin - aligned), reach)
        here = pl.ds(aligned, reach)
        dest, w = divmod(b, windows)
        taken = pltpu.roll(key_rows[here, :], back, axis=0)[:rows]
        send_ref[dest, w * rows:(w + 1) * rows, :] = taken - float(b * span)
        at = (windows + w) * rows
        send_ref[dest, at:at + rows, :] = pltpu.roll(val_rows[here, :], back, axis=0)[:rows]

    @pl.when(over > 0)
    def _():
        send_ref[...] = jnp.full(send_ref.shape, jnp.nan, jnp.float32)


def filter_and_sort(scan, resp, cycle, column, det_count, band_cycles):
    lines, length = scan.shape
    tiles = length // LANES
    windows = WINDOWS
    buckets = det_count * windows
    span = band_cycles * NPHI // buckets
    row_len = tiles * SUB
    rows = LANES // buckets + 2
    reach = (rows + 2 * SUB - 2) // SUB * SUB
    twiddle, forward, back = filter_tables(length)
    resp_rows = resp.reshape(lines, LANES, tiles).transpose(2, 0, 1).reshape(tiles * lines, LANES)
    body = functools.partial(sort_kernel, buckets=buckets, span=span, rows=rows, windows=windows)
    vmem = pl.BlockSpec(memory_space=pltpu.VMEM)
    return pl.pallas_call(
        body,
        out_shape=(
            jax.ShapeDtypeStruct((lines, length), jnp.float32),
            jax.ShapeDtypeStruct((det_count, 2 * windows * rows, row_len), jnp.float32),
        ),
        in_specs=[vmem] * 7,
        out_specs=(vmem, vmem),
        scratch_shapes=[
            pltpu.VMEM((tiles, SUB, LANES), jnp.float32),
            pltpu.VMEM((tiles, SUB, LANES), jnp.float32),
            pltpu.VMEM((tiles * lines, 2 * LANES), jnp.float32),
            pltpu.VMEM((LANES + reach, row_len), jnp.float32),
            pltpu.VMEM((LANES + reach, row_len), jnp.float32),
        ],
        compiler_params=pltpu.CompilerParams(vmem_limit_bytes=24 * 1024 * 1024),
        name="filter_sort",
    )(scan, resp_rows, cycle, column, jnp.asarray(twiddle), jnp.asarray(forward), jnp.asarray(back))


def split2(x):
    high = x.astype(jnp.bfloat16)
    low = (x - high.astype(jnp.float32)).astype(jnp.bfloat16)
    return high, low


def bin_kernel(
    me_ref, recv_ref, pick_ref, table_hi, table_lo, map_ref, *refs, windows, rows, window_cycles
):
    send_refs, (blocks_ref, left_a, left_b, right_a, right_b, acc_ref) = refs[:-6], refs[-6:]
    left_refs, right_refs = (left_a, left_b), (right_a, right_b)
    sources = recv_ref.shape[0]
    row_len = recv_ref.shape[2]
    parts = NPHI // ROW
    area = parts * window_cycles
    a_iota = lax.broadcasted_iota(jnp.int32, (area, row_len), 0).astype(jnp.float32).astype(jnp.bfloat16)
    b_iota = lax.broadcasted_iota(jnp.int32, (ROW, row_len), 0).astype(jnp.float32).astype(jnp.bfloat16)
    zero, one = jnp.zeros((), jnp.bfloat16), jnp.ones((), jnp.bfloat16)

    def build(e, w, slot):
        left, right = left_refs[slot], right_refs[slot]
        for r in range(rows):
            q = recv_ref[e, w * rows + r:w * rows + r + 1, :].astype(jnp.int32)
            v = recv_ref[e, (windows + w) * rows + r:(windows + w) * rows + r + 1, :]
            high, low = split2(v)
            cycle = q >> 11
            inside = (q >= 0) & (cycle < window_cycles)
            a = jnp.where(inside, ((q >> 8) & (parts - 1)) * window_cycles + cycle, -1)
            a = a.astype(jnp.float32).astype(jnp.bfloat16)
            b = (q & (ROW - 1)).astype(jnp.float32).astype(jnp.bfloat16)
            cols = slice(r * row_len, (r + 1) * row_len)
            hit = a_iota == a
            left[:area, cols] = jnp.where(hit, high, zero)
            left[area:2 * area, cols] = jnp.where(hit, low, zero)
            left[2 * area:, cols] = jnp.where(hit, one, zero)
            right[:, cols] = jnp.where(b_iota == b, one, zero)

    def multiply(slot):
        acc_ref[...] += lax.dot_general(
            left_refs[slot][...], right_refs[slot][...], NT, preferred_element_type=jnp.float32
        )

    build(0, 0, 0)
    for w in range(windows):
        acc_ref[...] = jnp.zeros(acc_ref.shape, jnp.float32)

        def body(i, carry):
            build(2 * i + 1, w, 1)
            multiply(0)
            build(jnp.minimum(2 * i + 2, sources - 1), w, 0)
            multiply(1)
            return carry

        lax.fori_loop(0, sources // 2 - 1, body, 0)
        build(sources - 1, w, 1)
        multiply(0)
        if w + 1 < windows:
            build(0, w + 1, 0)
        multiply(1)
        acc = acc_ref[...]
        sky = (acc[:area] + acc[area:2 * area]) / jnp.maximum(acc[2 * area:], 1.0)
        for c8 in range(parts):
            map_ref[w * window_cycles:(w + 1) * window_cycles, c8 * ROW:(c8 + 1) * ROW] = (
                sky[c8 * window_cycles:(c8 + 1) * window_cycles]
            )
    cycles = map_ref.shape[0]
    half = NPHI // 2
    modes = []
    for parity in (0, 1):
        a, b = map_ref[:, :half], map_ref[:, half:]
        high, low = split2(a + b if parity == 0 else a - b)
        first = jnp.dot(jnp.concatenate([high, low], axis=0), table_hi[parity], preferred_element_type=jnp.float32)
        second = jnp.dot(high, table_lo[parity], preferred_element_type=jnp.float32)
        modes.append(first[:cycles] + first[cycles:] + second)
    modes = jnp.concatenate(modes, axis=1)
    count = modes.shape[1]
    width = pick_ref.shape[1]
    high = modes.astype(jnp.bfloat16)
    rest = modes - high.astype(jnp.float32)
    middle = rest.astype(jnp.bfloat16)
    low = (rest - middle.astype(jnp.float32)).astype(jnp.bfloat16)
    pieces = jnp.concatenate([high, middle, low], axis=0)
    choose = (lax.broadcasted_iota(jnp.int32, (count, width), 0) == pick_ref[...])
    choose = jnp.where(choose, 1.0, 0.0).astype(jnp.bfloat16)
    moved = jnp.dot(pieces, choose, preferred_element_type=jnp.float32)
    moved = moved[:cycles] + moved[cycles:2 * cycles] + moved[2 * cycles:]
    owners, group_rows, lanes = blocks_ref.shape
    groups = cycles // group_rows
    lane_group = lax.broadcasted_iota(jnp.int32, (group_rows, lanes), 1) // (lanes // groups)
    values = recv_ref[:, windows * rows:, :]
    broken = jnp.max(jnp.where(values == values, 0.0, 1.0)) > 0.0
    for d in range(owners):
        block = moved[:, d * lanes:(d + 1) * lanes]
        out = block[:group_rows]
        for h in range(1, groups):
            out = jnp.where(lane_group == h, block[h * group_rows:(h + 1) * group_rows], out)
        blocks_ref[d] = jnp.where(broken, jnp.nan, out)
    for k in range(owners):
        send_refs[k][...] = blocks_ref[me_ref[0] ^ k]


def bin_and_modes(me, recv, order_slot, band_cycles):
    sources, lines, row_len = recv.shape
    windows = WINDOWS
    rows = lines // (2 * windows)
    cycles = band_cycles // sources
    count = order_slot.shape[0]
    slots = count // sources
    groups = LANES // (2 * slots)
    high, low = mode_tables(count)
    m = order_slot.reshape(sources, 1, 1, slots)
    part = jnp.arange(2, dtype=jnp.int32).reshape(1, 1, 2, 1)
    pick = (m & 1) * count + part * (count // 2) + (m >> 1)
    pick = jnp.broadcast_to(pick, (sources, groups, 2, slots)).reshape(1, sources * LANES)
    area = cycles // windows * (NPHI // ROW)
    depth = rows * row_len
    vmem = pl.BlockSpec(memory_space=pltpu.VMEM)
    return pl.pallas_call(
        functools.partial(bin_kernel, windows=windows, rows=rows, window_cycles=cycles // windows),
        out_shape=(
            jax.ShapeDtypeStruct((cycles, NPHI), jnp.float32),
        ) + (jax.ShapeDtypeStruct((cycles // groups, LANES), jnp.float32),) * sources,
        in_specs=[pl.BlockSpec(memory_space=pltpu.SMEM)] + [vmem] * 4,
        out_specs=(vmem,) * (sources + 1),
        scratch_shapes=[
            pltpu.VMEM((sources, cycles // groups, LANES), jnp.float32),
            pltpu.VMEM((3 * area, depth), jnp.bfloat16),
            pltpu.VMEM((3 * area, depth), jnp.bfloat16),
            pltpu.VMEM((ROW, depth), jnp.bfloat16),
            pltpu.VMEM((ROW, depth), jnp.bfloat16),
            pltpu.VMEM((3 * area, ROW), jnp.float32),
        ],
        compiler_params=pltpu.CompilerParams(vmem_limit_bytes=40 * 1024 * 1024),
        name="bin_modes",
    )(me, recv, pick, jnp.asarray(high), jnp.asarray(low))


def legendre_kernel(me_ref, *refs, sources, owners):
    recv_refs, table_ref = refs[:sources], refs[sources]
    out_refs = refs[sources + 1:sources + 1 + owners]
    leg_ref, arrived, modes_ref, wide_ref, block_ref, sums_ref = refs[sources + 1 + owners:]
    slots, band_cycles, degrees = table_ref.shape

    def load(slot):
        return pltpu.make_async_copy(table_ref.at[slot], leg_ref.at[slot], arrived.at[slot])

    def start(slot, carry):
        load(slot).start()
        return carry

    lax.fori_loop(0, slots, start, 0)
    group_rows, lanes = recv_refs[0].shape
    groups = lanes // (2 * slots)
    width = out_refs[0].shape[1]
    tiles = degrees // LANES
    cycles = group_rows * groups
    for k in range(sources):
        block = recv_refs[k][...]
        for h in range(groups):
            turned = block if h == 0 else pltpu.roll(block, lanes - h * 2 * slots, axis=1)
            block_ref[h * group_rows:(h + 1) * group_rows, :] = turned
        at = pl.multiple_of((me_ref[0] ^ k) * cycles, cycles)
        modes_ref[pl.ds(at, cycles), :] = block_ref[...]

    def widen(slot, half):
        turned = pltpu.roll(modes_ref[...], lax.rem(lanes - slot, lanes), axis=1)
        for c in range(2):
            column = turned[:, c * slots:c * slots + 1]
            wide_ref[half, c] = jnp.broadcast_to(column, (band_cycles, lanes))

    widen(0, 0)

    def body(slot, carry):
        half = slot & 1
        load(slot).wait()
        sums = [[jnp.zeros((SUB, LANES), jnp.float32) for _ in range(tiles)] for _ in range(2)]
        for r in range(0, band_cycles, SUB):
            factor = [wide_ref[half, c, r:r + SUB, :] for c in range(2)]
            for t in range(tiles):
                block = leg_ref[slot, r:r + SUB, t * LANES:(t + 1) * LANES]
                for c in range(2):
                    sums[c][t] = sums[c][t] + block * factor[c]
        widen(jnp.minimum(slot + 1, slots - 1), 1 - half)
        per_owner = width // LANES
        for c in range(2):
            lines = [jnp.sum(part, axis=0, keepdims=True) for part in sums[c]]
            for d in range(owners):
                line = jnp.concatenate(lines[d * per_owner:(d + 1) * per_owner], axis=1)
                sums_ref[d, pl.ds(c * slots + slot, 1), :] = line
        return carry

    lax.fori_loop(0, slots, body, 0)
    for k in range(owners):
        out_refs[k][...] = sums_ref[me_ref[1] ^ k]


def legendre_sums(me, recv, legendre, owners):
    slots, band_cycles, degrees = legendre.shape
    vmem = pl.BlockSpec(memory_space=pltpu.VMEM)
    return pl.pallas_call(
        functools.partial(legendre_kernel, sources=len(recv), owners=owners),
        out_shape=(jax.ShapeDtypeStruct((2 * slots, degrees // owners), jnp.float32),) * owners,
        in_specs=[pl.BlockSpec(memory_space=pltpu.SMEM)] + [vmem] * len(recv) + [pl.BlockSpec(memory_space=pl.ANY)],
        out_specs=(vmem,) * owners,
        scratch_shapes=[
            pltpu.VMEM(legendre.shape, jnp.float32),
            pltpu.SemaphoreType.DMA((slots,)),
            pltpu.VMEM((band_cycles, LANES), jnp.float32),
            pltpu.VMEM((2, 2, band_cycles, LANES), jnp.float32),
            pltpu.VMEM((band_cycles // len(recv), LANES), jnp.float32),
            pltpu.VMEM((owners, 2 * slots, degrees // owners), jnp.float32),
        ],
        compiler_params=pltpu.CompilerParams(vmem_limit_bytes=44 * 1024 * 1024),
        name="legendre_sums",
    )(me, *recv, legendre)


def exchange_and_sum(x, axis, count):
    parts = x.reshape(count, x.shape[0] // count, x.shape[1])
    return jnp.sum(lax.all_to_all(parts, axis, split_axis=0, concat_axis=0, tiled=True), axis=0)


def dense_path(filtered, cycle_offset, column, order_slot, legendre, det_count, band_count):
    band_cycles = legendre.shape[1]
    flat_index = (cycle_offset * NPHI + column).reshape(-1)
    empty = jnp.zeros((band_cycles * NPHI,), jnp.float32)
    partial_value = empty.at[flat_index].add(filtered.reshape(-1)).reshape(band_cycles, NPHI)
    counts = empty.at[flat_index].add(1.0).reshape(band_cycles, NPHI)
    summed = exchange_and_sum(partial_value, "det", det_count)
    hit_total = exchange_and_sum(counts, "det", det_count)
    sky_map = summed / jnp.maximum(hit_total, 1.0)
    pixel_index = jnp.arange(NPHI, dtype=jnp.int32)[:, None]
    phases = 2.0 * jnp.pi / NPHI * (pixel_index * order_slot[None, :] % NPHI).astype(jnp.float32)
    cycle_modes = jnp.stack([
        jnp.dot(sky_map, jnp.cos(phases), precision=precise),
        -jnp.dot(sky_map, jnp.sin(phases), precision=precise),
    ])
    slot_count, _, degrees = legendre.shape
    local_orders = lax.dynamic_slice_in_dim(order_slot, lax.axis_index("det") * slot_count, slot_count, 0)
    keep = jnp.arange(degrees, dtype=jnp.int32)[None, :] >= local_orders[:, None]
    terms = jnp.einsum(
        "crs,srl->csl",
        lax.all_to_all(cycle_modes, "det", split_axis=2, concat_axis=1, tiled=True),
        legendre,
        precision=precise,
    ) * keep.astype(jnp.float32)[None]
    harmonics = exchange_and_sum(terms.transpose(2, 0, 1).reshape(degrees, -1), "band", band_count)
    return harmonics.reshape(-1, 2, slot_count).transpose(1, 2, 0), sky_map


def swap_blocks(blocks, axis):
    count = len(blocks)
    return [blocks[0]] + [
        lax.ppermute(blocks[k], axis, [(i, i ^ k) for i in range(count)]) for k in range(1, count)
    ]


def local(scan_lines, response, cycle_offset, column, order_slot, legendre, *, det_count, band_count):
    slots, band_cycles, degrees = legendre.shape
    filtered, send = filter_and_sort(
        scan_lines, response, cycle_offset, column, det_count, band_cycles
    )
    me = jnp.stack([lax.axis_index("det"), lax.axis_index("band")]).astype(jnp.int32)
    recv = lax.all_to_all(send, "det", split_axis=0, concat_axis=0, tiled=True)
    sky_map, *modes = bin_and_modes(me, recv, order_slot, band_cycles)
    modes = swap_blocks(modes, "det")
    terms = swap_blocks(legendre_sums(me, modes, legendre, band_count), "band")
    sums = functools.reduce(jnp.add, terms)
    crowded = jnp.isnan(sums[0, 0])
    local_orders = lax.dynamic_slice_in_dim(order_slot, lax.axis_index("det") * slots, slots, 0)
    width = degrees // band_count
    degree = lax.axis_index("band") * width + jnp.arange(width, dtype=jnp.int32)
    keep = degree[None, None, :] >= local_orders[None, :, None]
    harmonics = jnp.where(keep, sums.reshape(2, slots, width), 0.0)
    return lax.cond(
        crowded,
        lambda: dense_path(
            filtered, cycle_offset, column, order_slot, legendre, det_count, band_count
        ),
        lambda: (harmonics, sky_map),
    )


def solution(mesh):
    sizes = dict(mesh.shape)
    return jax.shard_map(
        functools.partial(local, det_count=sizes["det"], band_count=sizes["band"]),
        mesh=mesh,
        in_specs=(
            P(("det", "band"), None),
            P(("det", "band"), None),
            P(("det", "band"), None),
            P(("det", "band"), None),
            P(),
            P("det", "band", None),
        ),
        out_specs=(P(None, "det", "band"), P(("band", "det"), None)),
        check_vma=False,
    )
```

```python
import functools

import jax
import jax.numpy as jnp
import numpy as np
from jax import lax
from jax.experimental import pallas as pl
from jax.experimental.pallas import tpu as pltpu
from jax.sharding import PartitionSpec as P

NPHI = 2048
LANES = 128
SUB = 8
WINDOWS = 2
ROW = 256

precise = lax.Precision.HIGHEST
NT = (((1,), (1,)), ((), ()))


def filter_tables(length):
    outer = length // LANES
    k1 = np.arange(outer)[:, None]
    n2 = np.arange(LANES)[None, :]
    turn = 2.0 * np.pi * ((k1 * n2) % length) / length
    twiddle = np.concatenate([np.cos(turn), np.sin(turn)], axis=1)
    a = np.arange(LANES)
    angle = 2.0 * np.pi * (np.outer(a, a) % LANES) / LANES
    c, s = np.cos(angle), np.sin(angle)
    forward = np.block([[c, -s], [s, c]])
    return twiddle.astype(np.float32), forward.astype(np.float32)


def mode_tables(count):
    half = NPHI // 2
    p = np.arange(half)[:, None]
    out = []
    for parity in (0, 1):
        m = 2 * np.arange(count // 2)[None, :] + parity
        angle = 2.0 * np.pi * ((p * m) % NPHI) / NPHI
        out.append(np.concatenate([np.cos(angle), -np.sin(angle)], axis=1))
    table = np.stack(out).astype(np.float32)
    high = table.astype(jnp.bfloat16)
    low = (table - high.astype(np.float32)).astype(jnp.bfloat16)
    return high, low


def small_fft(re, im, sign):
    count = len(re)
    if count == 1:
        return re, im
    even_re, even_im = small_fft(re[0::2], None if im is None else im[0::2], sign)
    odd_re, odd_im = small_fft(re[1::2], None if im is None else im[1::2], sign)
    half = count // 2
    out_re, out_im = [None] * count, [None] * count
    for k in range(half):
        wr = float(np.cos(2 * np.pi * k / count))
        wi = float(sign * np.sin(2 * np.pi * k / count))
        er, ei, orr, oi = even_re[k], even_im and even_im[k], odd_re[k], odd_im and odd_im[k]
        if k == 0:
            tr, ti = orr, oi
        elif 4 * k == count:
            tr = None if oi is None else -wi * oi
            ti = wi * orr
        elif oi is None:
            tr, ti = wr * orr, wi * orr
        else:
            tr, ti = wr * orr - wi * oi, wr * oi + wi * orr
        out_re[k] = er if tr is None else er + tr
        out_re[k + half] = er if tr is None else er - tr
        if ti is None:
            out_im[k] = out_im[k + half] = ei
        else:
            out_im[k] = ti if ei is None else ei + ti
            out_im[k + half] = -ti if ei is None else ei - ti
    if all(x is None for x in out_im):
        return out_re, None
    out_im = [jnp.zeros_like(out_re[0]) if x is None else x for x in out_im]
    return out_re, out_im


class Places:
    def __init__(self, tile_bits, total_bits):
        self.tile_bits, self.total_bits = tile_bits, total_bits
        self.of = list(range(total_bits))
        for level in range(tile_bits + 1, total_bits + 1):
            self.walk(level)
        held = [self.of.index(place) for place in range(total_bits)]
        self.of = held

    def swap(self, bit):
        other = self.of.index(0)
        self.of[bit], self.of[other] = 0, self.of[bit]

    def walk(self, level):
        for bit in range(level - 1, self.tile_bits - 1, -1):
            self.swap(bit)
        self.swap(0)

    def axis_distance(self, bit):
        place = self.of[bit] - self.tile_bits
        return (0, 1 << place) if place < 3 else (1, 1 << (place - 3))

    def mask(self, bit):
        axis, distance = self.axis_distance(bit)
        return (lax.broadcasted_iota(jnp.int32, (SUB, LANES), axis) & distance) != 0


def trade(low, high, upper, axis, distance):
    axis += low.ndim - 2
    size = low.shape[axis]
    return (
        jnp.where(upper, pltpu.roll(high, distance, axis=axis), low),
        jnp.where(upper, high, pltpu.roll(low, size - distance, axis=axis)),
    )


def exchange(keys, vals, a, b, down):
    if down is True:
        swap = keys[a] < keys[b]
    else:
        swap = keys[a] > keys[b]
        if down is not False:
            swap = jnp.logical_xor(swap, down)
    keys[a], keys[b] = jnp.where(swap, keys[b], keys[a]), jnp.where(swap, keys[a], keys[b])
    vals[a], vals[b] = jnp.where(swap, vals[b], vals[a]), jnp.where(swap, vals[a], vals[b])


def sort_inner(key_ref, val_ref, level, places, group):
    pairs = key_ref.shape[0]
    steps = []
    down = places.mask(level) if level < places.total_bits else False
    for bit in range(level - 1, places.tile_bits - 1, -1):
        steps.append((places.mask(bit),) + places.axis_distance(bit))
        places.swap(bit)

    def body(g, carry):
        part = pl.ds(g * group, group)
        keys = [key_ref[part, 0], key_ref[part, 1]]
        vals = [val_ref[part, 0], val_ref[part, 1]]
        for upper, axis, distance in steps:
            keys = list(trade(*keys, upper, axis, distance))
            vals = list(trade(*vals, upper, axis, distance))
            exchange(keys, vals, 0, 1, down)
        for i in range(2):
            key_ref[part, i] = keys[i]
            val_ref[part, i] = vals[i]
        return carry

    lax.fori_loop(0, pairs // group, body, 0)


def sort_across(key_ref, val_ref, level, places):
    tiles = 2 * key_ref.shape[0]
    tile_bits = places.tile_bits
    mask = places.mask(level) if tile_bits <= level < places.total_bits else None
    back = None
    if level > tile_bits:
        back = (places.mask(0),) + places.axis_distance(0)
        places.swap(0)
    bits = list(range(min(level, tile_bits) - 1, -1, -1))
    for chosen in [bits[:-3], bits[-3:]] if len(bits) > 3 else [bits]:
        low = min(chosen)
        members, stride = 1 << len(chosen), 1 << low
        for g in range(tiles // members):
            base = (g // stride) * (members * stride) + g % stride
            spots = [divmod(base + i * stride, 2) for i in range(members)]
            keys = [key_ref[spot] for spot in spots]
            vals = [val_ref[spot] for spot in spots]
            for bit in chosen:
                step = 1 << (bit - low)
                for i in range(members):
                    if i & step:
                        continue
                    if bit == 0 and back is not None:
                        keys[i], keys[i + 1] = trade(keys[i], keys[i + 1], *back)
                        vals[i], vals[i + 1] = trade(vals[i], vals[i + 1], *back)
                    down = mask
                    if level >= places.total_bits:
                        down = False
                    elif level < tile_bits:
                        down = ((base + i * stride) >> level) & 1 == 1
                    exchange(keys, vals, i, i + step, down)
            for spot, key, val in zip(spots, keys, vals):
                key_ref[spot] = key
                val_ref[spot] = val


def sort_kernel(
    scan_hbm, resp_hbm, cycle_hbm, column_hbm, twiddle_hbm, forward_hbm,
    filtered_ref, send_ref,
    scan_ref, resp_ref, cycle_ref, column_ref, twiddle_ref, forward_ref, arrived,
    key_ref, val_ref, spec_ref, key_rows, val_rows,
    *, buckets, span, rows, windows,
):
    lines, length = scan_ref.shape
    outer = length // LANES
    loads = [
        pltpu.make_async_copy(source, place, arrived.at[i])
        for i, (source, place) in enumerate([
            (scan_hbm, scan_ref), (twiddle_hbm, twiddle_ref), (forward_hbm, forward_ref),
            (resp_hbm, resp_ref), (cycle_hbm, cycle_ref), (column_hbm, column_ref),
        ])
    ]
    for load in loads:
        load.start()
    loads[0].wait()
    re, im = small_fft([scan_ref[:, n * LANES:(n + 1) * LANES] for n in range(outer)], None, -1)
    loads[1].wait()
    for k in range(outer):
        c, s = twiddle_ref[k:k + 1, :LANES], twiddle_ref[k:k + 1, LANES:]
        here = pl.ds(k * lines, lines)
        spec_ref[here, :LANES] = re[k] * c + im[k] * s
        spec_ref[here, LANES:] = im[k] * c - re[k] * s
    for load in loads[2:]:
        load.wait()
    spec = jnp.dot(spec_ref[...], forward_ref[...], precision=precise, preferred_element_type=jnp.float32)
    resp = resp_ref[...] * (1.0 / length)
    spec = spec * jnp.concatenate([resp, resp], axis=1)
    spec_ref[...] = lax.dot_general(
        spec, forward_ref[...], NT, precision=precise, preferred_element_type=jnp.float32
    )
    re, im = [], []
    for k in range(outer):
        c, s = twiddle_ref[k:k + 1, :LANES], twiddle_ref[k:k + 1, LANES:]
        here = pl.ds(k * lines, lines)
        ur, ui = spec_ref[here, :LANES], spec_ref[here, LANES:]
        re.append(ur * c - ui * s)
        im.append(ui * c + ur * s)
    out, _ = small_fft(re, im, 1)
    for n in range(outer):
        cols = slice(n * LANES, (n + 1) * LANES)
        filtered_ref[:, cols] = out[n]
        val_ref[divmod(n, 2)] = out[n]
        key_ref[divmod(n, 2)] = (cycle_ref[:, cols] * NPHI + column_ref[:, cols]).astype(jnp.float32)
    tiles = outer
    tile_bits = tiles.bit_length() - 1
    places = Places(tile_bits, tile_bits + 10)
    for level in range(1, places.total_bits + 1):
        if level > tile_bits:
            sort_inner(key_ref, val_ref, level, places, min(8, tiles // 2))
        sort_across(key_ref, val_ref, level, places)
    assert places.of == list(range(places.total_bits))
    row_len = tiles * SUB
    keys = key_ref[...].reshape(tiles, SUB, LANES)
    last = jnp.max(jnp.max(keys, axis=0), axis=0, keepdims=True)
    first = jnp.min(jnp.min(keys, axis=0), axis=0, keepdims=True)
    key_rows[:LANES, :] = keys.reshape(row_len, LANES).T
    val_rows[:LANES, :] = val_ref[...].reshape(row_len, LANES).T
    reach = key_rows.shape[0] - LANES
    key_rows[LANES:, :] = jnp.full((reach, row_len), 2.0 * buckets * span, jnp.float32)
    val_rows[LANES:, :] = jnp.zeros((reach, row_len), jnp.float32)
    over = jnp.int32(0)
    for b in range(buckets):
        begin = jnp.sum((last < float(b * span)).astype(jnp.float32)).astype(jnp.int32)
        end = jnp.sum((first < float((b + 1) * span)).astype(jnp.float32)).astype(jnp.int32)
        over = over + (end - begin > rows).astype(jnp.int32)
        begin = jnp.minimum(begin, LANES)
        aligned = pl.multiple_of((begin // SUB) * SUB, SUB)
        back = lax.rem(reach - (begin - aligned), reach)
        here = pl.ds(aligned, reach)
        dest, w = divmod(b, windows)
        taken = pltpu.roll(key_rows[here, :], back, axis=0)[:rows]
        send_ref[dest, w * rows:(w + 1) * rows, :] = taken - float(b * span)
        at = (windows + w) * rows
        send_ref[dest, at:at + rows, :] = pltpu.roll(val_rows[here, :], back, axis=0)[:rows]

    @pl.when(over > 0)
    def _():
        send_ref[...] = jnp.full(send_ref.shape, jnp.nan, jnp.float32)


def filter_and_sort(scan, resp, cycle, column, det_count, band_cycles):
    lines, length = scan.shape
    tiles = length // LANES
    windows = WINDOWS
    buckets = det_count * windows
    span = band_cycles * NPHI // buckets
    row_len = tiles * SUB
    rows = LANES // buckets + 2
    reach = (rows + 2 * SUB - 2) // SUB * SUB
    twiddle, forward = filter_tables(length)
    resp_rows = resp.reshape(lines, LANES, tiles).transpose(2, 0, 1).reshape(tiles * lines, LANES)
    operands = [scan, resp_rows, cycle, column, jnp.asarray(twiddle), jnp.asarray(forward)]
    body = functools.partial(sort_kernel, buckets=buckets, span=span, rows=rows, windows=windows)
    vmem = pl.BlockSpec(memory_space=pltpu.VMEM)
    return pl.pallas_call(
        body,
        out_shape=(
            jax.ShapeDtypeStruct((lines, length), jnp.float32),
            jax.ShapeDtypeStruct((det_count, 2 * windows * rows, row_len), jnp.float32),
        ),
        in_specs=[pl.BlockSpec(memory_space=pltpu.HBM)] * len(operands),
        out_specs=(vmem, vmem),
        scratch_shapes=[pltpu.VMEM(x.shape, x.dtype) for x in operands] + [
            pltpu.SemaphoreType.DMA((len(operands),)),
            pltpu.VMEM((tiles // 2, 2, SUB, LANES), jnp.float32),
            pltpu.VMEM((tiles // 2, 2, SUB, LANES), jnp.float32),
            pltpu.VMEM((tiles * lines, 2 * LANES), jnp.float32),
            pltpu.VMEM((LANES + reach, row_len), jnp.float32),
            pltpu.VMEM((LANES + reach, row_len), jnp.float32),
        ],
        compiler_params=pltpu.CompilerParams(vmem_limit_bytes=24 * 1024 * 1024),
        name="filter_sort",
    )(*operands)


def split2(x):
    high = x.astype(jnp.bfloat16)
    low = (x - high.astype(jnp.float32)).astype(jnp.bfloat16)
    return high, low


def bin_kernel(
    recv_ref, pick_ref, table_hi, table_lo, map_ref, send_ref, flag_ref,
    left_a, left_b, right_a, right_b, acc_ref, *, windows, rows, window_cycles
):
    left_refs, right_refs = (left_a, left_b), (right_a, right_b)
    sources = recv_ref.shape[0]
    row_len = recv_ref.shape[2]
    parts = NPHI // ROW
    area = parts * window_cycles
    a_iota = lax.broadcasted_iota(jnp.int32, (area, row_len), 0).astype(jnp.float32).astype(jnp.bfloat16)
    b_iota = lax.broadcasted_iota(jnp.int32, (ROW, row_len), 0).astype(jnp.float32).astype(jnp.bfloat16)
    zero, one = jnp.zeros((), jnp.bfloat16), jnp.ones((), jnp.bfloat16)

    def build(e, w, slot):
        left, right = left_refs[slot], right_refs[slot]
        for r in range(rows):
            q = recv_ref[e, w * rows + r:w * rows + r + 1, :].astype(jnp.int32)
            v = recv_ref[e, (windows + w) * rows + r:(windows + w) * rows + r + 1, :]
            high, low = split2(v)
            cycle = q >> 11
            inside = (q >= 0) & (cycle < window_cycles)
            a = jnp.where(inside, ((q >> 8) & (parts - 1)) * window_cycles + cycle, -1)
            a = a.astype(jnp.float32).astype(jnp.bfloat16)
            b = (q & (ROW - 1)).astype(jnp.float32).astype(jnp.bfloat16)
            cols = slice(r * row_len, (r + 1) * row_len)
            hit = a_iota == a
            left[:area, cols] = jnp.where(hit, high, zero)
            left[area:2 * area, cols] = jnp.where(hit, low, zero)
            left[2 * area:, cols] = jnp.where(hit, one, zero)
            right[:, cols] = jnp.where(b_iota == b, one, zero)

    def multiply(slot):
        acc_ref[...] += lax.dot_general(
            left_refs[slot][...], right_refs[slot][...], NT, preferred_element_type=jnp.float32
        )

    build(0, 0, 0)
    for w in range(windows):
        acc_ref[...] = jnp.zeros(acc_ref.shape, jnp.float32)

        def body(i, carry):
            build(2 * i + 1, w, 1)
            multiply(0)
            build(jnp.minimum(2 * i + 2, sources - 1), w, 0)
            multiply(1)
            return carry

        lax.fori_loop(0, sources // 2 - 1, body, 0)
        build(sources - 1, w, 1)
        multiply(0)
        if w + 1 < windows:
            build(0, w + 1, 0)
        multiply(1)
        acc = acc_ref[...]
        sky = (acc[:area] + acc[area:2 * area]) / jnp.maximum(acc[2 * area:], 1.0)
        for c8 in range(parts):
            map_ref[w * window_cycles:(w + 1) * window_cycles, c8 * ROW:(c8 + 1) * ROW] = (
                sky[c8 * window_cycles:(c8 + 1) * window_cycles]
            )
    cycles = map_ref.shape[0]
    half = NPHI // 2
    modes = []
    for parity in (0, 1):
        a, b = map_ref[:, :half], map_ref[:, half:]
        high, low = split2(a + b if parity == 0 else a - b)
        first = jnp.dot(jnp.concatenate([high, low], axis=0), table_hi[parity], preferred_element_type=jnp.float32)
        second = jnp.dot(high, table_lo[parity], preferred_element_type=jnp.float32)
        modes.append(first[:cycles] + first[cycles:] + second)
    modes = jnp.concatenate(modes, axis=1)
    count = modes.shape[1]
    width = pick_ref.shape[1]
    high = modes.astype(jnp.bfloat16)
    rest = modes - high.astype(jnp.float32)
    middle = rest.astype(jnp.bfloat16)
    low = (rest - middle.astype(jnp.float32)).astype(jnp.bfloat16)
    pieces = jnp.concatenate([high, middle, low], axis=0)
    choose = (lax.broadcasted_iota(jnp.int32, (count, width), 0) == pick_ref[...])
    choose = jnp.where(choose, 1.0, 0.0).astype(jnp.bfloat16)
    moved = jnp.dot(pieces, choose, preferred_element_type=jnp.float32)
    moved = moved[:cycles] + moved[cycles:2 * cycles] + moved[2 * cycles:]
    owners, group_rows, lanes = send_ref.shape
    groups = cycles // group_rows
    lane_group = lax.broadcasted_iota(jnp.int32, (group_rows, lanes), 1) // (lanes // groups)
    values = recv_ref[:, windows * rows:, :]
    flag_ref[0] = (jnp.max(jnp.where(values == values, 0.0, 1.0)) > 0.0).astype(jnp.int32)
    for d in range(owners):
        block = moved[:, d * lanes:(d + 1) * lanes]
        out = block[:group_rows]
        for h in range(1, groups):
            out = jnp.where(lane_group == h, block[h * group_rows:(h + 1) * group_rows], out)
        send_ref[d] = out


def bin_and_modes(recv, order_slot, band_cycles):
    sources, lines, row_len = recv.shape
    windows = WINDOWS
    rows = lines // (2 * windows)
    cycles = band_cycles // sources
    count = order_slot.shape[0]
    slots = count // sources
    groups = LANES // (2 * slots)
    high, low = mode_tables(count)
    m = order_slot.reshape(sources, 1, 1, slots)
    part = jnp.arange(2, dtype=jnp.int32).reshape(1, 1, 2, 1)
    pick = (m & 1) * count + part * (count // 2) + (m >> 1)
    pick = jnp.broadcast_to(pick, (sources, groups, 2, slots)).reshape(1, sources * LANES)
    area = cycles // windows * (NPHI // ROW)
    depth = rows * row_len
    vmem = pl.BlockSpec(memory_space=pltpu.VMEM)
    return pl.pallas_call(
        functools.partial(bin_kernel, windows=windows, rows=rows, window_cycles=cycles // windows),
        out_shape=(
            jax.ShapeDtypeStruct((cycles, NPHI), jnp.float32),
            jax.ShapeDtypeStruct((sources, cycles // groups, LANES), jnp.float32),
            jax.ShapeDtypeStruct((1,), jnp.int32),
        ),
        in_specs=[vmem] * 4,
        out_specs=(vmem, vmem, pl.BlockSpec(memory_space=pltpu.SMEM)),
        scratch_shapes=[
            pltpu.VMEM((3 * area, depth), jnp.bfloat16),
            pltpu.VMEM((3 * area, depth), jnp.bfloat16),
            pltpu.VMEM((ROW, depth), jnp.bfloat16),
            pltpu.VMEM((ROW, depth), jnp.bfloat16),
            pltpu.VMEM((3 * area, ROW), jnp.float32),
        ],
        compiler_params=pltpu.CompilerParams(vmem_limit_bytes=40 * 1024 * 1024),
        name="bin_modes",
    )(recv, pick, jnp.asarray(high), jnp.asarray(low))


def legendre_kernel(me_ref, recv_ref, table_ref, *refs, owners):
    out_refs, (leg_ref, arrived, modes_ref, wide_ref, sums_ref) = refs[:owners], refs[owners:]
    slots, band_cycles, degrees = table_ref.shape

    def load(slot):
        return pltpu.make_async_copy(table_ref.at[slot], leg_ref.at[slot], arrived.at[slot])

    def start(slot, carry):
        load(slot).start()
        return carry

    lax.fori_loop(0, slots, start, 0)
    sources, group_rows, lanes = recv_ref.shape
    groups = lanes // (2 * slots)
    width = out_refs[0].shape[1]
    tiles = degrees // LANES
    for e in range(sources):
        block = recv_ref[e]
        for h in range(groups):
            at = (e * groups + h) * group_rows
            turned = block if h == 0 else pltpu.roll(block, lanes - h * 2 * slots, axis=1)
            modes_ref[at:at + group_rows, :] = turned

    def widen(slot, half):
        turned = pltpu.roll(modes_ref[...], lax.rem(lanes - slot, lanes), axis=1)
        for c in range(2):
            column = turned[:, c * slots:c * slots + 1]
            wide_ref[half, c] = jnp.broadcast_to(column, (band_cycles, lanes))

    widen(0, 0)

    def body(slot, carry):
        half = slot & 1
        load(slot).wait()
        sums = [[jnp.zeros((SUB, LANES), jnp.float32) for _ in range(tiles)] for _ in range(2)]
        for r in range(0, band_cycles, SUB):
            factor = [wide_ref[half, c, r:r + SUB, :] for c in range(2)]
            for t in range(tiles):
                block = leg_ref[slot, r:r + SUB, t * LANES:(t + 1) * LANES]
                for c in range(2):
                    sums[c][t] = sums[c][t] + block * factor[c]
        widen(jnp.minimum(slot + 1, slots - 1), 1 - half)
        per_owner = width // LANES
        for c in range(2):
            lines = [jnp.sum(part, axis=0, keepdims=True) for part in sums[c]]
            for d in range(owners):
                line = jnp.concatenate(lines[d * per_owner:(d + 1) * per_owner], axis=1)
                sums_ref[d, pl.ds(c * slots + slot, 1), :] = line
        return carry

    lax.fori_loop(0, slots, body, 0)
    for k in range(owners):
        out_refs[k][...] = sums_ref[me_ref[0] ^ k]


def legendre_sums(me, recv, legendre, owners):
    slots, band_cycles, degrees = legendre.shape
    vmem = pl.BlockSpec(memory_space=pltpu.VMEM)
    return pl.pallas_call(
        functools.partial(legendre_kernel, owners=owners),
        out_shape=(jax.ShapeDtypeStruct((2 * slots, degrees // owners), jnp.float32),) * owners,
        in_specs=[pl.BlockSpec(memory_space=pltpu.SMEM), vmem, pl.BlockSpec(memory_space=pl.ANY)],
        out_specs=(vmem,) * owners,
        scratch_shapes=[
            pltpu.VMEM(legendre.shape, jnp.float32),
            pltpu.SemaphoreType.DMA((slots,)),
            pltpu.VMEM((band_cycles, LANES), jnp.float32),
            pltpu.VMEM((2, 2, band_cycles, LANES), jnp.float32),
            pltpu.VMEM((owners, 2 * slots, degrees // owners), jnp.float32),
        ],
        compiler_params=pltpu.CompilerParams(vmem_limit_bytes=44 * 1024 * 1024),
        name="legendre_sums",
    )(me, recv, legendre)


def exchange_and_sum(x, axis, count):
    parts = x.reshape(count, x.shape[0] // count, x.shape[1])
    return jnp.sum(lax.all_to_all(parts, axis, split_axis=0, concat_axis=0, tiled=True), axis=0)


def dense_path(filtered, cycle_offset, column, order_slot, band_cycles, det_count):
    flat_index = (cycle_offset * NPHI + column).reshape(-1)
    empty = jnp.zeros((band_cycles * NPHI,), jnp.float32)
    partial_value = empty.at[flat_index].add(filtered.reshape(-1)).reshape(band_cycles, NPHI)
    counts = empty.at[flat_index].add(1.0).reshape(band_cycles, NPHI)
    summed = exchange_and_sum(partial_value, "det", det_count)
    hit_total = exchange_and_sum(counts, "det", det_count)
    sky_map = summed / jnp.maximum(hit_total, 1.0)
    pixel_index = jnp.arange(NPHI, dtype=jnp.int32)[:, None]
    phases = 2.0 * jnp.pi / NPHI * (pixel_index * order_slot[None, :] % NPHI).astype(jnp.float32)
    modes = jnp.stack([
        jnp.dot(sky_map, jnp.cos(phases), precision=precise),
        -jnp.dot(sky_map, jnp.sin(phases), precision=precise),
    ])
    slots = order_slot.shape[0] // det_count
    groups = LANES // (2 * slots)
    blocks = modes.reshape(2, groups, -1, det_count, slots).transpose(3, 2, 1, 0, 4)
    blocks = blocks.reshape(det_count, -1, LANES)
    return sky_map, lax.all_to_all(blocks, "det", split_axis=0, concat_axis=0, tiled=True)


def swap_blocks(blocks, axis):
    count = len(blocks)
    return [blocks[0]] + [
        lax.ppermute(blocks[k], axis, [(i, i ^ k) for i in range(count)]) for k in range(1, count)
    ]


def local(scan_lines, response, cycle_offset, column, order_slot, legendre, *, det_count, band_count):
    slots, band_cycles, degrees = legendre.shape
    filtered, send = filter_and_sort(
        scan_lines, response, cycle_offset, column, det_count, band_cycles
    )
    recv = lax.all_to_all(send, "det", split_axis=0, concat_axis=0, tiled=True)
    sky_map, modes, crowded = bin_and_modes(recv, order_slot, band_cycles)
    modes = lax.all_to_all(modes, "det", split_axis=0, concat_axis=0, tiled=True)
    sky_map, modes = lax.cond(
        crowded[0] > 0,
        lambda: dense_path(filtered, cycle_offset, column, order_slot, band_cycles, det_count),
        lambda: (sky_map, modes),
    )
    band = lax.axis_index("band").astype(jnp.int32)
    terms = swap_blocks(legendre_sums(band.reshape(1), modes, legendre, band_count), "band")
    sums = functools.reduce(jnp.add, terms)
    local_orders = lax.dynamic_slice_in_dim(order_slot, lax.axis_index("det") * slots, slots, 0)
    width = degrees // band_count
    degree = band * width + jnp.arange(width, dtype=jnp.int32)
    keep = degree[None, None, :] >= local_orders[None, :, None]
    return jnp.where(keep, sums.reshape(2, slots, width), 0.0), sky_map


def solution(mesh):
    sizes = dict(mesh.shape)
    return jax.shard_map(
        functools.partial(local, det_count=sizes["det"], band_count=sizes["band"]),
        mesh=mesh,
        in_specs=(
            P(("det", "band"), None),
            P(("det", "band"), None),
            P(("det", "band"), None),
            P(("det", "band"), None),
            P(),
            P("det", "band", None),
        ),
        out_specs=(P(None, "det", "band"), P(("band", "det"), None)),
        check_vma=False,
    )
```

```python
import functools

import jax
import jax.numpy as jnp
import numpy as np
from jax import lax
from jax.experimental import pallas as pl
from jax.experimental.pallas import tpu as pltpu
from jax.sharding import PartitionSpec as P

NPHI = 2048
LANES = 128
SUB = 8
WINDOWS = 2
ROW = 256

precise = lax.Precision.HIGHEST
NT = (((1,), (1,)), ((), ()))


def filter_tables(length):
    outer = length // LANES
    k1 = np.arange(outer)[:, None]
    n2 = np.arange(LANES)[None, :]
    turn = 2.0 * np.pi * ((k1 * n2) % length) / length
    twiddle = np.concatenate([np.cos(turn), np.sin(turn)], axis=1)
    a = np.arange(LANES)
    angle = 2.0 * np.pi * (np.outer(a, a) % LANES) / LANES
    c, s = np.cos(angle), np.sin(angle)
    forward = np.block([[c, -s], [s, c]])
    return twiddle.astype(np.float32), forward.astype(np.float32)


def mode_tables(count):
    half = NPHI // 2
    p = np.arange(half)[:, None]
    out = []
    for parity in (0, 1):
        m = 2 * np.arange(count // 2)[None, :] + parity
        angle = 2.0 * np.pi * ((p * m) % NPHI) / NPHI
        out.append(np.concatenate([np.cos(angle), -np.sin(angle)], axis=1))
    table = np.stack(out).astype(np.float32)
    high = table.astype(jnp.bfloat16)
    low = (table - high.astype(np.float32)).astype(jnp.bfloat16)
    return high, low


def small_fft(re, im, sign):
    count = len(re)
    if count == 1:
        return re, im
    even_re, even_im = small_fft(re[0::2], None if im is None else im[0::2], sign)
    odd_re, odd_im = small_fft(re[1::2], None if im is None else im[1::2], sign)
    half = count // 2
    out_re, out_im = [None] * count, [None] * count
    for k in range(half):
        wr = float(np.cos(2 * np.pi * k / count))
        wi = float(sign * np.sin(2 * np.pi * k / count))
        er, ei, orr, oi = even_re[k], even_im and even_im[k], odd_re[k], odd_im and odd_im[k]
        if k == 0:
            tr, ti = orr, oi
        elif 4 * k == count:
            tr = None if oi is None else -wi * oi
            ti = wi * orr
        elif oi is None:
            tr, ti = wr * orr, wi * orr
        else:
            tr, ti = wr * orr - wi * oi, wr * oi + wi * orr
        out_re[k] = er if tr is None else er + tr
        out_re[k + half] = er if tr is None else er - tr
        if ti is None:
            out_im[k] = out_im[k + half] = ei
        else:
            out_im[k] = ti if ei is None else ei + ti
            out_im[k + half] = -ti if ei is None else ei - ti
    if all(x is None for x in out_im):
        return out_re, None
    out_im = [jnp.zeros_like(out_re[0]) if x is None else x for x in out_im]
    return out_re, out_im


class Places:
    def __init__(self, tile_bits, total_bits):
        self.tile_bits, self.total_bits = tile_bits, total_bits
        self.of = list(range(total_bits))
        for level in range(tile_bits + 1, total_bits + 1):
            self.walk(level)
        held = [self.of.index(place) for place in range(total_bits)]
        self.of = held

    def swap(self, bit):
        other = self.of.index(0)
        self.of[bit], self.of[other] = 0, self.of[bit]

    def walk(self, level):
        for bit in range(level - 1, self.tile_bits - 1, -1):
            self.swap(bit)
        self.swap(0)

    def axis_distance(self, bit):
        place = self.of[bit] - self.tile_bits
        return (0, 1 << place) if place < 3 else (1, 1 << (place - 3))

    def mask(self, bit):
        axis, distance = self.axis_distance(bit)
        return (lax.broadcasted_iota(jnp.int32, (SUB, LANES), axis) & distance) != 0


def trade(low, high, upper, axis, distance):
    axis += low.ndim - 2
    size = low.shape[axis]
    return (
        jnp.where(upper, pltpu.roll(high, distance, axis=axis), low),
        jnp.where(upper, high, pltpu.roll(low, size - distance, axis=axis)),
    )


def exchange(keys, vals, a, b, down):
    if down:
        a, b = b, a
    swap = keys[a] > keys[b]
    keys[a], keys[b] = jnp.minimum(keys[a], keys[b]), jnp.maximum(keys[a], keys[b])
    vals[a], vals[b] = jnp.where(swap, vals[b], vals[a]), jnp.where(swap, vals[a], vals[b])


def sort_registers(keys, vals):
    tiles = len(keys)
    tile_bits = tiles.bit_length() - 1
    places = Places(tile_bits, tile_bits + 10)

    def flip(bit):
        return jnp.where(places.mask(bit), -1.0, 1.0)

    def trade_all(bit):
        upper, (axis, distance) = places.mask(bit), places.axis_distance(bit)
        places.swap(bit)
        for i in range(0, tiles, 2):
            keys[i], keys[i + 1] = trade(keys[i], keys[i + 1], upper, axis, distance)
            vals[i], vals[i + 1] = trade(vals[i], vals[i + 1], upper, axis, distance)

    for level in range(1, places.total_bits + 1):
        if level >= tile_bits:
            sign = 1.0
            if level > tile_bits:
                sign = flip(level - 1)
            if level < places.total_bits:
                sign = sign * flip(level)
            for i in range(tiles):
                keys[i] = keys[i] * sign
        for bit in range(level - 1, -1, -1):
            if bit >= tile_bits or (bit == 0 and level > tile_bits):
                trade_all(bit)
            step = 1 << bit if bit < tile_bits else 1
            for i in range(tiles):
                if not i & step:
                    exchange(keys, vals, i, i + step, level < tile_bits and (i >> level) & 1 == 1)
    assert places.of == list(range(places.total_bits))


def sort_kernel(
    me_ref, scan_hbm, resp_hbm, cycle_hbm, column_hbm, twiddle_hbm, forward_hbm, filtered_ref, *refs,
    buckets, span, rows, windows,
):
    send_refs, refs = refs[:buckets // windows], refs[buckets // windows:]
    scan_ref, resp_ref, cycle_ref, column_ref, twiddle_ref, forward_ref, arrived = refs[:7]
    key_ref, val_ref, spec_ref, key_rows, val_rows = refs[7:]
    lines, length = scan_ref.shape
    outer = length // LANES
    loads = [
        pltpu.make_async_copy(source, place, arrived.at[i])
        for i, (source, place) in enumerate([
            (scan_hbm, scan_ref), (twiddle_hbm, twiddle_ref), (forward_hbm, forward_ref),
            (resp_hbm, resp_ref), (cycle_hbm, cycle_ref), (column_hbm, column_ref),
        ])
    ]
    for load in loads:
        load.start()
    loads[0].wait()
    re, im = small_fft([scan_ref[:, n * LANES:(n + 1) * LANES] for n in range(outer)], None, -1)
    loads[1].wait()
    for k in range(outer):
        c, s = twiddle_ref[k:k + 1, :LANES], twiddle_ref[k:k + 1, LANES:]
        here = pl.ds(k * lines, lines)
        spec_ref[here, :LANES] = re[k] * c + im[k] * s
        spec_ref[here, LANES:] = im[k] * c - re[k] * s
    for load in loads[2:]:
        load.wait()
    spec = jnp.dot(spec_ref[...], forward_ref[...], precision=precise, preferred_element_type=jnp.float32)
    resp = resp_ref[...] * (1.0 / length)
    spec = spec * jnp.concatenate([resp, resp], axis=1)
    spec_ref[...] = lax.dot_general(
        spec, forward_ref[...], NT, precision=precise, preferred_element_type=jnp.float32
    )
    re, im = [], []
    for k in range(outer):
        c, s = twiddle_ref[k:k + 1, :LANES], twiddle_ref[k:k + 1, LANES:]
        here = pl.ds(k * lines, lines)
        ur, ui = spec_ref[here, :LANES], spec_ref[here, LANES:]
        re.append(ur * c - ui * s)
        im.append(ui * c + ur * s)
    out, _ = small_fft(re, im, 1)
    keys = []
    for n in range(outer):
        cols = slice(n * LANES, (n + 1) * LANES)
        filtered_ref[:, cols] = out[n]
        keys.append((cycle_ref[:, cols] * NPHI + column_ref[:, cols]).astype(jnp.float32))
    vals = list(out)
    sort_registers(keys, vals)
    row_len = outer * SUB
    last = functools.reduce(jnp.maximum, keys)
    first = functools.reduce(jnp.minimum, keys)
    last = jnp.max(last, axis=0, keepdims=True)
    first = jnp.min(first, axis=0, keepdims=True)
    for i in range(outer):
        key_ref[i * SUB:(i + 1) * SUB, :] = keys[i]
        val_ref[i * SUB:(i + 1) * SUB, :] = vals[i]
    key_rows[:LANES, :] = key_ref[...].T
    val_rows[:LANES, :] = val_ref[...].T
    reach = key_rows.shape[0] - LANES
    key_rows[LANES:, :] = jnp.full((reach, row_len), 2.0 * buckets * span, jnp.float32)
    val_rows[LANES:, :] = jnp.zeros((reach, row_len), jnp.float32)
    over = jnp.int32(0)
    for k, send_ref in enumerate(send_refs):
        for w in range(windows):
            bucket = (me_ref[0] ^ k) * windows + w
            low = (bucket * span).astype(jnp.float32)
            high = low + float(span)
            begin = jnp.sum((last < low).astype(jnp.float32)).astype(jnp.int32)
            end = jnp.sum((first < high).astype(jnp.float32)).astype(jnp.int32)
            over = over + (end - begin > rows).astype(jnp.int32)
            begin = jnp.minimum(begin, LANES)
            aligned = pl.multiple_of((begin // SUB) * SUB, SUB)
            back = lax.rem(reach - (begin - aligned), reach)
            here = pl.ds(aligned, reach)
            taken = pltpu.roll(key_rows[here, :], back, axis=0)[:rows]
            send_ref[w * rows:(w + 1) * rows, :] = taken - low
            at = (windows + w) * rows
            send_ref[at:at + rows, :] = pltpu.roll(val_rows[here, :], back, axis=0)[:rows]

    @pl.when(over > 0)
    def _():
        for send_ref in send_refs:
            send_ref[...] = jnp.full(send_ref.shape, jnp.nan, jnp.float32)


def filter_and_sort(me, scan, resp, cycle, column, det_count, band_cycles):
    lines, length = scan.shape
    tiles = length // LANES
    windows = WINDOWS
    buckets = det_count * windows
    span = band_cycles * NPHI // buckets
    row_len = tiles * SUB
    rows = LANES // buckets + 2
    reach = (rows + 2 * SUB - 2) // SUB * SUB
    twiddle, forward = filter_tables(length)
    resp_rows = resp.reshape(lines, LANES, tiles).transpose(2, 0, 1).reshape(tiles * lines, LANES)
    operands = [scan, resp_rows, cycle, column, jnp.asarray(twiddle), jnp.asarray(forward)]
    body = functools.partial(sort_kernel, buckets=buckets, span=span, rows=rows, windows=windows)
    vmem = pl.BlockSpec(memory_space=pltpu.VMEM)
    return pl.pallas_call(
        body,
        out_shape=(
            jax.ShapeDtypeStruct((lines, length), jnp.float32),
        ) + (jax.ShapeDtypeStruct((2 * windows * rows, row_len), jnp.float32),) * det_count,
        in_specs=[pl.BlockSpec(memory_space=pltpu.SMEM)]
        + [pl.BlockSpec(memory_space=pltpu.HBM)] * len(operands),
        out_specs=(vmem,) * (1 + det_count),
        scratch_shapes=[pltpu.VMEM(x.shape, x.dtype) for x in operands] + [
            pltpu.SemaphoreType.DMA((len(operands),)),
            pltpu.VMEM((row_len, LANES), jnp.float32),
            pltpu.VMEM((row_len, LANES), jnp.float32),
            pltpu.VMEM((tiles * lines, 2 * LANES), jnp.float32),
            pltpu.VMEM((LANES + reach, row_len), jnp.float32),
            pltpu.VMEM((LANES + reach, row_len), jnp.float32),
        ],
        compiler_params=pltpu.CompilerParams(vmem_limit_bytes=63 * 1024 * 1024),
        name="filter_sort",
    )(me, *operands)


def split2(x):
    high = x.astype(jnp.bfloat16)
    low = (x - high.astype(jnp.float32)).astype(jnp.bfloat16)
    return high, low


def bin_kernel(
    *refs, sources, windows, rows, window_cycles
):
    recv_refs, (pick_ref, table_hi, table_lo, map_ref, send_ref, flag_ref) = refs[:sources], refs[sources:-6]
    recv_ref, left_a, left_b, right_a, right_b, acc_ref = refs[-6:]
    for e in range(sources):
        recv_ref[e] = recv_refs[e][...]
    left_refs, right_refs = (left_a, left_b), (right_a, right_b)
    row_len = recv_ref.shape[2]
    parts = NPHI // ROW
    area = parts * window_cycles
    a_iota = lax.broadcasted_iota(jnp.int32, (area, row_len), 0).astype(jnp.float32).astype(jnp.bfloat16)
    b_iota = lax.broadcasted_iota(jnp.int32, (ROW, row_len), 0).astype(jnp.float32).astype(jnp.bfloat16)
    zero, one = jnp.zeros((), jnp.bfloat16), jnp.ones((), jnp.bfloat16)

    def build(e, w, slot):
        left, right = left_refs[slot], right_refs[slot]
        for r in range(rows):
            q = recv_ref[e, w * rows + r:w * rows + r + 1, :].astype(jnp.int32)
            v = recv_ref[e, (windows + w) * rows + r:(windows + w) * rows + r + 1, :]
            high, low = split2(v)
            cycle = q >> 11
            inside = (q >= 0) & (cycle < window_cycles)
            a = jnp.where(inside, ((q >> 8) & (parts - 1)) * window_cycles + cycle, -1)
            a = a.astype(jnp.float32).astype(jnp.bfloat16)
            b = (q & (ROW - 1)).astype(jnp.float32).astype(jnp.bfloat16)
            cols = slice(r * row_len, (r + 1) * row_len)
            hit = a_iota == a
            left[:area, cols] = jnp.where(hit, high, zero)
            left[area:2 * area, cols] = jnp.where(hit, low, zero)
            left[2 * area:, cols] = jnp.where(hit, one, zero)
            right[:, cols] = jnp.where(b_iota == b, one, zero)

    def multiply(slot):
        acc_ref[...] += lax.dot_general(
            left_refs[slot][...], right_refs[slot][...], NT, preferred_element_type=jnp.float32
        )

    build(0, 0, 0)
    for w in range(windows):
        acc_ref[...] = jnp.zeros(acc_ref.shape, jnp.float32)

        def body(i, carry):
            build(2 * i + 1, w, 1)
            multiply(0)
            build(jnp.minimum(2 * i + 2, sources - 1), w, 0)
            multiply(1)
            return carry

        lax.fori_loop(0, sources // 2 - 1, body, 0)
        build(sources - 1, w, 1)
        multiply(0)
        if w + 1 < windows:
            build(0, w + 1, 0)
        multiply(1)
        acc = acc_ref[...]
        sky = (acc[:area] + acc[area:2 * area]) / jnp.maximum(acc[2 * area:], 1.0)
        for c8 in range(parts):
            map_ref[w * window_cycles:(w + 1) * window_cycles, c8 * ROW:(c8 + 1) * ROW] = (
                sky[c8 * window_cycles:(c8 + 1) * window_cycles]
            )
    cycles = map_ref.shape[0]
    half = NPHI // 2
    modes = []
    for parity in (0, 1):
        a, b = map_ref[:, :half], map_ref[:, half:]
        high, low = split2(a + b if parity == 0 else a - b)
        first = jnp.dot(jnp.concatenate([high, low], axis=0), table_hi[parity], preferred_element_type=jnp.float32)
        second = jnp.dot(high, table_lo[parity], preferred_element_type=jnp.float32)
        modes.append(first[:cycles] + first[cycles:] + second)
    modes = jnp.concatenate(modes, axis=1)
    count = modes.shape[1]
    width = pick_ref.shape[1]
    high = modes.astype(jnp.bfloat16)
    rest = modes - high.astype(jnp.float32)
    middle = rest.astype(jnp.bfloat16)
    low = (rest - middle.astype(jnp.float32)).astype(jnp.bfloat16)
    pieces = jnp.concatenate([high, middle, low], axis=0)
    choose = (lax.broadcasted_iota(jnp.int32, (count, width), 0) == pick_ref[...])
    choose = jnp.where(choose, 1.0, 0.0).astype(jnp.bfloat16)
    moved = jnp.dot(pieces, choose, preferred_element_type=jnp.float32)
    moved = moved[:cycles] + moved[cycles:2 * cycles] + moved[2 * cycles:]
    owners, group_rows, lanes = send_ref.shape
    groups = cycles // group_rows
    lane_group = lax.broadcasted_iota(jnp.int32, (group_rows, lanes), 1) // (lanes // groups)
    values = recv_ref[:, windows * rows:, :]
    flag_ref[0] = (jnp.max(jnp.where(values == values, 0.0, 1.0)) > 0.0).astype(jnp.int32)
    for d in range(owners):
        block = moved[:, d * lanes:(d + 1) * lanes]
        out = block[:group_rows]
        for h in range(1, groups):
            out = jnp.where(lane_group == h, block[h * group_rows:(h + 1) * group_rows], out)
        send_ref[d] = out


def bin_and_modes(recv, order_slot, band_cycles):
    sources = len(recv)
    lines, row_len = recv[0].shape
    windows = WINDOWS
    rows = lines // (2 * windows)
    cycles = band_cycles // sources
    count = order_slot.shape[0]
    slots = count // sources
    groups = LANES // (2 * slots)
    high, low = mode_tables(count)
    m = order_slot.reshape(sources, 1, 1, slots)
    part = jnp.arange(2, dtype=jnp.int32).reshape(1, 1, 2, 1)
    pick = (m & 1) * count + part * (count // 2) + (m >> 1)
    pick = jnp.broadcast_to(pick, (sources, groups, 2, slots)).reshape(1, sources * LANES)
    area = cycles // windows * (NPHI // ROW)
    depth = rows * row_len
    vmem = pl.BlockSpec(memory_space=pltpu.VMEM)
    return pl.pallas_call(
        functools.partial(bin_kernel, sources=sources, windows=windows, rows=rows, window_cycles=cycles // windows),
        out_shape=(
            jax.ShapeDtypeStruct((cycles, NPHI), jnp.float32),
            jax.ShapeDtypeStruct((sources, cycles // groups, LANES), jnp.float32),
            jax.ShapeDtypeStruct((1,), jnp.int32),
        ),
        in_specs=[vmem] * (sources + 3),
        out_specs=(vmem, vmem, pl.BlockSpec(memory_space=pltpu.SMEM)),
        scratch_shapes=[
            pltpu.VMEM((sources, lines, row_len), jnp.float32),
            pltpu.VMEM((3 * area, depth), jnp.bfloat16),
            pltpu.VMEM((3 * area, depth), jnp.bfloat16),
            pltpu.VMEM((ROW, depth), jnp.bfloat16),
            pltpu.VMEM((ROW, depth), jnp.bfloat16),
            pltpu.VMEM((3 * area, ROW), jnp.float32),
        ],
        compiler_params=pltpu.CompilerParams(vmem_limit_bytes=40 * 1024 * 1024),
        name="bin_modes",
    )(*recv, pick, jnp.asarray(high), jnp.asarray(low))


def legendre_kernel(me_ref, recv_ref, table_ref, *refs, owners):
    out_refs, (leg_ref, arrived, modes_ref, wide_ref, sums_ref) = refs[:owners], refs[owners:]
    slots, band_cycles, degrees = table_ref.shape

    def load(slot):
        return pltpu.make_async_copy(table_ref.at[slot], leg_ref.at[slot], arrived.at[slot])

    def start(slot, carry):
        load(slot).start()
        return carry

    lax.fori_loop(0, slots, start, 0)
    sources, group_rows, lanes = recv_ref.shape
    groups = lanes // (2 * slots)
    width = out_refs[0].shape[1]
    tiles = degrees // LANES
    for e in range(sources):
        block = recv_ref[e]
        for h in range(groups):
            at = (e * groups + h) * group_rows
            turned = block if h == 0 else pltpu.roll(block, lanes - h * 2 * slots, axis=1)
            modes_ref[at:at + group_rows, :] = turned

    def widen(slot, half):
        turned = pltpu.roll(modes_ref[...], lax.rem(lanes - slot, lanes), axis=1)
        for c in range(2):
            column = turned[:, c * slots:c * slots + 1]
            wide_ref[half, c] = jnp.broadcast_to(column, (band_cycles, lanes))

    widen(0, 0)

    def body(slot, carry):
        half = slot & 1
        load(slot).wait()
        sums = [[jnp.zeros((SUB, LANES), jnp.float32) for _ in range(tiles)] for _ in range(2)]
        for r in range(0, band_cycles, SUB):
            factor = [wide_ref[half, c, r:r + SUB, :] for c in range(2)]
            for t in range(tiles):
                block = leg_ref[slot, r:r + SUB, t * LANES:(t + 1) * LANES]
                for c in range(2):
                    sums[c][t] = sums[c][t] + block * factor[c]
        widen(jnp.minimum(slot + 1, slots - 1), 1 - half)
        per_owner = width // LANES
        for c in range(2):
            lines = [jnp.sum(part, axis=0, keepdims=True) for part in sums[c]]
            for d in range(owners):
                line = jnp.concatenate(lines[d * per_owner:(d + 1) * per_owner], axis=1)
                sums_ref[d, pl.ds(c * slots + slot, 1), :] = line
        return carry

    lax.fori_loop(0, slots, body, 0)
    for k in range(owners):
        out_refs[k][...] = sums_ref[me_ref[0] ^ k]


def legendre_sums(me, recv, legendre, owners):
    slots, band_cycles, degrees = legendre.shape
    vmem = pl.BlockSpec(memory_space=pltpu.VMEM)
    return pl.pallas_call(
        functools.partial(legendre_kernel, owners=owners),
        out_shape=(jax.ShapeDtypeStruct((2 * slots, degrees // owners), jnp.float32),) * owners,
        in_specs=[pl.BlockSpec(memory_space=pltpu.SMEM), vmem, pl.BlockSpec(memory_space=pl.ANY)],
        out_specs=(vmem,) * owners,
        scratch_shapes=[
            pltpu.VMEM(legendre.shape, jnp.float32),
            pltpu.SemaphoreType.DMA((slots,)),
            pltpu.VMEM((band_cycles, LANES), jnp.float32),
            pltpu.VMEM((2, 2, band_cycles, LANES), jnp.float32),
            pltpu.VMEM((owners, 2 * slots, degrees // owners), jnp.float32),
        ],
        compiler_params=pltpu.CompilerParams(vmem_limit_bytes=44 * 1024 * 1024),
        name="legendre_sums",
    )(me, recv, legendre)


def exchange_and_sum(x, axis, count):
    parts = x.reshape(count, x.shape[0] // count, x.shape[1])
    return jnp.sum(lax.all_to_all(parts, axis, split_axis=0, concat_axis=0, tiled=True), axis=0)


def dense_path(filtered, cycle_offset, column, order_slot, band_cycles, det_count):
    flat_index = (cycle_offset * NPHI + column).reshape(-1)
    empty = jnp.zeros((band_cycles * NPHI,), jnp.float32)
    partial_value = empty.at[flat_index].add(filtered.reshape(-1)).reshape(band_cycles, NPHI)
    counts = empty.at[flat_index].add(1.0).reshape(band_cycles, NPHI)
    summed = exchange_and_sum(partial_value, "det", det_count)
    hit_total = exchange_and_sum(counts, "det", det_count)
    sky_map = summed / jnp.maximum(hit_total, 1.0)
    pixel_index = jnp.arange(NPHI, dtype=jnp.int32)[:, None]
    phases = 2.0 * jnp.pi / NPHI * (pixel_index * order_slot[None, :] % NPHI).astype(jnp.float32)
    modes = jnp.stack([
        jnp.dot(sky_map, jnp.cos(phases), precision=precise),
        -jnp.dot(sky_map, jnp.sin(phases), precision=precise),
    ])
    slots = order_slot.shape[0] // det_count
    groups = LANES // (2 * slots)
    blocks = modes.reshape(2, groups, -1, det_count, slots).transpose(3, 2, 1, 0, 4)
    blocks = blocks.reshape(det_count, -1, LANES)
    return sky_map, lax.all_to_all(blocks, "det", split_axis=0, concat_axis=0, tiled=True)


def swap_blocks(blocks, axis):
    count = len(blocks)
    return [blocks[0]] + [
        lax.ppermute(blocks[k], axis, [(i, i ^ k) for i in range(count)]) for k in range(1, count)
    ]


def local(scan_lines, response, cycle_offset, column, order_slot, legendre, *, det_count, band_count):
    slots, band_cycles, degrees = legendre.shape
    me = lax.axis_index("det").astype(jnp.int32).reshape(1)
    filtered, *send = filter_and_sort(
        me, scan_lines, response, cycle_offset, column, det_count, band_cycles
    )
    recv = swap_blocks(send, "det")
    sky_map, modes, crowded = bin_and_modes(recv, order_slot, band_cycles)
    modes = lax.all_to_all(modes, "det", split_axis=0, concat_axis=0, tiled=True)
    sky_map, modes = lax.cond(
        crowded[0] > 0,
        lambda: dense_path(filtered, cycle_offset, column, order_slot, band_cycles, det_count),
        lambda: (sky_map, modes),
    )
    band = lax.axis_index("band").astype(jnp.int32)
    terms = swap_blocks(legendre_sums(band.reshape(1), modes, legendre, band_count), "band")
    sums = functools.reduce(jnp.add, terms)
    local_orders = lax.dynamic_slice_in_dim(order_slot, lax.axis_index("det") * slots, slots, 0)
    width = degrees // band_count
    degree = band * width + jnp.arange(width, dtype=jnp.int32)
    keep = degree[None, None, :] >= local_orders[None, :, None]
    return jnp.where(keep, sums.reshape(2, slots, width), 0.0), sky_map


def solution(mesh):
    sizes = dict(mesh.shape)
    return jax.shard_map(
        functools.partial(local, det_count=sizes["det"], band_count=sizes["band"]),
        mesh=mesh,
        in_specs=(
            P(("det", "band"), None),
            P(("det", "band"), None),
            P(("det", "band"), None),
            P(("det", "band"), None),
            P(),
            P("det", "band", None),
        ),
        out_specs=(P(None, "det", "band"), P(("band", "det"), None)),
        check_vma=False,
    )
```

```python
import functools

import jax
import jax.numpy as jnp
import numpy as np
from jax import lax
from jax.experimental import pallas as pl
from jax.experimental.pallas import tpu as pltpu
from jax.sharding import PartitionSpec as P

NPHI = 2048
LANES = 128
SUB = 8
WINDOWS = 2
ROW = 256

precise = lax.Precision.HIGHEST
NT = (((1,), (1,)), ((), ()))


def filter_tables(length):
    outer = length // LANES
    k1 = np.arange(outer)[:, None]
    n2 = np.arange(LANES)[None, :]
    turn = 2.0 * np.pi * ((k1 * n2) % length) / length
    twiddle = np.concatenate([np.cos(turn), np.sin(turn)], axis=1)
    a = np.arange(LANES)
    angle = 2.0 * np.pi * (np.outer(a, a) % LANES) / LANES
    c, s = np.cos(angle), np.sin(angle)
    forward = np.block([[c, -s], [s, c]])
    return twiddle.astype(np.float32), forward.astype(np.float32)


def mode_tables(count):
    half = NPHI // 2
    p = np.arange(half)[:, None]
    out = []
    for parity in (0, 1):
        m = 2 * np.arange(count // 2)[None, :] + parity
        angle = 2.0 * np.pi * ((p * m) % NPHI) / NPHI
        out.append(np.concatenate([np.cos(angle), -np.sin(angle)], axis=1))
    table = np.stack(out).astype(np.float32)
    high = table.astype(jnp.bfloat16)
    low = (table - high.astype(np.float32)).astype(jnp.bfloat16)
    return high, low


def small_fft(re, im, sign):
    count = len(re)
    if count == 1:
        return re, im
    even_re, even_im = small_fft(re[0::2], None if im is None else im[0::2], sign)
    odd_re, odd_im = small_fft(re[1::2], None if im is None else im[1::2], sign)
    half = count // 2
    out_re, out_im = [None] * count, [None] * count
    for k in range(half):
        wr = float(np.cos(2 * np.pi * k / count))
        wi = float(sign * np.sin(2 * np.pi * k / count))
        er, ei, orr, oi = even_re[k], even_im and even_im[k], odd_re[k], odd_im and odd_im[k]
        if k == 0:
            tr, ti = orr, oi
        elif 4 * k == count:
            tr = None if oi is None else -wi * oi
            ti = wi * orr
        elif oi is None:
            tr, ti = wr * orr, wi * orr
        else:
            tr, ti = wr * orr - wi * oi, wr * oi + wi * orr
        out_re[k] = er if tr is None else er + tr
        out_re[k + half] = er if tr is None else er - tr
        if ti is None:
            out_im[k] = out_im[k + half] = ei
        else:
            out_im[k] = ti if ei is None else ei + ti
            out_im[k + half] = -ti if ei is None else ei - ti
    if all(x is None for x in out_im):
        return out_re, None
    out_im = [jnp.zeros_like(out_re[0]) if x is None else x for x in out_im]
    return out_re, out_im


class Places:
    def __init__(self, tile_bits, total_bits):
        self.tile_bits, self.total_bits = tile_bits, total_bits
        self.of = list(range(total_bits))
        for level in range(tile_bits + 1, total_bits + 1):
            self.walk(level)
        held = [self.of.index(place) for place in range(total_bits)]
        self.of = held

    def swap(self, bit):
        other = self.of.index(0)
        self.of[bit], self.of[other] = 0, self.of[bit]

    def walk(self, level):
        for bit in range(level - 1, self.tile_bits - 1, -1):
            self.swap(bit)
        self.swap(0)

    def axis_distance(self, bit):
        place = self.of[bit] - self.tile_bits
        return (0, 1 << place) if place < 3 else (1, 1 << (place - 3))

    def mask(self, bit):
        axis, distance = self.axis_distance(bit)
        return (lax.broadcasted_iota(jnp.int32, (SUB, LANES), axis) & distance) != 0


def trade(low, high, upper, axis, distance):
    axis += low.ndim - 2
    size = low.shape[axis]
    return (
        jnp.where(upper, pltpu.roll(high, distance, axis=axis), low),
        jnp.where(upper, high, pltpu.roll(low, size - distance, axis=axis)),
    )


def exchange(keys, vals, a, b, down):
    if down:
        a, b = b, a
    swap = keys[a] > keys[b]
    keys[a], keys[b] = jnp.minimum(keys[a], keys[b]), jnp.maximum(keys[a], keys[b])
    vals[a], vals[b] = jnp.where(swap, vals[b], vals[a]), jnp.where(swap, vals[a], vals[b])


def sort_registers(keys, vals):
    tiles = len(keys)
    tile_bits = tiles.bit_length() - 1
    places = Places(tile_bits, tile_bits + 10)

    def flip(bit):
        return jnp.where(places.mask(bit), -1.0, 1.0)

    def trade_all(bit):
        upper, (axis, distance) = places.mask(bit), places.axis_distance(bit)
        places.swap(bit)
        for i in range(0, tiles, 2):
            keys[i], keys[i + 1] = trade(keys[i], keys[i + 1], upper, axis, distance)
            vals[i], vals[i + 1] = trade(vals[i], vals[i + 1], upper, axis, distance)

    for level in range(1, places.total_bits + 1):
        if level >= tile_bits:
            sign = 1.0
            if level > tile_bits:
                sign = flip(level - 1)
            if level < places.total_bits:
                sign = sign * flip(level)
            for i in range(tiles):
                keys[i] = keys[i] * sign
        for bit in range(level - 1, -1, -1):
            if bit >= tile_bits or (bit == 0 and level > tile_bits):
                trade_all(bit)
            step = 1 << bit if bit < tile_bits else 1
            for i in range(tiles):
                if not i & step:
                    exchange(keys, vals, i, i + step, level < tile_bits and (i >> level) & 1 == 1)
    assert places.of == list(range(places.total_bits))


def sort_kernel(
    me_ref, scan_hbm, resp_hbm, cycle_hbm, column_hbm, twiddle_hbm, forward_hbm, filtered_ref, *refs,
    buckets, span, rows, windows,
):
    chips = buckets // windows // 2
    own_refs, pair_ref, refs = refs[:chips], refs[chips], refs[chips + 1:]
    scan_ref, resp_ref, cycle_ref, column_ref, twiddle_ref, forward_ref, arrived = refs[:7]
    key_ref, val_ref, spec_ref, key_rows, val_rows = refs[7:]
    lines, length = scan_ref.shape
    outer = length // LANES
    loads = [
        pltpu.make_async_copy(source, place, arrived.at[i])
        for i, (source, place) in enumerate([
            (scan_hbm, scan_ref), (twiddle_hbm, twiddle_ref), (forward_hbm, forward_ref),
            (resp_hbm, resp_ref), (cycle_hbm, cycle_ref), (column_hbm, column_ref),
        ])
    ]
    for load in loads:
        load.start()
    loads[0].wait()
    re, im = small_fft([scan_ref[:, n * LANES:(n + 1) * LANES] for n in range(outer)], None, -1)
    loads[1].wait()
    for k in range(outer):
        c, s = twiddle_ref[k:k + 1, :LANES], twiddle_ref[k:k + 1, LANES:]
        here = pl.ds(k * lines, lines)
        spec_ref[here, :LANES] = re[k] * c + im[k] * s
        spec_ref[here, LANES:] = im[k] * c - re[k] * s
    for load in loads[2:]:
        load.wait()
    spec = jnp.dot(spec_ref[...], forward_ref[...], precision=precise, preferred_element_type=jnp.float32)
    resp = resp_ref[...] * (1.0 / length)
    spec = spec * jnp.concatenate([resp, resp], axis=1)
    spec_ref[...] = lax.dot_general(
        spec, forward_ref[...], NT, precision=precise, preferred_element_type=jnp.float32
    )
    re, im = [], []
    for k in range(outer):
        c, s = twiddle_ref[k:k + 1, :LANES], twiddle_ref[k:k + 1, LANES:]
        here = pl.ds(k * lines, lines)
        ur, ui = spec_ref[here, :LANES], spec_ref[here, LANES:]
        re.append(ur * c - ui * s)
        im.append(ui * c + ur * s)
    out, _ = small_fft(re, im, 1)
    keys = []
    for n in range(outer):
        cols = slice(n * LANES, (n + 1) * LANES)
        filtered_ref[:, cols] = out[n]
        keys.append((cycle_ref[:, cols] * NPHI + column_ref[:, cols]).astype(jnp.float32))
    vals = list(out)
    sort_registers(keys, vals)
    row_len = outer * SUB
    last = functools.reduce(jnp.maximum, keys)
    first = functools.reduce(jnp.minimum, keys)
    last = jnp.max(last, axis=0, keepdims=True)
    first = jnp.min(first, axis=0, keepdims=True)
    for i in range(outer):
        key_ref[i * SUB:(i + 1) * SUB, :] = keys[i]
        val_ref[i * SUB:(i + 1) * SUB, :] = vals[i]
    key_rows[:LANES, :] = key_ref[...].T
    val_rows[:LANES, :] = val_ref[...].T
    reach = key_rows.shape[0] - LANES
    key_rows[LANES:, :] = jnp.full((reach, row_len), 2.0 * buckets * span, jnp.float32)
    val_rows[LANES:, :] = jnp.zeros((reach, row_len), jnp.float32)
    over = jnp.int32(0)
    depth = 2 * windows * rows
    for j in range(len(own_refs) * 2):
        send_ref, base = (pair_ref, j // 2 * depth) if j & 1 else (own_refs[j // 2], 0)
        for w in range(windows):
            bucket = (me_ref[0] ^ j) * windows + w
            low = (bucket * span).astype(jnp.float32)
            high = low + float(span)
            begin = jnp.sum((last < low).astype(jnp.float32)).astype(jnp.int32)
            end = jnp.sum((first < high).astype(jnp.float32)).astype(jnp.int32)
            over = over + (end - begin > rows).astype(jnp.int32)
            begin = jnp.minimum(begin, LANES)
            aligned = pl.multiple_of((begin // SUB) * SUB, SUB)
            back = lax.rem(reach - (begin - aligned), reach)
            here = pl.ds(aligned, reach)
            at = base + w * rows
            send_ref[at:at + rows, :] = pltpu.roll(key_rows[here, :], back, axis=0)[:rows] - low
            at = base + (windows + w) * rows
            send_ref[at:at + rows, :] = pltpu.roll(val_rows[here, :], back, axis=0)[:rows]

    @pl.when(over > 0)
    def _():
        for send_ref in own_refs + (pair_ref,):
            send_ref[...] = jnp.full(send_ref.shape, jnp.nan, jnp.float32)


def filter_and_sort(me, scan, resp, cycle, column, det_count, band_cycles):
    lines, length = scan.shape
    tiles = length // LANES
    windows = WINDOWS
    buckets = det_count * windows
    span = band_cycles * NPHI // buckets
    row_len = tiles * SUB
    rows = LANES // buckets + 2
    reach = (rows + 2 * SUB - 2) // SUB * SUB
    chips = det_count // 2
    depth = 2 * windows * rows
    twiddle, forward = filter_tables(length)
    resp_rows = resp.reshape(lines, LANES, tiles).transpose(2, 0, 1).reshape(tiles * lines, LANES)
    operands = [scan, resp_rows, cycle, column, jnp.asarray(twiddle), jnp.asarray(forward)]
    body = functools.partial(sort_kernel, buckets=buckets, span=span, rows=rows, windows=windows)
    vmem = pl.BlockSpec(memory_space=pltpu.VMEM)
    return pl.pallas_call(
        body,
        out_shape=(
            jax.ShapeDtypeStruct((lines, length), jnp.float32),
        ) + (jax.ShapeDtypeStruct((depth, row_len), jnp.float32),) * chips
        + (jax.ShapeDtypeStruct((chips * depth, row_len), jnp.float32),),
        in_specs=[pl.BlockSpec(memory_space=pltpu.SMEM)]
        + [pl.BlockSpec(memory_space=pl.ANY)] * len(operands),
        out_specs=(vmem,) * (chips + 2),
        scratch_shapes=[pltpu.VMEM(x.shape, x.dtype) for x in operands] + [
            pltpu.SemaphoreType.DMA((len(operands),)),
            pltpu.VMEM((row_len, LANES), jnp.float32),
            pltpu.VMEM((row_len, LANES), jnp.float32),
            pltpu.VMEM((tiles * lines, 2 * LANES), jnp.float32),
            pltpu.VMEM((LANES + reach, row_len), jnp.float32),
            pltpu.VMEM((LANES + reach, row_len), jnp.float32),
        ],
        compiler_params=pltpu.CompilerParams(vmem_limit_bytes=63 * 1024 * 1024),
        name="filter_sort",
    )(me, *operands)


def split2(x):
    high = x.astype(jnp.bfloat16)
    low = (x - high.astype(jnp.float32)).astype(jnp.bfloat16)
    return high, low


def bin_kernel(me_ref, *refs, sources, windows, rows, window_cycles):
    chips = sources // 2
    recv_hbm, (pick_hbm, hi_hbm, lo_hbm) = refs[:chips + 1], refs[chips + 1:chips + 4]
    map_ref, own_refs, pair_ref = refs[chips + 4], refs[chips + 5:2 * chips + 5], refs[2 * chips + 5]
    flag_ref, recv_ref, left_a, left_b, right_a, right_b, acc_ref = refs[2 * chips + 6:2 * chips + 13]
    pick_ref, table_hi, table_lo, blocks_ref, arrived = refs[2 * chips + 13:]
    left_refs, right_refs = (left_a, left_b), (right_a, right_b)
    deep = 2 * windows * rows
    parts = [(recv_hbm[0], recv_ref.at[0]), (recv_hbm[1].at[pl.ds(0, deep)], recv_ref.at[1])]
    for k in range(1, chips):
        for half in range(2):
            parts.append((recv_hbm[k + 1].at[pl.ds(half * deep, deep)], recv_ref.at[2 * k + half]))
    parts += [(pick_hbm, pick_ref), (hi_hbm, table_hi), (lo_hbm, table_lo)]
    loads = [pltpu.make_async_copy(a, b, arrived.at[i]) for i, (a, b) in enumerate(parts)]
    for load in loads:
        load.start()
    for load in loads[:sources]:
        load.wait()
    row_len = recv_ref.shape[2]
    parts = NPHI // ROW
    area = parts * window_cycles
    a_iota = lax.broadcasted_iota(jnp.int32, (area, row_len), 0).astype(jnp.float32).astype(jnp.bfloat16)
    b_iota = lax.broadcasted_iota(jnp.int32, (ROW, row_len), 0).astype(jnp.float32).astype(jnp.bfloat16)
    zero, one = jnp.zeros((), jnp.bfloat16), jnp.ones((), jnp.bfloat16)

    def build(e, w, slot):
        left, right = left_refs[slot], right_refs[slot]
        for r in range(rows):
            q = recv_ref[e, w * rows + r:w * rows + r + 1, :].astype(jnp.int32)
            v = recv_ref[e, (windows + w) * rows + r:(windows + w) * rows + r + 1, :]
            high, low = split2(v)
            cycle = q >> 11
            inside = (q >= 0) & (cycle < window_cycles)
            a = jnp.where(inside, ((q >> 8) & (parts - 1)) * window_cycles + cycle, -1)
            a = a.astype(jnp.float32).astype(jnp.bfloat16)
            b = (q & (ROW - 1)).astype(jnp.float32).astype(jnp.bfloat16)
            cols = slice(r * row_len, (r + 1) * row_len)
            hit = a_iota == a
            left[:area, cols] = jnp.where(hit, high, zero)
            left[area:2 * area, cols] = jnp.where(hit, low, zero)
            left[2 * area:, cols] = jnp.where(hit, one, zero)
            right[:, cols] = jnp.where(b_iota == b, one, zero)

    def multiply(slot):
        acc_ref[...] += lax.dot_general(
            left_refs[slot][...], right_refs[slot][...], NT, preferred_element_type=jnp.float32
        )

    build(0, 0, 0)
    for w in range(windows):
        acc_ref[...] = jnp.zeros(acc_ref.shape, jnp.float32)

        def body(i, carry):
            build(2 * i + 1, w, 1)
            multiply(0)
            build(jnp.minimum(2 * i + 2, sources - 1), w, 0)
            multiply(1)
            return carry

        lax.fori_loop(0, sources // 2 - 1, body, 0)
        build(sources - 1, w, 1)
        multiply(0)
        if w + 1 < windows:
            build(0, w + 1, 0)
        multiply(1)
        acc = acc_ref[...]
        sky = (acc[:area] + acc[area:2 * area]) / jnp.maximum(acc[2 * area:], 1.0)
        for c8 in range(parts):
            map_ref[w * window_cycles:(w + 1) * window_cycles, c8 * ROW:(c8 + 1) * ROW] = (
                sky[c8 * window_cycles:(c8 + 1) * window_cycles]
            )
    for load in loads[sources:]:
        load.wait()
    cycles = map_ref.shape[0]
    half = NPHI // 2
    modes = []
    for parity in (0, 1):
        a, b = map_ref[:, :half], map_ref[:, half:]
        high, low = split2(a + b if parity == 0 else a - b)
        first = jnp.dot(jnp.concatenate([high, low], axis=0), table_hi[parity], preferred_element_type=jnp.float32)
        second = jnp.dot(high, table_lo[parity], preferred_element_type=jnp.float32)
        modes.append(first[:cycles] + first[cycles:] + second)
    modes = jnp.concatenate(modes, axis=1)
    count = modes.shape[1]
    width = pick_ref.shape[1]
    high = modes.astype(jnp.bfloat16)
    rest = modes - high.astype(jnp.float32)
    middle = rest.astype(jnp.bfloat16)
    low = (rest - middle.astype(jnp.float32)).astype(jnp.bfloat16)
    pieces = jnp.concatenate([high, middle, low], axis=0)
    choose = (lax.broadcasted_iota(jnp.int32, (count, width), 0) == pick_ref[...])
    choose = jnp.where(choose, 1.0, 0.0).astype(jnp.bfloat16)
    moved = jnp.dot(pieces, choose, preferred_element_type=jnp.float32)
    moved = moved[:cycles] + moved[cycles:2 * cycles] + moved[2 * cycles:]
    group_rows, lanes = own_refs[0].shape
    groups = cycles // group_rows
    lane_group = lax.broadcasted_iota(jnp.int32, (group_rows, lanes), 1) // (lanes // groups)
    values = recv_ref[:, windows * rows:, :]
    flag_ref[0] = (jnp.max(jnp.where(values == values, 0.0, 1.0)) > 0.0).astype(jnp.int32)
    for d in range(sources):
        block = moved[:, d * lanes:(d + 1) * lanes]
        out = block[:group_rows]
        for h in range(1, groups):
            out = jnp.where(lane_group == h, block[h * group_rows:(h + 1) * group_rows], out)
        blocks_ref[d] = out
    for k in range(chips):
        own_refs[k][...] = blocks_ref[me_ref[0] ^ (2 * k)]
        pair_ref[k * group_rows:(k + 1) * group_rows, :] = blocks_ref[me_ref[0] ^ (2 * k + 1)]


def bin_and_modes(me, recv, order_slot, band_cycles):
    chips = len(recv) - 1
    sources = 2 * chips
    lines, row_len = recv[0].shape
    windows = WINDOWS
    rows = lines // (2 * windows)
    cycles = band_cycles // sources
    count = order_slot.shape[0]
    slots = count // sources
    groups = LANES // (2 * slots)
    high, low = mode_tables(count)
    m = order_slot.reshape(sources, 1, 1, slots)
    part = jnp.arange(2, dtype=jnp.int32).reshape(1, 1, 2, 1)
    pick = (m & 1) * count + part * (count // 2) + (m >> 1)
    pick = jnp.broadcast_to(pick, (sources, groups, 2, slots)).reshape(1, sources * LANES)
    area = cycles // windows * (NPHI // ROW)
    depth = rows * row_len
    block = (cycles // groups, LANES)
    vmem = pl.BlockSpec(memory_space=pltpu.VMEM)
    return pl.pallas_call(
        functools.partial(
            bin_kernel, sources=sources, windows=windows, rows=rows, window_cycles=cycles // windows
        ),
        out_shape=(jax.ShapeDtypeStruct((cycles, NPHI), jnp.float32),)
        + (jax.ShapeDtypeStruct(block, jnp.float32),) * chips
        + (
            jax.ShapeDtypeStruct((chips * block[0], LANES), jnp.float32),
            jax.ShapeDtypeStruct((1,), jnp.int32),
        ),
        in_specs=[pl.BlockSpec(memory_space=pltpu.SMEM)] + [pl.BlockSpec(memory_space=pl.ANY)] * (chips + 4),
        out_specs=(vmem,) * (chips + 2) + (pl.BlockSpec(memory_space=pltpu.SMEM),),
        scratch_shapes=[
            pltpu.VMEM((sources, lines, row_len), jnp.float32),
            pltpu.VMEM((3 * area, depth), jnp.bfloat16),
            pltpu.VMEM((3 * area, depth), jnp.bfloat16),
            pltpu.VMEM((ROW, depth), jnp.bfloat16),
            pltpu.VMEM((ROW, depth), jnp.bfloat16),
            pltpu.VMEM((3 * area, ROW), jnp.float32),
            pltpu.VMEM(pick.shape, jnp.int32),
            pltpu.VMEM(high.shape, jnp.bfloat16),
            pltpu.VMEM(low.shape, jnp.bfloat16),
            pltpu.VMEM((sources,) + block, jnp.float32),
            pltpu.SemaphoreType.DMA((sources + 3,)),
        ],
        compiler_params=pltpu.CompilerParams(vmem_limit_bytes=63 * 1024 * 1024),
        name="bin_modes",
    )(me, *recv, pick, jnp.asarray(high), jnp.asarray(low))


def legendre_kernel(me_ref, *refs, chips, owners):
    recv_refs, table_ref, refs = refs[:chips + 1], refs[chips + 1], refs[chips + 2:]
    out_refs, (leg_ref, arrived, modes_ref, wide_ref, sums_ref) = refs[:owners], refs[owners:]
    slots, band_cycles, degrees = table_ref.shape

    def load(slot):
        return pltpu.make_async_copy(table_ref.at[slot], leg_ref.at[slot], arrived.at[slot])

    def start(slot, carry):
        load(slot).start()
        return carry

    lax.fori_loop(0, slots, start, 0)
    group_rows, lanes = recv_refs[0].shape
    groups = lanes // (2 * slots)
    width = out_refs[0].shape[1]
    tiles = degrees // LANES
    cycles = group_rows * groups
    for j in range(2 * chips):
        if j < 2:
            block = recv_refs[j][:group_rows, :]
        else:
            block = recv_refs[j // 2 + 1][j % 2 * group_rows:(j % 2 + 1) * group_rows, :]
        turned = [block] + [pltpu.roll(block, lanes - h * 2 * slots, axis=1) for h in range(1, groups)]
        at = pl.multiple_of((me_ref[0] ^ j) * cycles, cycles)
        modes_ref[pl.ds(at, cycles), :] = jnp.concatenate(turned, axis=0)

    def widen(slot, half):
        turned = pltpu.roll(modes_ref[...], lax.rem(lanes - slot, lanes), axis=1)
        for c in range(2):
            column = turned[:, c * slots:c * slots + 1]
            wide_ref[half, c] = jnp.broadcast_to(column, (band_cycles, lanes))

    widen(0, 0)

    def body(slot, carry):
        half = slot & 1
        load(slot).wait()
        sums = [[jnp.zeros((SUB, LANES), jnp.float32) for _ in range(tiles)] for _ in range(2)]
        for r in range(0, band_cycles, SUB):
            factor = [wide_ref[half, c, r:r + SUB, :] for c in range(2)]
            for t in range(tiles):
                block = leg_ref[slot, r:r + SUB, t * LANES:(t + 1) * LANES]
                for c in range(2):
                    sums[c][t] = sums[c][t] + block * factor[c]
        widen(jnp.minimum(slot + 1, slots - 1), 1 - half)
        per_owner = width // LANES
        for c in range(2):
            lines = [jnp.sum(part, axis=0, keepdims=True) for part in sums[c]]
            for d in range(owners):
                line = jnp.concatenate(lines[d * per_owner:(d + 1) * per_owner], axis=1)
                sums_ref[d, pl.ds(c * slots + slot, 1), :] = line
        return carry

    lax.fori_loop(0, slots, body, 0)
    for k in range(owners):
        out_refs[k][...] = sums_ref[me_ref[1] ^ k]


def legendre_sums(me, recv, legendre, owners):
    slots, band_cycles, degrees = legendre.shape
    vmem = pl.BlockSpec(memory_space=pltpu.VMEM)
    return pl.pallas_call(
        functools.partial(legendre_kernel, chips=len(recv) - 1, owners=owners),
        out_shape=(jax.ShapeDtypeStruct((2 * slots, degrees // owners), jnp.float32),) * owners,
        in_specs=[pl.BlockSpec(memory_space=pltpu.SMEM)] + [vmem] * len(recv) + [pl.BlockSpec(memory_space=pl.ANY)],
        out_specs=(vmem,) * owners,
        scratch_shapes=[
            pltpu.VMEM(legendre.shape, jnp.float32),
            pltpu.SemaphoreType.DMA((slots,)),
            pltpu.VMEM((band_cycles, LANES), jnp.float32),
            pltpu.VMEM((2, 2, band_cycles, LANES), jnp.float32),
            pltpu.VMEM((owners, 2 * slots, degrees // owners), jnp.float32),
        ],
        compiler_params=pltpu.CompilerParams(vmem_limit_bytes=44 * 1024 * 1024),
        name="legendre_sums",
    )(me, *recv, legendre)


def exchange_and_sum(x, axis, count):
    parts = x.reshape(count, x.shape[0] // count, x.shape[1])
    return jnp.sum(lax.all_to_all(parts, axis, split_axis=0, concat_axis=0, tiled=True), axis=0)


def dense_path(filtered, cycle_offset, column, order_slot, band_cycles, det_count):
    flat_index = (cycle_offset * NPHI + column).reshape(-1)
    empty = jnp.zeros((band_cycles * NPHI,), jnp.float32)
    partial_value = empty.at[flat_index].add(filtered.reshape(-1)).reshape(band_cycles, NPHI)
    counts = empty.at[flat_index].add(1.0).reshape(band_cycles, NPHI)
    summed = exchange_and_sum(partial_value, "det", det_count)
    hit_total = exchange_and_sum(counts, "det", det_count)
    sky_map = summed / jnp.maximum(hit_total, 1.0)
    pixel_index = jnp.arange(NPHI, dtype=jnp.int32)[:, None]
    phases = 2.0 * jnp.pi / NPHI * (pixel_index * order_slot[None, :] % NPHI).astype(jnp.float32)
    modes = jnp.stack([
        jnp.dot(sky_map, jnp.cos(phases), precision=precise),
        -jnp.dot(sky_map, jnp.sin(phases), precision=precise),
    ])
    slots = order_slot.shape[0] // det_count
    groups = LANES // (2 * slots)
    blocks = modes.reshape(2, groups, -1, det_count, slots).transpose(3, 2, 1, 0, 4)
    blocks = blocks.reshape(det_count, -1, LANES)
    me = lax.axis_index("det")
    mine = [lax.dynamic_index_in_dim(blocks, me ^ j, 0, keepdims=False) for j in range(det_count)]
    return (sky_map, *two_level_swap(mine[0::2], jnp.concatenate(mine[1::2]), "det"))


def two_level_swap(own, pair, axis):
    chips, rows = len(own), own[0].shape[0]
    pair = lax.ppermute(pair, axis, [(i, i ^ 1) for i in range(2 * chips)])
    both = {}
    for k in range(chips - 1, 0, -1):
        both[k] = lax.ppermute(
            jnp.concatenate([own[k], pair[k * rows:(k + 1) * rows]]),
            axis,
            [(i, i ^ (2 * k)) for i in range(2 * chips)],
        )
    return [own[0], pair] + [both[k] for k in range(1, chips)]


def swap_blocks(blocks, axis):
    count = len(blocks)
    return [blocks[0]] + [
        lax.ppermute(blocks[k], axis, [(i, i ^ k) for i in range(count)]) for k in range(1, count)
    ]


def local(scan_lines, response, cycle_offset, column, order_slot, legendre, *, det_count, band_count):
    slots, band_cycles, degrees = legendre.shape
    band = lax.axis_index("band").astype(jnp.int32)
    me = jnp.stack([lax.axis_index("det").astype(jnp.int32), band])
    filtered, *own, pair = filter_and_sort(
        me, scan_lines, response, cycle_offset, column, det_count, band_cycles
    )
    recv = two_level_swap(own, pair, "det")
    sky_map, *own, pair, crowded = bin_and_modes(me, recv, order_slot, band_cycles)
    modes = two_level_swap(own, pair, "det")
    sky_map, *modes = lax.cond(
        crowded[0] > 0,
        lambda: dense_path(filtered, cycle_offset, column, order_slot, band_cycles, det_count),
        lambda: (sky_map, *modes),
    )
    terms = swap_blocks(legendre_sums(me, modes, legendre, band_count), "band")
    sums = functools.reduce(jnp.add, terms)
    local_orders = lax.dynamic_slice_in_dim(order_slot, lax.axis_index("det") * slots, slots, 0)
    width = degrees // band_count
    degree = band * width + jnp.arange(width, dtype=jnp.int32)
    keep = degree[None, None, :] >= local_orders[None, :, None]
    return jnp.where(keep, sums.reshape(2, slots, width), 0.0), sky_map


def solution(mesh):
    sizes = dict(mesh.shape)
    return jax.shard_map(
        functools.partial(local, det_count=sizes["det"], band_count=sizes["band"]),
        mesh=mesh,
        in_specs=(
            P(("det", "band"), None),
            P(("det", "band"), None),
            P(("det", "band"), None),
            P(("det", "band"), None),
            P(),
            P("det", "band", None),
        ),
        out_specs=(P(None, "det", "band"), P(("band", "det"), None)),
        check_vma=False,
    )
```

```python
import functools

import jax
import jax.numpy as jnp
import numpy as np
from jax import lax
from jax.experimental import pallas as pl
from jax.experimental.pallas import tpu as pltpu
from jax.sharding import PartitionSpec as P

NPHI = 2048
LANES = 128
SUB = 8
WINDOWS = 2
ROW = 256

precise = lax.Precision.HIGHEST
NT = (((1,), (1,)), ((), ()))


def filter_tables(length):
    outer = length // LANES
    k1 = np.arange(outer)[:, None]
    n2 = np.arange(LANES)[None, :]
    turn = 2.0 * np.pi * ((k1 * n2) % length) / length
    twiddle = np.concatenate([np.cos(turn), np.sin(turn)], axis=1)
    a = np.arange(LANES)
    angle = 2.0 * np.pi * (np.outer(a, a) % LANES) / LANES
    c, s = np.cos(angle), np.sin(angle)
    order = (a % outer) * (LANES // outer) + a // outer
    c, s = c[:, order], s[:, order]
    forward = np.block([[c, -s], [s, c]])
    return twiddle.astype(np.float32), forward.astype(np.float32)


def mode_tables(count):
    half = NPHI // 2
    p = np.arange(half)[:, None]
    out = []
    for parity in (0, 1):
        m = 2 * np.arange(count // 2)[None, :] + parity
        angle = 2.0 * np.pi * ((p * m) % NPHI) / NPHI
        out.append(np.concatenate([np.cos(angle), -np.sin(angle)], axis=1))
    table = np.stack(out).astype(np.float32)
    high = table.astype(jnp.bfloat16)
    low = (table - high.astype(np.float32)).astype(jnp.bfloat16)
    return np.stack([high, low])


def small_fft(re, im, sign):
    count = len(re)
    if count == 1:
        return re, im
    even_re, even_im = small_fft(re[0::2], None if im is None else im[0::2], sign)
    odd_re, odd_im = small_fft(re[1::2], None if im is None else im[1::2], sign)
    half = count // 2
    out_re, out_im = [None] * count, [None] * count
    for k in range(half):
        wr = float(np.cos(2 * np.pi * k / count))
        wi = float(sign * np.sin(2 * np.pi * k / count))
        er, ei, orr, oi = even_re[k], even_im and even_im[k], odd_re[k], odd_im and odd_im[k]
        if k == 0:
            tr, ti = orr, oi
        elif 4 * k == count:
            tr = None if oi is None else -wi * oi
            ti = wi * orr
        elif oi is None:
            tr, ti = wr * orr, wi * orr
        else:
            tr, ti = wr * orr - wi * oi, wr * oi + wi * orr
        out_re[k] = er if tr is None else er + tr
        out_re[k + half] = er if tr is None else er - tr
        if ti is None:
            out_im[k] = out_im[k + half] = ei
        else:
            out_im[k] = ti if ei is None else ei + ti
            out_im[k + half] = -ti if ei is None else ei - ti
    if all(x is None for x in out_im):
        return out_re, None
    out_im = [jnp.zeros_like(out_re[0]) if x is None else x for x in out_im]
    return out_re, out_im


class Places:
    def __init__(self, tile_bits, total_bits):
        self.tile_bits, self.total_bits = tile_bits, total_bits
        self.of = list(range(total_bits))
        for level in range(tile_bits + 1, total_bits + 1):
            self.walk(level)
        held = [self.of.index(place) for place in range(total_bits)]
        self.of = held

    def swap(self, bit):
        other = self.of.index(0)
        self.of[bit], self.of[other] = 0, self.of[bit]

    def walk(self, level):
        for bit in range(level - 1, self.tile_bits - 1, -1):
            self.swap(bit)
        self.swap(0)

    def axis_distance(self, bit):
        place = self.of[bit] - self.tile_bits
        return (0, 1 << place) if place < 3 else (1, 1 << (place - 3))

    def mask(self, bit):
        axis, distance = self.axis_distance(bit)
        return (lax.broadcasted_iota(jnp.int32, (SUB, LANES), axis) & distance) != 0


def trade(low, high, upper, axis, distance):
    axis += low.ndim - 2
    size = low.shape[axis]
    return (
        jnp.where(upper, pltpu.roll(high, distance, axis=axis), low),
        jnp.where(upper, high, pltpu.roll(low, size - distance, axis=axis)),
    )


def exchange(keys, vals, a, b, down):
    if down:
        a, b = b, a
    swap = keys[a] > keys[b]
    keys[a], keys[b] = jnp.minimum(keys[a], keys[b]), jnp.maximum(keys[a], keys[b])
    vals[a], vals[b] = jnp.where(swap, vals[b], vals[a]), jnp.where(swap, vals[a], vals[b])


def sort_registers(keys, vals):
    tiles = len(keys)
    tile_bits = tiles.bit_length() - 1
    places = Places(tile_bits, tile_bits + 10)

    def flip(bit):
        return jnp.where(places.mask(bit), -1.0, 1.0)

    def trade_all(bit):
        upper, (axis, distance) = places.mask(bit), places.axis_distance(bit)
        places.swap(bit)
        for i in range(0, tiles, 2):
            keys[i], keys[i + 1] = trade(keys[i], keys[i + 1], upper, axis, distance)
            vals[i], vals[i + 1] = trade(vals[i], vals[i + 1], upper, axis, distance)

    for level in range(1, places.total_bits + 1):
        if level >= tile_bits:
            sign = 1.0
            if level > tile_bits:
                sign = flip(level - 1)
            if level < places.total_bits:
                sign = sign * flip(level)
            for i in range(tiles):
                keys[i] = keys[i] * sign
        for bit in range(level - 1, -1, -1):
            if bit >= tile_bits or (bit == 0 and level > tile_bits):
                trade_all(bit)
            step = 1 << bit if bit < tile_bits else 1
            for i in range(tiles):
                if not i & step:
                    exchange(keys, vals, i, i + step, level < tile_bits and (i >> level) & 1 == 1)
    assert places.of == list(range(places.total_bits))


def sort_kernel(
    me_ref, scan_hbm, resp_hbm, cycle_hbm, column_hbm, twiddle_hbm, forward_hbm, filtered_ref, *refs,
    buckets, span, rows, windows,
):
    send_refs, refs = refs[:buckets // windows], refs[buckets // windows:]
    scan_ref, resp_ref, cycle_ref, column_ref, twiddle_ref, forward_ref, arrived = refs[:7]
    key_ref, val_ref, spec_ref, key_rows, val_rows = refs[7:]
    lines, length = scan_ref.shape
    outer = length // LANES
    loads = [
        pltpu.make_async_copy(source, place, arrived.at[i])
        for i, (source, place) in enumerate([
            (scan_hbm, scan_ref), (twiddle_hbm, twiddle_ref), (forward_hbm, forward_ref),
            (resp_hbm, resp_ref), (cycle_hbm, cycle_ref), (column_hbm, column_ref),
        ])
    ]
    for load in loads:
        load.start()
    loads[0].wait()
    re, im = small_fft([scan_ref[:, n * LANES:(n + 1) * LANES] for n in range(outer)], None, -1)
    loads[1].wait()
    for k in range(outer):
        c, s = twiddle_ref[k:k + 1, :LANES], twiddle_ref[k:k + 1, LANES:]
        here = pl.ds(k * lines, lines)
        spec_ref[here, :LANES] = re[k] * c + im[k] * s
        spec_ref[here, LANES:] = im[k] * c - re[k] * s
    for load in loads[2:]:
        load.wait()
    spec = jnp.dot(spec_ref[...], forward_ref[...], precision=precise, preferred_element_type=jnp.float32)
    resp = [resp_ref[:, n * LANES:(n + 1) * LANES] * (1.0 / length) for n in range(outer)]
    step = 1
    while step < outer:
        upper = (lax.broadcasted_iota(jnp.int32, (lines, LANES), 1) & step) != 0
        for n in range(outer):
            if not n & step:
                resp[n], resp[n + step] = trade(resp[n], resp[n + step], upper, 1, step)
        step *= 2
    resp = jnp.concatenate(resp, axis=0)
    spec = spec * jnp.concatenate([resp, resp], axis=1)
    spec_ref[...] = lax.dot_general(
        spec, forward_ref[...], NT, precision=precise, preferred_element_type=jnp.float32
    )
    re, im = [], []
    for k in range(outer):
        c, s = twiddle_ref[k:k + 1, :LANES], twiddle_ref[k:k + 1, LANES:]
        here = pl.ds(k * lines, lines)
        ur, ui = spec_ref[here, :LANES], spec_ref[here, LANES:]
        re.append(ur * c - ui * s)
        im.append(ui * c + ur * s)
    out, _ = small_fft(re, im, 1)
    keys = []
    for n in range(outer):
        cols = slice(n * LANES, (n + 1) * LANES)
        filtered_ref[:, cols] = out[n]
        keys.append((cycle_ref[:, cols] * NPHI + column_ref[:, cols]).astype(jnp.float32))
    vals = list(out)
    sort_registers(keys, vals)
    row_len = outer * SUB
    last = functools.reduce(jnp.maximum, keys)
    first = functools.reduce(jnp.minimum, keys)
    last = jnp.max(last, axis=0, keepdims=True)
    first = jnp.min(first, axis=0, keepdims=True)
    for i in range(outer):
        key_ref[i * SUB:(i + 1) * SUB, :] = keys[i]
        val_ref[i * SUB:(i + 1) * SUB, :] = vals[i]
    key_rows[:LANES, :] = key_ref[...].T
    val_rows[:LANES, :] = val_ref[...].T
    reach = key_rows.shape[0] - LANES
    key_rows[LANES:, :] = jnp.full((reach, row_len), 2.0 * buckets * span, jnp.float32)
    val_rows[LANES:, :] = jnp.zeros((reach, row_len), jnp.float32)
    over = jnp.int32(0)
    for k, send_ref in enumerate(send_refs):
        for w in range(windows):
            bucket = (me_ref[0] ^ k) * windows + w
            low = (bucket * span).astype(jnp.float32)
            high = low + float(span)
            begin = jnp.sum((last < low).astype(jnp.float32)).astype(jnp.int32)
            end = jnp.sum((first < high).astype(jnp.float32)).astype(jnp.int32)
            over = over + (end - begin > rows).astype(jnp.int32)
            begin = jnp.minimum(begin, LANES)
            aligned = pl.multiple_of((begin // SUB) * SUB, SUB)
            back = lax.rem(reach - (begin - aligned), reach)
            here = pl.ds(aligned, reach)
            taken = pltpu.roll(key_rows[here, :], back, axis=0)[:rows]
            send_ref[w * rows:(w + 1) * rows, :] = taken - low
            at = (windows + w) * rows
            send_ref[at:at + rows, :] = pltpu.roll(val_rows[here, :], back, axis=0)[:rows]

    @pl.when(over > 0)
    def _():
        for send_ref in send_refs:
            send_ref[...] = jnp.full(send_ref.shape, jnp.nan, jnp.float32)


def filter_and_sort(me, scan, resp, cycle, column, det_count, band_cycles):
    lines, length = scan.shape
    tiles = length // LANES
    windows = WINDOWS
    buckets = det_count * windows
    span = band_cycles * NPHI // buckets
    row_len = tiles * SUB
    rows = LANES // buckets + 2
    reach = (rows + 2 * SUB - 2) // SUB * SUB
    twiddle, forward = filter_tables(length)
    operands = [scan, resp, cycle, column, jnp.asarray(twiddle), jnp.asarray(forward)]
    body = functools.partial(sort_kernel, buckets=buckets, span=span, rows=rows, windows=windows)
    vmem = pl.BlockSpec(memory_space=pltpu.VMEM)
    return pl.pallas_call(
        body,
        out_shape=(
            jax.ShapeDtypeStruct((lines, length), jnp.float32),
        ) + (jax.ShapeDtypeStruct((2 * windows * rows, row_len), jnp.float32),) * det_count,
        in_specs=[pl.BlockSpec(memory_space=pltpu.SMEM)]
        + [pl.BlockSpec(memory_space=pl.ANY)] * len(operands),
        out_specs=(vmem,) * (1 + det_count),
        scratch_shapes=[pltpu.VMEM(x.shape, x.dtype) for x in operands] + [
            pltpu.SemaphoreType.DMA((len(operands),)),
            pltpu.VMEM((row_len, LANES), jnp.float32),
            pltpu.VMEM((row_len, LANES), jnp.float32),
            pltpu.VMEM((tiles * lines, 2 * LANES), jnp.float32),
            pltpu.VMEM((LANES + reach, row_len), jnp.float32),
            pltpu.VMEM((LANES + reach, row_len), jnp.float32),
        ],
        compiler_params=pltpu.CompilerParams(vmem_limit_bytes=63 * 1024 * 1024),
        name="filter_sort",
    )(me, *operands)


def split2(x):
    high = x.astype(jnp.bfloat16)
    low = (x - high.astype(jnp.float32)).astype(jnp.bfloat16)
    return high, low


def bin_kernel(
    *refs, sources, windows, rows, window_cycles
):
    recv_refs, (pick_ref, table_hbm, map_ref, send_ref, flag_ref) = refs[:sources], refs[sources:-9]
    recv_ref, column_ref, left_a, left_b, right_a, right_b, acc_ref, table_ref, arrived = refs[-9:]
    load = pltpu.make_async_copy(table_hbm, table_ref, arrived)
    load.start()
    wide_rows = column_ref.shape[2]
    for e in range(sources):
        block = recv_refs[e][...]
        recv_ref[e] = block
        column_ref[e] = (block[:wide_rows].astype(jnp.int32) & (ROW - 1)).astype(jnp.float32).T
    left_refs, right_refs = (left_a, left_b), (right_a, right_b)
    row_len = recv_ref.shape[2]
    parts = NPHI // ROW
    area = parts * window_cycles
    a_iota = lax.broadcasted_iota(jnp.int32, (area, row_len), 0).astype(jnp.float32).astype(jnp.bfloat16)
    b_iota = [
        (lax.broadcasted_iota(jnp.int32, (row_len, LANES), 1) + first).astype(jnp.float32).astype(jnp.bfloat16)
        for first in range(0, ROW, LANES)
    ]
    zero, one = jnp.zeros((), jnp.bfloat16), jnp.ones((), jnp.bfloat16)

    def build(e, w, slot):
        left, right = left_refs[slot], right_refs[slot]
        for r in range(rows):
            q = recv_ref[e, w * rows + r:w * rows + r + 1, :].astype(jnp.int32)
            v = recv_ref[e, (windows + w) * rows + r:(windows + w) * rows + r + 1, :]
            high, low = split2(v)
            cycle = q >> 11
            inside = (q >= 0) & (cycle < window_cycles)
            a = jnp.where(inside, ((q >> 8) & (parts - 1)) * window_cycles + cycle, -1)
            a = a.astype(jnp.float32).astype(jnp.bfloat16)
            at = w * rows + r
            b = jnp.broadcast_to(column_ref[e, :, at:at + 1], (row_len, LANES)).astype(jnp.bfloat16)
            cols = slice(r * row_len, (r + 1) * row_len)
            hit = a_iota == a
            left[:area, cols] = jnp.where(hit, high, zero)
            left[area:2 * area, cols] = jnp.where(hit, low, zero)
            left[2 * area:, cols] = jnp.where(hit, one, zero)
            for i, iota in enumerate(b_iota):
                right[cols, i * LANES:(i + 1) * LANES] = jnp.where(iota == b, one, zero)

    def multiply(slot):
        acc_ref[...] += jnp.dot(left_refs[slot][...], right_refs[slot][...], preferred_element_type=jnp.float32)

    build(0, 0, 0)
    for w in range(windows):
        acc_ref[...] = jnp.zeros(acc_ref.shape, jnp.float32)

        def body(i, carry):
            build(2 * i + 1, w, 1)
            multiply(0)
            build(jnp.minimum(2 * i + 2, sources - 1), w, 0)
            multiply(1)
            return carry

        lax.fori_loop(0, sources // 2 - 1, body, 0)
        build(sources - 1, w, 1)
        multiply(0)
        if w + 1 < windows:
            build(0, w + 1, 0)
        multiply(1)
        acc = acc_ref[...]
        sky = (acc[:area] + acc[area:2 * area]) / jnp.maximum(acc[2 * area:], 1.0)
        for c8 in range(parts):
            map_ref[w * window_cycles:(w + 1) * window_cycles, c8 * ROW:(c8 + 1) * ROW] = (
                sky[c8 * window_cycles:(c8 + 1) * window_cycles]
            )
    load.wait()
    cycles = map_ref.shape[0]
    half = NPHI // 2
    modes = []
    for parity in (0, 1):
        a, b = map_ref[:, :half], map_ref[:, half:]
        high, low = split2(a + b if parity == 0 else a - b)
        first = jnp.dot(jnp.concatenate([high, low], axis=0), table_ref[0, parity], preferred_element_type=jnp.float32)
        second = jnp.dot(high, table_ref[1, parity], preferred_element_type=jnp.float32)
        modes.append(first[:cycles] + first[cycles:] + second)
    modes = jnp.concatenate(modes, axis=1)
    count = modes.shape[1]
    width = pick_ref.shape[1]
    high = modes.astype(jnp.bfloat16)
    rest = modes - high.astype(jnp.float32)
    middle = rest.astype(jnp.bfloat16)
    low = (rest - middle.astype(jnp.float32)).astype(jnp.bfloat16)
    pieces = jnp.concatenate([high, middle, low], axis=0)
    choose = (lax.broadcasted_iota(jnp.int32, (count, width), 0) == pick_ref[...])
    choose = jnp.where(choose, 1.0, 0.0).astype(jnp.bfloat16)
    moved = jnp.dot(pieces, choose, preferred_element_type=jnp.float32)
    moved = moved[:cycles] + moved[cycles:2 * cycles] + moved[2 * cycles:]
    owners, group_rows, lanes = send_ref.shape
    groups = cycles // group_rows
    lane_group = lax.broadcasted_iota(jnp.int32, (group_rows, lanes), 1) // (lanes // groups)
    values = recv_ref[:, windows * rows:, :]
    flag_ref[0] = (jnp.max(jnp.where(values == values, 0.0, 1.0)) > 0.0).astype(jnp.int32)
    for d in range(owners):
        block = moved[:, d * lanes:(d + 1) * lanes]
        out = block[:group_rows]
        for h in range(1, groups):
            out = jnp.where(lane_group == h, block[h * group_rows:(h + 1) * group_rows], out)
        send_ref[d] = out


def bin_and_modes(recv, order_slot, band_cycles):
    sources = len(recv)
    lines, row_len = recv[0].shape
    windows = WINDOWS
    rows = lines // (2 * windows)
    cycles = band_cycles // sources
    count = order_slot.shape[0]
    slots = count // sources
    groups = LANES // (2 * slots)
    tables = jnp.asarray(mode_tables(count))
    m = order_slot.reshape(sources, 1, 1, slots)
    part = jnp.arange(2, dtype=jnp.int32).reshape(1, 1, 2, 1)
    pick = (m & 1) * count + part * (count // 2) + (m >> 1)
    pick = jnp.broadcast_to(pick, (sources, groups, 2, slots)).reshape(1, sources * LANES)
    area = cycles // windows * (NPHI // ROW)
    depth = rows * row_len
    vmem = pl.BlockSpec(memory_space=pltpu.VMEM)
    return pl.pallas_call(
        functools.partial(bin_kernel, sources=sources, windows=windows, rows=rows, window_cycles=cycles // windows),
        out_shape=(
            jax.ShapeDtypeStruct((cycles, NPHI), jnp.float32),
            jax.ShapeDtypeStruct((sources, cycles // groups, LANES), jnp.float32),
            jax.ShapeDtypeStruct((1,), jnp.int32),
        ),
        in_specs=[vmem] * (sources + 1) + [pl.BlockSpec(memory_space=pl.ANY)],
        out_specs=(vmem, vmem, pl.BlockSpec(memory_space=pltpu.SMEM)),
        scratch_shapes=[
            pltpu.VMEM((sources, lines, row_len), jnp.float32),
            pltpu.VMEM((sources, row_len, -(-windows * rows // SUB) * SUB), jnp.float32),
            pltpu.VMEM((3 * area, depth), jnp.bfloat16),
            pltpu.VMEM((3 * area, depth), jnp.bfloat16),
            pltpu.VMEM((depth, ROW), jnp.bfloat16),
            pltpu.VMEM((depth, ROW), jnp.bfloat16),
            pltpu.VMEM((3 * area, ROW), jnp.float32),
            pltpu.VMEM(tables.shape, jnp.bfloat16),
            pltpu.SemaphoreType.DMA,
        ],
        compiler_params=pltpu.CompilerParams(vmem_limit_bytes=48 * 1024 * 1024),
        name="bin_modes",
    )(*recv, pick, tables)


def legendre_kernel(me_ref, recv_ref, table_ref, *refs, owners):
    out_refs, (leg_ref, arrived, modes_ref, wide_ref, sums_ref) = refs[:owners], refs[owners:]
    slots, band_cycles, degrees = table_ref.shape

    def load(slot):
        return pltpu.make_async_copy(table_ref.at[slot], leg_ref.at[slot], arrived.at[slot])

    def start(slot, carry):
        load(slot).start()
        return carry

    lax.fori_loop(0, slots, start, 0)
    sources, group_rows, lanes = recv_ref.shape
    groups = lanes // (2 * slots)
    width = out_refs[0].shape[1]
    tiles = degrees // LANES
    for e in range(sources):
        block = recv_ref[e]
        for h in range(groups):
            at = (e * groups + h) * group_rows
            turned = block if h == 0 else pltpu.roll(block, lanes - h * 2 * slots, axis=1)
            modes_ref[at:at + group_rows, :] = turned

    def widen(slot, half):
        turned = pltpu.roll(modes_ref[...], lax.rem(lanes - slot, lanes), axis=1)
        for c in range(2):
            column = turned[:, c * slots:c * slots + 1]
            wide_ref[half, c] = jnp.broadcast_to(column, (band_cycles, lanes))

    widen(0, 0)

    def body(slot, carry):
        half = slot & 1
        load(slot).wait()
        sums = [[jnp.zeros((SUB, LANES), jnp.float32) for _ in range(tiles)] for _ in range(2)]
        for r in range(0, band_cycles, SUB):
            factor = [wide_ref[half, c, r:r + SUB, :] for c in range(2)]
            for t in range(tiles):
                block = leg_ref[slot, r:r + SUB, t * LANES:(t + 1) * LANES]
                for c in range(2):
                    sums[c][t] = sums[c][t] + block * factor[c]
        widen(jnp.minimum(slot + 1, slots - 1), 1 - half)
        per_owner = width // LANES
        for c in range(2):
            lines = [jnp.sum(part, axis=0, keepdims=True) for part in sums[c]]
            for d in range(owners):
                line = jnp.concatenate(lines[d * per_owner:(d + 1) * per_owner], axis=1)
                sums_ref[d, pl.ds(c * slots + slot, 1), :] = line
        return carry

    lax.fori_loop(0, slots, body, 0)
    for k in range(owners):
        out_refs[k][...] = sums_ref[me_ref[0] ^ k]


def legendre_sums(me, recv, legendre, owners):
    slots, band_cycles, degrees = legendre.shape
    vmem = pl.BlockSpec(memory_space=pltpu.VMEM)
    return pl.pallas_call(
        functools.partial(legendre_kernel, owners=owners),
        out_shape=(jax.ShapeDtypeStruct((2 * slots, degrees // owners), jnp.float32),) * owners,
        in_specs=[pl.BlockSpec(memory_space=pltpu.SMEM), vmem, pl.BlockSpec(memory_space=pl.ANY)],
        out_specs=(vmem,) * owners,
        scratch_shapes=[
            pltpu.VMEM(legendre.shape, jnp.float32),
            pltpu.SemaphoreType.DMA((slots,)),
            pltpu.VMEM((band_cycles, LANES), jnp.float32),
            pltpu.VMEM((2, 2, band_cycles, LANES), jnp.float32),
            pltpu.VMEM((owners, 2 * slots, degrees // owners), jnp.float32),
        ],
        compiler_params=pltpu.CompilerParams(vmem_limit_bytes=44 * 1024 * 1024),
        name="legendre_sums",
    )(me, recv, legendre)


def exchange_and_sum(x, axis, count):
    parts = x.reshape(count, x.shape[0] // count, x.shape[1])
    return jnp.sum(lax.all_to_all(parts, axis, split_axis=0, concat_axis=0, tiled=True), axis=0)


def dense_path(filtered, cycle_offset, column, order_slot, band_cycles, det_count):
    flat_index = (cycle_offset * NPHI + column).reshape(-1)
    empty = jnp.zeros((band_cycles * NPHI,), jnp.float32)
    partial_value = empty.at[flat_index].add(filtered.reshape(-1)).reshape(band_cycles, NPHI)
    counts = empty.at[flat_index].add(1.0).reshape(band_cycles, NPHI)
    summed = exchange_and_sum(partial_value, "det", det_count)
    hit_total = exchange_and_sum(counts, "det", det_count)
    sky_map = summed / jnp.maximum(hit_total, 1.0)
    pixel_index = jnp.arange(NPHI, dtype=jnp.int32)[:, None]
    phases = 2.0 * jnp.pi / NPHI * (pixel_index * order_slot[None, :] % NPHI).astype(jnp.float32)
    modes = jnp.stack([
        jnp.dot(sky_map, jnp.cos(phases), precision=precise),
        -jnp.dot(sky_map, jnp.sin(phases), precision=precise),
    ])
    slots = order_slot.shape[0] // det_count
    groups = LANES // (2 * slots)
    blocks = modes.reshape(2, groups, -1, det_count, slots).transpose(3, 2, 1, 0, 4)
    blocks = blocks.reshape(det_count, -1, LANES)
    return sky_map, lax.all_to_all(blocks, "det", split_axis=0, concat_axis=0, tiled=True)


def swap_blocks(blocks, axis):
    count = len(blocks)
    out = list(blocks)
    for k in range(count - 1, 0, -1):
        out[k] = lax.ppermute(blocks[k], axis, [(i, i ^ k) for i in range(count)])
    return out


def local(scan_lines, response, cycle_offset, column, order_slot, legendre, *, det_count, band_count):
    slots, band_cycles, degrees = legendre.shape
    me = lax.axis_index("det").astype(jnp.int32).reshape(1)
    filtered, *send = filter_and_sort(
        me, scan_lines, response, cycle_offset, column, det_count, band_cycles
    )
    recv = swap_blocks(send, "det")
    sky_map, modes, crowded = bin_and_modes(recv, order_slot, band_cycles)
    modes = lax.all_to_all(modes, "det", split_axis=0, concat_axis=0, tiled=True)
    sky_map, modes = lax.cond(
        crowded[0] > 0,
        lambda: dense_path(filtered, cycle_offset, column, order_slot, band_cycles, det_count),
        lambda: (sky_map, modes),
    )
    band = lax.axis_index("band").astype(jnp.int32)
    terms = swap_blocks(legendre_sums(band.reshape(1), modes, legendre, band_count), "band")
    sums = functools.reduce(jnp.add, terms)
    local_orders = lax.dynamic_slice_in_dim(order_slot, lax.axis_index("det") * slots, slots, 0)
    width = degrees // band_count
    degree = band * width + jnp.arange(width, dtype=jnp.int32)
    keep = degree[None, None, :] >= local_orders[None, :, None]
    return jnp.where(keep, sums.reshape(2, slots, width), 0.0), sky_map


def solution(mesh):
    sizes = dict(mesh.shape)
    return jax.shard_map(
        functools.partial(local, det_count=sizes["det"], band_count=sizes["band"]),
        mesh=mesh,
        in_specs=(
            P(("det", "band"), None),
            P(("det", "band"), None),
            P(("det", "band"), None),
            P(("det", "band"), None),
            P(),
            P("det", "band", None),
        ),
        out_specs=(P(None, "det", "band"), P(("band", "det"), None)),
        check_vma=False,
    )
```

```python
import functools

import jax
import jax.numpy as jnp
import numpy as np
from jax import lax
from jax.experimental import pallas as pl
from jax.experimental.pallas import tpu as pltpu
from jax.sharding import PartitionSpec as P

NPHI = 2048
LANES = 128
SUB = 8
WINDOWS = 2
ROW = 256
PIECE, PIECES, STEP, TOP = jnp.float8_e4m3fn, 3, 32.0, 224.0

precise = lax.Precision.HIGHEST
NT = (((1,), (1,)), ((), ()))


def filter_tables(length):
    outer = length // LANES
    k1 = np.arange(outer)[:, None]
    n2 = np.arange(LANES)[None, :]
    turn = 2.0 * np.pi * ((k1 * n2) % length) / length
    twiddle = np.concatenate([np.cos(turn), np.sin(turn)], axis=1)
    a = np.arange(LANES)
    angle = 2.0 * np.pi * (np.outer(a, a) % LANES) / LANES
    c, s = np.cos(angle), np.sin(angle)
    order = (a % outer) * (LANES // outer) + a // outer
    c, s = c[:, order], s[:, order]
    forward = np.block([[c, -s], [s, c]])
    return np.concatenate([forward, twiddle]).astype(np.float32)


def mode_tables(count):
    half = NPHI // 2
    p = np.arange(half)[:, None]
    out = []
    for parity in (0, 1):
        m = 2 * np.arange(count // 2)[None, :] + parity
        angle = 2.0 * np.pi * ((p * m) % NPHI) / NPHI
        out.append(np.concatenate([np.cos(angle), -np.sin(angle)], axis=1))
    table = np.stack(out).astype(np.float32)
    high = table.astype(jnp.bfloat16)
    low = (table - high.astype(np.float32)).astype(jnp.bfloat16)
    return high, low


def small_fft(re, im, sign):
    count = len(re)
    if count == 1:
        return re, im
    even_re, even_im = small_fft(re[0::2], None if im is None else im[0::2], sign)
    odd_re, odd_im = small_fft(re[1::2], None if im is None else im[1::2], sign)
    half = count // 2
    out_re, out_im = [None] * count, [None] * count
    for k in range(half):
        wr = float(np.cos(2 * np.pi * k / count))
        wi = float(sign * np.sin(2 * np.pi * k / count))
        er, ei, orr, oi = even_re[k], even_im and even_im[k], odd_re[k], odd_im and odd_im[k]
        if k == 0:
            tr, ti = orr, oi
        elif 4 * k == count:
            tr = None if oi is None else -wi * oi
            ti = wi * orr
        elif oi is None:
            tr, ti = wr * orr, wi * orr
        else:
            tr, ti = wr * orr - wi * oi, wr * oi + wi * orr
        out_re[k] = er if tr is None else er + tr
        out_re[k + half] = er if tr is None else er - tr
        if ti is None:
            out_im[k] = out_im[k + half] = ei
        else:
            out_im[k] = ti if ei is None else ei + ti
            out_im[k + half] = -ti if ei is None else ei - ti
    if all(x is None for x in out_im):
        return out_re, None
    out_im = [jnp.zeros_like(out_re[0]) if x is None else x for x in out_im]
    return out_re, out_im


class Places:
    def __init__(self, tile_bits, total_bits):
        self.tile_bits, self.total_bits = tile_bits, total_bits
        self.of = list(range(total_bits))
        for level in range(tile_bits + 1, total_bits + 1):
            self.walk(level)
        held = [self.of.index(place) for place in range(total_bits)]
        self.of = held

    def swap(self, bit):
        other = self.of.index(0)
        self.of[bit], self.of[other] = 0, self.of[bit]

    def walk(self, level):
        for bit in range(level - 1, self.tile_bits - 1, -1):
            self.swap(bit)
        self.swap(0)

    def axis_distance(self, bit):
        place = self.of[bit] - self.tile_bits
        return (0, 1 << place) if place < 3 else (1, 1 << (place - 3))

    def mask(self, bit):
        axis, distance = self.axis_distance(bit)
        return (lax.broadcasted_iota(jnp.int32, (SUB, LANES), axis) & distance) != 0


def trade(low, high, upper, axis, distance):
    axis += low.ndim - 2
    size = low.shape[axis]
    return (
        jnp.where(upper, pltpu.roll(high, distance, axis=axis), low),
        jnp.where(upper, high, pltpu.roll(low, size - distance, axis=axis)),
    )


def exchange(keys, vals, a, b, down):
    if down:
        a, b = b, a
    swap = keys[a] > keys[b]
    keys[a], keys[b] = jnp.minimum(keys[a], keys[b]), jnp.maximum(keys[a], keys[b])
    vals[a], vals[b] = jnp.where(swap, vals[b], vals[a]), jnp.where(swap, vals[a], vals[b])


def sort_registers(keys, vals):
    tiles = len(keys)
    tile_bits = tiles.bit_length() - 1
    places = Places(tile_bits, tile_bits + 10)

    def flip(bit):
        return jnp.where(places.mask(bit), -1.0, 1.0)

    def trade_all(bit):
        upper, (axis, distance) = places.mask(bit), places.axis_distance(bit)
        places.swap(bit)
        for i in range(0, tiles, 2):
            keys[i], keys[i + 1] = trade(keys[i], keys[i + 1], upper, axis, distance)
            vals[i], vals[i + 1] = trade(vals[i], vals[i + 1], upper, axis, distance)

    for level in range(1, places.total_bits + 1):
        if level >= tile_bits:
            sign = 1.0
            if level > tile_bits:
                sign = flip(level - 1)
            if level < places.total_bits:
                sign = sign * flip(level)
            for i in range(tiles):
                keys[i] = keys[i] * sign
        for bit in range(level - 1, -1, -1):
            if bit >= tile_bits or (bit == 0 and level > tile_bits):
                trade_all(bit)
            step = 1 << bit if bit < tile_bits else 1
            for i in range(tiles):
                if not i & step:
                    exchange(keys, vals, i, i + step, level < tile_bits and (i >> level) & 1 == 1)
    assert places.of == list(range(places.total_bits))


def sort_kernel(
    me_ref, scan_hbm, resp_hbm, cycle_hbm, column_hbm, table_hbm, *refs,
    buckets, span, rows, windows,
):
    send_refs, refs = refs[:buckets // windows], refs[buckets // windows:]
    scan_ref, resp_ref, cycle_ref, column_ref, table_ref, arrived = refs[:6]
    key_ref, val_ref, spec_ref, key_rows, val_rows = refs[6:]
    lines, length = scan_ref.shape
    outer = length // LANES
    loads = [
        pltpu.make_async_copy(source, place, arrived.at[i])
        for i, (source, place) in enumerate([
            (scan_hbm, scan_ref), (table_hbm, table_ref), (resp_hbm, resp_ref),
            (cycle_hbm, cycle_ref), (column_hbm, column_ref),
        ])
    ]
    for load in loads:
        load.start()
    def twiddle_row(k):
        at = 2 * LANES + k
        return table_ref[at:at + 1, :LANES], table_ref[at:at + 1, LANES:]

    loads[0].wait()
    re, im = small_fft([scan_ref[:, n * LANES:(n + 1) * LANES] for n in range(outer)], None, -1)
    loads[1].wait()
    forward = table_ref[:2 * LANES, :]
    for k in range(outer):
        c, s = twiddle_row(k)
        here = pl.ds(k * lines, lines)
        spec_ref[here, :LANES] = re[k] * c + im[k] * s
        spec_ref[here, LANES:] = im[k] * c - re[k] * s
    for load in loads[2:]:
        load.wait()
    spec = jnp.dot(spec_ref[...], forward, precision=precise, preferred_element_type=jnp.float32)
    resp = [resp_ref[:, n * LANES:(n + 1) * LANES] * (1.0 / length) for n in range(outer)]
    step = 1
    while step < outer:
        upper = (lax.broadcasted_iota(jnp.int32, (lines, LANES), 1) & step) != 0
        for n in range(outer):
            if not n & step:
                resp[n], resp[n + step] = trade(resp[n], resp[n + step], upper, 1, step)
        step *= 2
    resp = jnp.concatenate(resp, axis=0)
    spec = spec * jnp.concatenate([resp, resp], axis=1)
    spec_ref[...] = lax.dot_general(
        spec, forward, NT, precision=precise, preferred_element_type=jnp.float32
    )
    re, im = [], []
    for k in range(outer):
        c, s = twiddle_row(k)
        here = pl.ds(k * lines, lines)
        ur, ui = spec_ref[here, :LANES], spec_ref[here, LANES:]
        re.append(ur * c - ui * s)
        im.append(ui * c + ur * s)
    out, _ = small_fft(re, im, 1)
    keys = []
    for n in range(outer):
        cols = slice(n * LANES, (n + 1) * LANES)
        keys.append((cycle_ref[:, cols] * NPHI + column_ref[:, cols]).astype(jnp.float32))
    vals = list(out)
    sort_registers(keys, vals)
    row_len = outer * SUB
    last = functools.reduce(jnp.maximum, keys)
    first = functools.reduce(jnp.minimum, keys)
    last = jnp.max(last, axis=0, keepdims=True)
    first = jnp.min(first, axis=0, keepdims=True)
    for i in range(outer):
        key_ref[i * SUB:(i + 1) * SUB, :] = keys[i]
        val_ref[i * SUB:(i + 1) * SUB, :] = vals[i]
    key_rows[:LANES, :] = key_ref[...].T
    val_rows[:LANES, :] = val_ref[...].T
    reach = key_rows.shape[0] - LANES
    key_rows[LANES:, :] = jnp.full((reach, row_len), 2.0 * buckets * span, jnp.float32)
    val_rows[LANES:, :] = jnp.zeros((reach, row_len), jnp.float32)
    over = jnp.int32(0)
    for k, send_ref in enumerate(send_refs):
        for w in range(windows):
            bucket = (me_ref[0] ^ k) * windows + w
            low = (bucket * span).astype(jnp.float32)
            high = low + float(span)
            begin = jnp.sum((last < low).astype(jnp.float32)).astype(jnp.int32)
            end = jnp.sum((first < high).astype(jnp.float32)).astype(jnp.int32)
            over = over + (end - begin > rows).astype(jnp.int32)
            begin = jnp.minimum(begin, LANES)
            aligned = pl.multiple_of((begin // SUB) * SUB, SUB)
            back = lax.rem(reach - (begin - aligned), reach)
            here = pl.ds(aligned, reach)
            taken = pltpu.roll(key_rows[here, :], back, axis=0)[:rows]
            send_ref[w * rows:(w + 1) * rows, :] = taken - low
            at = (windows + w) * rows
            send_ref[at:at + rows, :] = pltpu.roll(val_rows[here, :], back, axis=0)[:rows]

    @pl.when(over > 0)
    def _():
        for send_ref in send_refs:
            send_ref[...] = jnp.full(send_ref.shape, jnp.nan, jnp.float32)


def filter_and_sort(me, table, scan, resp, cycle, column, det_count, band_cycles):
    lines, length = scan.shape
    tiles = length // LANES
    windows = WINDOWS
    buckets = det_count * windows
    span = band_cycles * NPHI // buckets
    row_len = tiles * SUB
    rows = LANES // buckets + 2
    reach = (rows + 2 * SUB - 2) // SUB * SUB
    operands = [scan, resp, cycle, column, table]
    body = functools.partial(sort_kernel, buckets=buckets, span=span, rows=rows, windows=windows)
    vmem = pl.BlockSpec(memory_space=pltpu.VMEM)
    return pl.pallas_call(
        body,
        out_shape=(jax.ShapeDtypeStruct((2 * windows * rows, row_len), jnp.float32),) * det_count,
        in_specs=[pl.BlockSpec(memory_space=pltpu.SMEM)]
        + [pl.BlockSpec(memory_space=pl.ANY)] * len(operands),
        out_specs=(vmem,) * det_count,
        scratch_shapes=[pltpu.VMEM(x.shape, x.dtype) for x in operands] + [
            pltpu.SemaphoreType.DMA((len(operands),)),
            pltpu.VMEM((row_len, LANES), jnp.float32),
            pltpu.VMEM((row_len, LANES), jnp.float32),
            pltpu.VMEM((tiles * lines, 2 * LANES), jnp.float32),
            pltpu.VMEM((LANES + reach, row_len), jnp.float32),
            pltpu.VMEM((LANES + reach, row_len), jnp.float32),
        ],
        compiler_params=pltpu.CompilerParams(vmem_limit_bytes=24 * 1024 * 1024),
        name="filter_sort",
    )(me, *operands)


def split2(x):
    high = x.astype(jnp.bfloat16)
    low = (x - high.astype(jnp.float32)).astype(jnp.bfloat16)
    return high, low


def bin_kernel(
    *refs, sources, windows, rows, window_cycles
):
    recv_refs, (pick_ref, table_hi, table_lo, map_ref, send_ref, flag_ref) = refs[:sources], refs[sources:-6]
    recv_ref, left_a, left_b, right_a, right_b, acc_ref = refs[-6:]
    for e in range(sources):
        recv_ref[e] = recv_refs[e][...]
    left_refs, right_refs = (left_a, left_b), (right_a, right_b)
    row_len = recv_ref.shape[2]
    parts = NPHI // ROW
    area = parts * window_cycles
    a_iota = lax.broadcasted_iota(jnp.int32, (area, row_len), 0).astype(jnp.int8)
    b_iota = (lax.broadcasted_iota(jnp.int32, (ROW, row_len), 0) - ROW // 2).astype(jnp.int8)
    zero, one = jnp.zeros((), PIECE), jnp.ones((), PIECE)
    values = recv_ref[:, windows * rows:, :]
    largest = jnp.max(jnp.max(jnp.abs(values), axis=0), axis=(0, 1), keepdims=True)
    scale = jnp.where(largest > 0.0, TOP / largest, 1.0)

    def build(e, w, slot):
        left, right = left_refs[slot], right_refs[slot]
        for r in range(rows):
            q = recv_ref[e, w * rows + r:w * rows + r + 1, :].astype(jnp.int32)
            rest = recv_ref[e, (windows + w) * rows + r:(windows + w) * rows + r + 1, :] * scale
            cycle = q >> 11
            inside = (q >= 0) & (cycle < window_cycles)
            a = jnp.where(inside, ((q >> 8) & (parts - 1)) * window_cycles + cycle, -1).astype(jnp.int8)
            b = ((q & (ROW - 1)) - ROW // 2).astype(jnp.int8)
            cols = slice(r * row_len, (r + 1) * row_len)
            hit = a_iota == a
            for p in range(PIECES):
                piece = rest.astype(PIECE)
                rest = (rest - piece.astype(jnp.float32)) * STEP
                left[p * area:(p + 1) * area, cols] = jnp.where(hit, piece, zero)
            left[PIECES * area:, cols] = jnp.where(hit, one, zero)
            right[:, cols] = jnp.where(b_iota == b, one, zero)

    def multiply(slot):
        acc_ref[...] += lax.dot_general(
            left_refs[slot][...], right_refs[slot][...], NT, preferred_element_type=jnp.float32
        )

    build(0, 0, 0)
    for w in range(windows):
        acc_ref[...] = jnp.zeros(acc_ref.shape, jnp.float32)

        def body(i, carry):
            build(2 * i + 1, w, 1)
            multiply(0)
            build(jnp.minimum(2 * i + 2, sources - 1), w, 0)
            multiply(1)
            return carry

        lax.fori_loop(0, sources // 2 - 1, body, 0)
        build(sources - 1, w, 1)
        multiply(0)
        if w + 1 < windows:
            build(0, w + 1, 0)
        multiply(1)
        acc = acc_ref[...]
        total = acc[(PIECES - 1) * area:PIECES * area]
        for p in range(PIECES - 2, -1, -1):
            total = acc[p * area:(p + 1) * area] + total * (1.0 / STEP)
        sky = total / scale / jnp.maximum(acc[PIECES * area:], 1.0)
        for c8 in range(parts):
            map_ref[w * window_cycles:(w + 1) * window_cycles, c8 * ROW:(c8 + 1) * ROW] = (
                sky[c8 * window_cycles:(c8 + 1) * window_cycles]
            )
    cycles = map_ref.shape[0]
    half = NPHI // 2
    modes = []
    for parity in (0, 1):
        a, b = map_ref[:, :half], map_ref[:, half:]
        high, low = split2(a + b if parity == 0 else a - b)
        first = jnp.dot(jnp.concatenate([high, low], axis=0), table_hi[parity], preferred_element_type=jnp.float32)
        second = jnp.dot(high, table_lo[parity], preferred_element_type=jnp.float32)
        modes.append(first[:cycles] + first[cycles:] + second)
    modes = jnp.concatenate(modes, axis=1)
    count = modes.shape[1]
    width = pick_ref.shape[1]
    high = modes.astype(jnp.bfloat16)
    rest = modes - high.astype(jnp.float32)
    middle = rest.astype(jnp.bfloat16)
    low = (rest - middle.astype(jnp.float32)).astype(jnp.bfloat16)
    pieces = jnp.concatenate([high, middle, low], axis=0)
    choose = (lax.broadcasted_iota(jnp.int32, (count, width), 0) == pick_ref[...])
    choose = jnp.where(choose, 1.0, 0.0).astype(jnp.bfloat16)
    moved = jnp.dot(pieces, choose, preferred_element_type=jnp.float32)
    moved = moved[:cycles] + moved[cycles:2 * cycles] + moved[2 * cycles:]
    owners, group_rows, lanes = send_ref.shape
    groups = cycles // group_rows
    lane_group = lax.broadcasted_iota(jnp.int32, (group_rows, lanes), 1) // (lanes // groups)
    flag_ref[0] = (jnp.max(jnp.where(values == values, 0.0, 1.0)) > 0.0).astype(jnp.int32)
    for d in range(owners):
        block = moved[:, d * lanes:(d + 1) * lanes]
        out = block[:group_rows]
        for h in range(1, groups):
            out = jnp.where(lane_group == h, block[h * group_rows:(h + 1) * group_rows], out)
        send_ref[d] = out


def bin_and_modes(recv, order_slot, band_cycles):
    sources = len(recv)
    lines, row_len = recv[0].shape
    windows = WINDOWS
    rows = lines // (2 * windows)
    cycles = band_cycles // sources
    count = order_slot.shape[0]
    slots = count // sources
    groups = LANES // (2 * slots)
    high, low = mode_tables(count)
    m = order_slot.reshape(sources, 1, 1, slots)
    part = jnp.arange(2, dtype=jnp.int32).reshape(1, 1, 2, 1)
    pick = (m & 1) * count + part * (count // 2) + (m >> 1)
    pick = jnp.broadcast_to(pick, (sources, groups, 2, slots)).reshape(1, sources * LANES)
    area = cycles // windows * (NPHI // ROW)
    depth = rows * row_len
    vmem = pl.BlockSpec(memory_space=pltpu.VMEM)
    return pl.pallas_call(
        functools.partial(bin_kernel, sources=sources, windows=windows, rows=rows, window_cycles=cycles // windows),
        out_shape=(
            jax.ShapeDtypeStruct((cycles, NPHI), jnp.float32),
            jax.ShapeDtypeStruct((sources, cycles // groups, LANES), jnp.float32),
            jax.ShapeDtypeStruct((1,), jnp.int32),
        ),
        in_specs=[vmem] * (sources + 3),
        out_specs=(vmem, vmem, pl.BlockSpec(memory_space=pltpu.SMEM)),
        scratch_shapes=[
            pltpu.VMEM((sources, lines, row_len), jnp.float32),
            pltpu.VMEM(((PIECES + 1) * area, depth), PIECE),
            pltpu.VMEM(((PIECES + 1) * area, depth), PIECE),
            pltpu.VMEM((ROW, depth), PIECE),
            pltpu.VMEM((ROW, depth), PIECE),
            pltpu.VMEM(((PIECES + 1) * area, ROW), jnp.float32),
        ],
        compiler_params=pltpu.CompilerParams(vmem_limit_bytes=40 * 1024 * 1024),
        name="bin_modes",
    )(*recv, pick, jnp.asarray(high), jnp.asarray(low))


def legendre_kernel(me_ref, recv_ref, table_ref, *refs, owners):
    out_refs, (leg_ref, arrived, modes_ref, wide_ref, sums_ref) = refs[:owners], refs[owners:]
    slots, band_cycles, degrees = table_ref.shape

    def load(slot):
        return pltpu.make_async_copy(table_ref.at[slot], leg_ref.at[slot], arrived.at[slot])

    def start(slot, carry):
        load(slot).start()
        return carry

    lax.fori_loop(0, slots, start, 0)
    sources, group_rows, lanes = recv_ref.shape
    groups = lanes // (2 * slots)
    width = out_refs[0].shape[1]
    tiles = degrees // LANES
    for e in range(sources):
        block = recv_ref[e]
        for h in range(groups):
            at = (e * groups + h) * group_rows
            turned = block if h == 0 else pltpu.roll(block, lanes - h * 2 * slots, axis=1)
            modes_ref[at:at + group_rows, :] = turned

    def widen(slot, half):
        turned = pltpu.roll(modes_ref[...], lax.rem(lanes - slot, lanes), axis=1)
        for c in range(2):
            column = turned[:, c * slots:c * slots + 1]
            wide_ref[half, c] = jnp.broadcast_to(column, (band_cycles, lanes))

    widen(0, 0)

    def body(slot, carry):
        half = slot & 1
        load(slot).wait()
        sums = [[jnp.zeros((SUB, LANES), jnp.float32) for _ in range(tiles)] for _ in range(2)]
        for r in range(0, band_cycles, SUB):
            factor = [wide_ref[half, c, r:r + SUB, :] for c in range(2)]
            for t in range(tiles):
                block = leg_ref[slot, r:r + SUB, t * LANES:(t + 1) * LANES]
                for c in range(2):
                    sums[c][t] = sums[c][t] + block * factor[c]
        widen(jnp.minimum(slot + 1, slots - 1), 1 - half)
        per_owner = width // LANES
        for c in range(2):
            lines = [jnp.sum(part, axis=0, keepdims=True) for part in sums[c]]
            for d in range(owners):
                line = jnp.concatenate(lines[d * per_owner:(d + 1) * per_owner], axis=1)
                sums_ref[d, pl.ds(c * slots + slot, 1), :] = line
        return carry

    lax.fori_loop(0, slots, body, 0)
    for k in range(owners):
        out_refs[k][...] = sums_ref[me_ref[0] ^ k]


def legendre_sums(me, recv, legendre, owners):
    slots, band_cycles, degrees = legendre.shape
    vmem = pl.BlockSpec(memory_space=pltpu.VMEM)
    return pl.pallas_call(
        functools.partial(legendre_kernel, owners=owners),
        out_shape=(jax.ShapeDtypeStruct((2 * slots, degrees // owners), jnp.float32),) * owners,
        in_specs=[pl.BlockSpec(memory_space=pltpu.SMEM), vmem, pl.BlockSpec(memory_space=pl.ANY)],
        out_specs=(vmem,) * owners,
        scratch_shapes=[
            pltpu.VMEM(legendre.shape, jnp.float32),
            pltpu.SemaphoreType.DMA((slots,)),
            pltpu.VMEM((band_cycles, LANES), jnp.float32),
            pltpu.VMEM((2, 2, band_cycles, LANES), jnp.float32),
            pltpu.VMEM((owners, 2 * slots, degrees // owners), jnp.float32),
        ],
        compiler_params=pltpu.CompilerParams(vmem_limit_bytes=44 * 1024 * 1024),
        name="legendre_sums",
    )(me, recv, legendre)


def exchange_and_sum(x, axis, count):
    parts = x.reshape(count, x.shape[0] // count, x.shape[1])
    return jnp.sum(lax.all_to_all(parts, axis, split_axis=0, concat_axis=0, tiled=True), axis=0)


def dense_filter(table, scan, resp):
    lines, length = scan.shape
    outer = length // LANES
    forward = table[:2 * LANES]
    c, s = table[2 * LANES:, :LANES], table[2 * LANES:, LANES:]
    k = jnp.arange(outer, dtype=jnp.int32)
    angle = 2.0 * jnp.pi / outer * (k[:, None] * k[None, :] % outer).astype(jnp.float32)
    x = scan.reshape(lines, outer, LANES)
    re = jnp.einsum("lna,nk->lka", x, jnp.cos(angle), precision=precise)
    im = -jnp.einsum("lna,nk->lka", x, jnp.sin(angle), precision=precise)
    spec = jnp.concatenate([re * c + im * s, im * c - re * s], axis=-1)
    spec = jnp.einsum("lki,ij->lkj", spec, forward, precision=precise)
    split = LANES // outer
    weight = resp.reshape(lines, outer, split, outer).transpose(0, 3, 2, 1).reshape(lines, outer, LANES)
    spec = spec * jnp.concatenate([weight, weight], axis=-1)
    spec = jnp.einsum("lki,ji->lkj", spec, forward, precision=precise)
    ur, ui = spec[..., :LANES], spec[..., LANES:]
    out = jnp.einsum("lka,kn->lna", ur * c - ui * s, jnp.cos(angle), precision=precise)
    out = out - jnp.einsum("lka,kn->lna", ui * c + ur * s, jnp.sin(angle), precision=precise)
    return (out / length).reshape(lines, length)


def dense_path(table, scan_lines, response, cycle_offset, column, order_slot, band_cycles, det_count):
    filtered = dense_filter(table, scan_lines, response)
    flat_index = (cycle_offset * NPHI + column).reshape(-1)
    empty = jnp.zeros((band_cycles * NPHI,), jnp.float32)
    partial_value = empty.at[flat_index].add(filtered.reshape(-1)).reshape(band_cycles, NPHI)
    counts = empty.at[flat_index].add(1.0).reshape(band_cycles, NPHI)
    summed = exchange_and_sum(partial_value, "det", det_count)
    hit_total = exchange_and_sum(counts, "det", det_count)
    sky_map = summed / jnp.maximum(hit_total, 1.0)
    pixel_index = jnp.arange(NPHI, dtype=jnp.int32)[:, None]
    phases = 2.0 * jnp.pi / NPHI * (pixel_index * order_slot[None, :] % NPHI).astype(jnp.float32)
    modes = jnp.stack([
        jnp.dot(sky_map, jnp.cos(phases), precision=precise),
        -jnp.dot(sky_map, jnp.sin(phases), precision=precise),
    ])
    slots = order_slot.shape[0] // det_count
    groups = LANES // (2 * slots)
    blocks = modes.reshape(2, groups, -1, det_count, slots).transpose(3, 2, 1, 0, 4)
    blocks = blocks.reshape(det_count, -1, LANES)
    return sky_map, lax.all_to_all(blocks, "det", split_axis=0, concat_axis=0, tiled=True)


def swap_blocks(blocks, axis):
    count = len(blocks)
    out = list(blocks)
    for k in range(count - 1, 0, -1):
        out[k] = lax.ppermute(blocks[k], axis, [(i, i ^ k) for i in range(count)])
    return out


def local(scan_lines, response, cycle_offset, column, order_slot, legendre, *, det_count, band_count):
    slots, band_cycles, degrees = legendre.shape
    me = lax.axis_index("det").astype(jnp.int32).reshape(1)
    table = jnp.asarray(filter_tables(scan_lines.shape[1]))
    send = filter_and_sort(
        me, table, scan_lines, response, cycle_offset, column, det_count, band_cycles
    )
    recv = swap_blocks(send, "det")
    sky_map, modes, crowded = bin_and_modes(recv[::-1], order_slot, band_cycles)
    modes = lax.all_to_all(modes, "det", split_axis=0, concat_axis=0, tiled=True)
    sky_map, modes = lax.cond(
        crowded[0] > 0,
        lambda: dense_path(
            table, scan_lines, response, cycle_offset, column, order_slot, band_cycles, det_count
        ),
        lambda: (sky_map, modes),
    )
    band = lax.axis_index("band").astype(jnp.int32)
    terms = swap_blocks(legendre_sums(band.reshape(1), modes, legendre, band_count), "band")
    sums = functools.reduce(jnp.add, terms)
    local_orders = lax.dynamic_slice_in_dim(order_slot, lax.axis_index("det") * slots, slots, 0)
    width = degrees // band_count
    degree = band * width + jnp.arange(width, dtype=jnp.int32)
    keep = degree[None, None, :] >= local_orders[None, :, None]
    return jnp.where(keep, sums.reshape(2, slots, width), 0.0), sky_map


def solution(mesh):
    sizes = dict(mesh.shape)
    return jax.shard_map(
        functools.partial(local, det_count=sizes["det"], band_count=sizes["band"]),
        mesh=mesh,
        in_specs=(
            P(("det", "band"), None),
            P(("det", "band"), None),
            P(("det", "band"), None),
            P(("det", "band"), None),
            P(),
            P("det", "band", None),
        ),
        out_specs=(P(None, "det", "band"), P(("band", "det"), None)),
        check_vma=False,
    )
```

```python
import functools

import jax
import jax.numpy as jnp
import numpy as np
from jax import lax
from jax.experimental import pallas as pl
from jax.experimental.pallas import tpu as pltpu
from jax.sharding import PartitionSpec as P

NPHI = 2048
LANES = 128
SUB = 8
WINDOWS = 2
ROW = 256
PIECE, PIECES, STEP, TOP = jnp.float8_e4m3fn, 3, 32.0, 224.0
KEEP = 2.0**20 + 1.0

precise = lax.Precision.HIGHEST
NT = (((1,), (1,)), ((), ()))


def filter_tables(length):
    outer = length // LANES
    k1 = np.arange(outer)[:, None]
    n2 = np.arange(LANES)[None, :]
    turn = 2.0 * np.pi * ((k1 * n2) % length) / length
    twiddle = np.concatenate([np.cos(turn), np.sin(turn)], axis=1)
    a = np.arange(LANES)
    angle = 2.0 * np.pi * (np.outer(a, a) % LANES) / LANES
    c, s = np.cos(angle), np.sin(angle)
    order = (a % outer) * (LANES // outer) + a // outer
    c, s = c[:, order], s[:, order]
    forward = np.block([[c, -s], [s, c]])
    return np.concatenate([forward, twiddle]).astype(np.float32)


def mode_tables(count):
    half = NPHI // 2
    p = np.arange(half)[:, None]
    out = []
    for parity in (0, 1):
        m = 2 * np.arange(count // 2)[None, :] + parity
        angle = 2.0 * np.pi * ((p * m) % NPHI) / NPHI
        out.append(np.concatenate([np.cos(angle), -np.sin(angle)], axis=1))
    table = np.stack(out).astype(np.float32)
    high = table.astype(jnp.bfloat16)
    low = (table - high.astype(np.float32)).astype(jnp.bfloat16)
    return np.stack([high, low])


def small_fft(re, im, sign):
    count = len(re)
    if count == 1:
        return re, im
    even_re, even_im = small_fft(re[0::2], None if im is None else im[0::2], sign)
    odd_re, odd_im = small_fft(re[1::2], None if im is None else im[1::2], sign)
    half = count // 2
    out_re, out_im = [None] * count, [None] * count
    for k in range(half):
        wr = float(np.cos(2 * np.pi * k / count))
        wi = float(sign * np.sin(2 * np.pi * k / count))
        er, ei, orr, oi = even_re[k], even_im and even_im[k], odd_re[k], odd_im and odd_im[k]
        if k == 0:
            tr, ti = orr, oi
        elif 4 * k == count:
            tr = None if oi is None else -wi * oi
            ti = wi * orr
        elif oi is None:
            tr, ti = wr * orr, wi * orr
        else:
            tr, ti = wr * orr - wi * oi, wr * oi + wi * orr
        out_re[k] = er if tr is None else er + tr
        out_re[k + half] = er if tr is None else er - tr
        if ti is None:
            out_im[k] = out_im[k + half] = ei
        else:
            out_im[k] = ti if ei is None else ei + ti
            out_im[k + half] = -ti if ei is None else ei - ti
    if all(x is None for x in out_im):
        return out_re, None
    out_im = [jnp.zeros_like(out_re[0]) if x is None else x for x in out_im]
    return out_re, out_im


class Places:
    def __init__(self, tile_bits, total_bits):
        self.tile_bits, self.total_bits = tile_bits, total_bits
        self.of = list(range(total_bits))
        for level in range(tile_bits + 1, total_bits + 1):
            self.walk(level)
        held = [self.of.index(place) for place in range(total_bits)]
        self.of = held

    def swap(self, bit):
        other = self.of.index(0)
        self.of[bit], self.of[other] = 0, self.of[bit]

    def walk(self, level):
        for bit in range(level - 1, self.tile_bits - 1, -1):
            self.swap(bit)
        self.swap(0)

    def axis_distance(self, bit):
        place = self.of[bit] - self.tile_bits
        return (0, 1 << place) if place < 3 else (1, 1 << (place - 3))

    def mask(self, bit):
        axis, distance = self.axis_distance(bit)
        return (lax.broadcasted_iota(jnp.int32, (SUB, LANES), axis) & distance) != 0


def trade(low, high, upper, axis, distance):
    axis += low.ndim - 2
    size = low.shape[axis]
    return (
        jnp.where(upper, pltpu.roll(high, distance, axis=axis), low),
        jnp.where(upper, high, pltpu.roll(low, size - distance, axis=axis)),
    )


def exchange(keys, vals, a, b, down):
    if down:
        a, b = b, a
    swap = keys[a] > keys[b]
    keys[a], keys[b] = jnp.minimum(keys[a], keys[b]), jnp.maximum(keys[a], keys[b])
    vals[a], vals[b] = jnp.where(swap, vals[b], vals[a]), jnp.where(swap, vals[a], vals[b])


def sort_registers(keys, vals):
    tiles = len(keys)
    tile_bits = tiles.bit_length() - 1
    places = Places(tile_bits, tile_bits + 10)

    def flip(bit):
        return jnp.where(places.mask(bit), -1.0, 1.0)

    def trade_all(bit):
        upper, (axis, distance) = places.mask(bit), places.axis_distance(bit)
        places.swap(bit)
        for i in range(0, tiles, 2):
            keys[i], keys[i + 1] = trade(keys[i], keys[i + 1], upper, axis, distance)
            vals[i], vals[i + 1] = trade(vals[i], vals[i + 1], upper, axis, distance)

    for level in range(1, places.total_bits + 1):
        if level >= tile_bits:
            sign = 1.0
            if level > tile_bits:
                sign = flip(level - 1)
            if level < places.total_bits:
                sign = sign * flip(level)
            for i in range(tiles):
                keys[i] = keys[i] * sign
        for bit in range(level - 1, -1, -1):
            if bit >= tile_bits or (bit == 0 and level > tile_bits):
                trade_all(bit)
            step = 1 << bit if bit < tile_bits else 1
            for i in range(tiles):
                if not i & step:
                    exchange(keys, vals, i, i + step, level < tile_bits and (i >> level) & 1 == 1)
    assert places.of == list(range(places.total_bits))


def sort_kernel(
    me_ref, scan_hbm, resp_hbm, cycle_hbm, column_hbm, table_hbm, modes_hbm, *refs,
    buckets, span, rows, windows,
):
    send_refs, refs = refs[:buckets // windows], refs[buckets // windows:]
    modes_ref, refs = refs[0], refs[1:]
    scan_ref, resp_ref, cycle_ref, column_ref, table_ref, arrived = refs[:6]
    key_ref, val_ref, spec_ref, key_rows, val_rows = refs[6:]
    lines, length = scan_ref.shape
    outer = length // LANES
    loads = [
        pltpu.make_async_copy(source, place, arrived.at[i])
        for i, (source, place) in enumerate([
            (scan_hbm, scan_ref), (table_hbm, table_ref), (resp_hbm, resp_ref),
            (cycle_hbm, cycle_ref), (column_hbm, column_ref), (modes_hbm, modes_ref),
        ])
    ]
    for load in loads:
        load.start()
    def twiddle_row(k):
        at = 2 * LANES + k
        return table_ref[at:at + 1, :LANES], table_ref[at:at + 1, LANES:]

    loads[0].wait()
    re, im = small_fft([scan_ref[:, n * LANES:(n + 1) * LANES] for n in range(outer)], None, -1)
    loads[1].wait()
    forward = table_ref[:2 * LANES, :]
    for k in range(outer):
        c, s = twiddle_row(k)
        here = pl.ds(k * lines, lines)
        spec_ref[here, :LANES] = re[k] * c + im[k] * s
        spec_ref[here, LANES:] = im[k] * c - re[k] * s
    for load in loads[2:-1]:
        load.wait()
    spec = jnp.dot(spec_ref[...], forward, precision=precise, preferred_element_type=jnp.float32)
    resp = [resp_ref[:, n * LANES:(n + 1) * LANES] * (1.0 / length) for n in range(outer)]
    step = 1
    while step < outer:
        upper = (lax.broadcasted_iota(jnp.int32, (lines, LANES), 1) & step) != 0
        for n in range(outer):
            if not n & step:
                resp[n], resp[n + step] = trade(resp[n], resp[n + step], upper, 1, step)
        step *= 2
    resp = jnp.concatenate(resp, axis=0)
    spec = spec * jnp.concatenate([resp, resp], axis=1)
    spec_ref[...] = lax.dot_general(
        spec, forward, NT, precision=precise, preferred_element_type=jnp.float32
    )
    re, im = [], []
    for k in range(outer):
        c, s = twiddle_row(k)
        here = pl.ds(k * lines, lines)
        ur, ui = spec_ref[here, :LANES], spec_ref[here, LANES:]
        re.append(ur * c - ui * s)
        im.append(ui * c + ur * s)
    out, _ = small_fft(re, im, 1)
    keys = []
    for n in range(outer):
        cols = slice(n * LANES, (n + 1) * LANES)
        keys.append((cycle_ref[:, cols] * NPHI + column_ref[:, cols]).astype(jnp.float32))
    vals = list(out)
    sort_registers(keys, vals)
    row_len = outer * SUB
    last = functools.reduce(jnp.maximum, keys)
    first = functools.reduce(jnp.minimum, keys)
    last = jnp.max(last, axis=0, keepdims=True)
    first = jnp.min(first, axis=0, keepdims=True)
    for i in range(outer):
        key_ref[i * SUB:(i + 1) * SUB, :] = keys[i]
        val_ref[i * SUB:(i + 1) * SUB, :] = vals[i]
    key_rows[:LANES, :] = key_ref[...].T
    val_rows[:LANES, :] = val_ref[...].T
    reach = key_rows.shape[0] - LANES
    key_rows[LANES:, :] = jnp.full((reach, row_len), 2.0 * buckets * span, jnp.float32)
    val_rows[LANES:, :] = jnp.zeros((reach, row_len), jnp.float32)
    over = jnp.int32(0)
    for k, send_ref in enumerate(send_refs):
        for w in range(windows):
            bucket = (me_ref[0] ^ k) * windows + w
            low = (bucket * span).astype(jnp.float32)
            high = low + float(span)
            begin = jnp.sum((last < low).astype(jnp.float32)).astype(jnp.int32)
            end = jnp.sum((first < high).astype(jnp.float32)).astype(jnp.int32)
            over = over + (end - begin > rows).astype(jnp.int32)
            begin = jnp.minimum(begin, LANES)
            aligned = pl.multiple_of((begin // SUB) * SUB, SUB)
            back = lax.rem(reach - (begin - aligned), reach)
            here = pl.ds(aligned, reach)
            taken = pltpu.roll(key_rows[here, :], back, axis=0)[:rows]
            send_ref[w * rows:(w + 1) * rows, :] = taken - low
            at = (windows + w) * rows
            send_ref[at:at + rows, :] = pltpu.roll(val_rows[here, :], back, axis=0)[:rows]

    @pl.when(over > 0)
    def _():
        for send_ref in send_refs:
            send_ref[...] = jnp.full(send_ref.shape, jnp.nan, jnp.float32)

    loads[-1].wait()


def filter_and_sort(me, table, mode_table, scan, resp, cycle, column, det_count, band_cycles):
    lines, length = scan.shape
    tiles = length // LANES
    windows = WINDOWS
    buckets = det_count * windows
    span = band_cycles * NPHI // buckets
    row_len = tiles * SUB
    rows = LANES // buckets + 2
    reach = (rows + 2 * SUB - 2) // SUB * SUB
    operands = [scan, resp, cycle, column, table]
    body = functools.partial(sort_kernel, buckets=buckets, span=span, rows=rows, windows=windows)
    vmem = pl.BlockSpec(memory_space=pltpu.VMEM)
    return pl.pallas_call(
        body,
        out_shape=(jax.ShapeDtypeStruct((2 * windows * rows, row_len), jnp.float32),) * det_count
        + (jax.ShapeDtypeStruct(mode_table.shape, mode_table.dtype),),
        in_specs=[pl.BlockSpec(memory_space=pltpu.SMEM)]
        + [pl.BlockSpec(memory_space=pl.ANY)] * (len(operands) + 1),
        out_specs=(vmem,) * (det_count + 1),
        scratch_shapes=[pltpu.VMEM(x.shape, x.dtype) for x in operands] + [
            pltpu.SemaphoreType.DMA((len(operands) + 1,)),
            pltpu.VMEM((row_len, LANES), jnp.float32),
            pltpu.VMEM((row_len, LANES), jnp.float32),
            pltpu.VMEM((tiles * lines, 2 * LANES), jnp.float32),
            pltpu.VMEM((LANES + reach, row_len), jnp.float32),
            pltpu.VMEM((LANES + reach, row_len), jnp.float32),
        ],
        compiler_params=pltpu.CompilerParams(vmem_limit_bytes=24 * 1024 * 1024),
        name="filter_sort",
    )(me, *operands, mode_table)


def split2(x):
    high = x.astype(jnp.bfloat16)
    low = (x - high.astype(jnp.float32)).astype(jnp.bfloat16)
    return high, low


def bin_kernel(
    *refs, sources, windows, rows, window_cycles
):
    recv_refs, (pick_ref, table_ref, map_ref, send_ref, flag_ref) = refs[:sources], refs[sources:-6]
    recv_ref, left_a, left_b, right_a, right_b, acc_ref = refs[-6:]
    for e in range(sources):
        recv_ref[e] = recv_refs[e][...]
    left_refs, right_refs = (left_a, left_b), (right_a, right_b)
    row_len = recv_ref.shape[2]
    parts = NPHI // ROW
    area = parts * window_cycles
    a_iota = lax.broadcasted_iota(jnp.int32, (area, row_len), 0).astype(jnp.int8)
    b_iota = (lax.broadcasted_iota(jnp.int32, (ROW, row_len), 0) - ROW // 2).astype(jnp.int8)
    zero, one = jnp.zeros((), PIECE), jnp.ones((), PIECE)
    values = recv_ref[:, windows * rows:, :]
    largest = jnp.max(jnp.max(jnp.abs(values), axis=0), axis=(0, 1), keepdims=True)
    scale = jnp.where(largest > 0.0, TOP / largest, 1.0)

    def build(e, w, slot):
        left, right = left_refs[slot], right_refs[slot]
        for r in range(rows):
            q = recv_ref[e, w * rows + r:w * rows + r + 1, :].astype(jnp.int32)
            rest = recv_ref[e, (windows + w) * rows + r:(windows + w) * rows + r + 1, :] * scale
            cycle = q >> 11
            inside = (q >= 0) & (cycle < window_cycles)
            a = jnp.where(inside, ((q >> 8) & (parts - 1)) * window_cycles + cycle, -1).astype(jnp.int8)
            b = ((q & (ROW - 1)) - ROW // 2).astype(jnp.int8)
            cols = slice(r * row_len, (r + 1) * row_len)
            hit = a_iota == a
            for p in range(PIECES):
                spread = rest * KEEP
                piece = (spread - (spread - rest)).astype(PIECE)
                rest = (rest - piece.astype(jnp.float32)) * STEP
                left[p * area:(p + 1) * area, cols] = jnp.where(hit, piece, zero)
            left[PIECES * area:, cols] = jnp.where(hit, one, zero)
            right[:, cols] = jnp.where(b_iota == b, one, zero)

    def multiply(slot):
        acc_ref[...] += lax.dot_general(
            left_refs[slot][...], right_refs[slot][...], NT, preferred_element_type=jnp.float32
        )

    build(0, 0, 0)
    for w in range(windows):
        acc_ref[...] = jnp.zeros(acc_ref.shape, jnp.float32)

        def body(i, carry):
            build(2 * i + 1, w, 1)
            multiply(0)
            build(jnp.minimum(2 * i + 2, sources - 1), w, 0)
            multiply(1)
            return carry

        lax.fori_loop(0, sources // 2 - 1, body, 0)
        build(sources - 1, w, 1)
        multiply(0)
        if w + 1 < windows:
            build(0, w + 1, 0)
        multiply(1)
        acc = acc_ref[...]
        total = acc[(PIECES - 1) * area:PIECES * area]
        for p in range(PIECES - 2, -1, -1):
            total = acc[p * area:(p + 1) * area] + total * (1.0 / STEP)
        sky = total / scale / jnp.maximum(acc[PIECES * area:], 1.0)
        for c8 in range(parts):
            map_ref[w * window_cycles:(w + 1) * window_cycles, c8 * ROW:(c8 + 1) * ROW] = (
                sky[c8 * window_cycles:(c8 + 1) * window_cycles]
            )
    cycles = map_ref.shape[0]
    half = NPHI // 2
    modes = []
    for parity in (0, 1):
        a, b = map_ref[:, :half], map_ref[:, half:]
        high, low = split2(a + b if parity == 0 else a - b)
        first = jnp.dot(jnp.concatenate([high, low], axis=0), table_ref[0, parity], preferred_element_type=jnp.float32)
        second = jnp.dot(high, table_ref[1, parity], preferred_element_type=jnp.float32)
        modes.append(first[:cycles] + first[cycles:] + second)
    modes = jnp.concatenate(modes, axis=1)
    count = modes.shape[1]
    width = pick_ref.shape[1]
    high = modes.astype(jnp.bfloat16)
    rest = modes - high.astype(jnp.float32)
    middle = rest.astype(jnp.bfloat16)
    low = (rest - middle.astype(jnp.float32)).astype(jnp.bfloat16)
    pieces = jnp.concatenate([high, middle, low], axis=0)
    choose = (lax.broadcasted_iota(jnp.int32, (count, width), 0) == pick_ref[...])
    choose = jnp.where(choose, 1.0, 0.0).astype(jnp.bfloat16)
    moved = jnp.dot(pieces, choose, preferred_element_type=jnp.float32)
    moved = moved[:cycles] + moved[cycles:2 * cycles] + moved[2 * cycles:]
    owners, group_rows, lanes = send_ref.shape
    groups = cycles // group_rows
    lane_group = lax.broadcasted_iota(jnp.int32, (group_rows, lanes), 1) // (lanes // groups)
    flag_ref[0] = (jnp.max(jnp.where(values == values, 0.0, 1.0)) > 0.0).astype(jnp.int32)
    for d in range(owners):
        block = moved[:, d * lanes:(d + 1) * lanes]
        out = block[:group_rows]
        for h in range(1, groups):
            out = jnp.where(lane_group == h, block[h * group_rows:(h + 1) * group_rows], out)
        send_ref[d] = out


def bin_and_modes(mode_table, recv, order_slot, band_cycles):
    sources = len(recv)
    lines, row_len = recv[0].shape
    windows = WINDOWS
    rows = lines // (2 * windows)
    cycles = band_cycles // sources
    count = order_slot.shape[0]
    slots = count // sources
    groups = LANES // (2 * slots)
    m = order_slot.reshape(sources, 1, 1, slots)
    part = jnp.arange(2, dtype=jnp.int32).reshape(1, 1, 2, 1)
    pick = (m & 1) * count + part * (count // 2) + (m >> 1)
    pick = jnp.broadcast_to(pick, (sources, groups, 2, slots)).reshape(1, sources * LANES)
    area = cycles // windows * (NPHI // ROW)
    depth = rows * row_len
    vmem = pl.BlockSpec(memory_space=pltpu.VMEM)
    return pl.pallas_call(
        functools.partial(bin_kernel, sources=sources, windows=windows, rows=rows, window_cycles=cycles // windows),
        out_shape=(
            jax.ShapeDtypeStruct((cycles, NPHI), jnp.float32),
            jax.ShapeDtypeStruct((sources, cycles // groups, LANES), jnp.float32),
            jax.ShapeDtypeStruct((1,), jnp.int32),
        ),
        in_specs=[vmem] * (sources + 2),
        out_specs=(vmem, vmem, pl.BlockSpec(memory_space=pltpu.SMEM)),
        scratch_shapes=[
            pltpu.VMEM((sources, lines, row_len), jnp.float32),
            pltpu.VMEM(((PIECES + 1) * area, depth), PIECE),
            pltpu.VMEM(((PIECES + 1) * area, depth), PIECE),
            pltpu.VMEM((ROW, depth), PIECE),
            pltpu.VMEM((ROW, depth), PIECE),
            pltpu.VMEM(((PIECES + 1) * area, ROW), jnp.float32),
        ],
        compiler_params=pltpu.CompilerParams(vmem_limit_bytes=40 * 1024 * 1024),
        name="bin_modes",
    )(*recv, pick, mode_table)


def legendre_kernel(me_ref, order_ref, recv_ref, table_ref, *refs, owners):
    out_refs, (leg_ref, arrived, modes_ref, wide_ref, sums_ref) = refs[:owners], refs[owners:]
    slots, band_cycles, degrees = table_ref.shape

    def load(slot, act):
        skip = order_ref[slot] >= LANES

        @pl.when(skip)
        def _():
            upper = pl.ds(LANES, degrees - LANES)
            act(pltpu.make_async_copy(
                table_ref.at[slot, :, upper], leg_ref.at[slot, :, upper], arrived.at[slot]
            ))

        @pl.when(jnp.logical_not(skip))
        def _():
            act(pltpu.make_async_copy(table_ref.at[slot], leg_ref.at[slot], arrived.at[slot]))

    def start(slot, carry):
        load(slot, lambda copy: copy.start())
        return carry

    lax.fori_loop(0, slots, start, 0)
    sources, group_rows, lanes = recv_ref.shape
    groups = lanes // (2 * slots)
    width = out_refs[0].shape[1]
    tiles = degrees // LANES
    for e in range(sources):
        block = recv_ref[e]
        for h in range(groups):
            at = (e * groups + h) * group_rows
            turned = block if h == 0 else pltpu.roll(block, lanes - h * 2 * slots, axis=1)
            modes_ref[at:at + group_rows, :] = turned

    def widen(slot, half):
        turned = pltpu.roll(modes_ref[...], lax.rem(lanes - slot, lanes), axis=1)
        for c in range(2):
            column = turned[:, c * slots:c * slots + 1]
            wide_ref[half, c] = jnp.broadcast_to(column, (band_cycles, lanes))

    widen(0, 0)

    def body(slot, carry):
        half = slot & 1
        load(slot, lambda copy: copy.wait())
        sums = [[jnp.zeros((SUB, LANES), jnp.float32) for _ in range(tiles)] for _ in range(2)]
        for r in range(0, band_cycles, SUB):
            factor = [wide_ref[half, c, r:r + SUB, :] for c in range(2)]
            for t in range(tiles):
                block = leg_ref[slot, r:r + SUB, t * LANES:(t + 1) * LANES]
                for c in range(2):
                    sums[c][t] = sums[c][t] + block * factor[c]
        widen(jnp.minimum(slot + 1, slots - 1), 1 - half)
        per_owner = width // LANES
        for c in range(2):
            lines = [jnp.sum(part, axis=0, keepdims=True) for part in sums[c]]
            for d in range(owners):
                line = jnp.concatenate(lines[d * per_owner:(d + 1) * per_owner], axis=1)
                sums_ref[d, pl.ds(c * slots + slot, 1), :] = line
        return carry

    lax.fori_loop(0, slots, body, 0)
    for k in range(owners):
        out_refs[k][...] = sums_ref[me_ref[0] ^ k]


def legendre_sums(me, orders, recv, legendre, owners):
    slots, band_cycles, degrees = legendre.shape
    vmem = pl.BlockSpec(memory_space=pltpu.VMEM)
    return pl.pallas_call(
        functools.partial(legendre_kernel, owners=owners),
        out_shape=(jax.ShapeDtypeStruct((2 * slots, degrees // owners), jnp.float32),) * owners,
        in_specs=[pl.BlockSpec(memory_space=pltpu.SMEM)] * 2 + [vmem, pl.BlockSpec(memory_space=pl.ANY)],
        out_specs=(vmem,) * owners,
        scratch_shapes=[
            pltpu.VMEM(legendre.shape, jnp.float32),
            pltpu.SemaphoreType.DMA((slots,)),
            pltpu.VMEM((band_cycles, LANES), jnp.float32),
            pltpu.VMEM((2, 2, band_cycles, LANES), jnp.float32),
            pltpu.VMEM((owners, 2 * slots, degrees // owners), jnp.float32),
        ],
        compiler_params=pltpu.CompilerParams(vmem_limit_bytes=44 * 1024 * 1024),
        name="legendre_sums",
    )(me, orders, recv, legendre)


def exchange_and_sum(x, axis, count):
    parts = x.reshape(count, x.shape[0] // count, x.shape[1])
    return jnp.sum(lax.all_to_all(parts, axis, split_axis=0, concat_axis=0, tiled=True), axis=0)


def dense_filter(table, scan, resp):
    lines, length = scan.shape
    outer = length // LANES
    forward = table[:2 * LANES]
    c, s = table[2 * LANES:, :LANES], table[2 * LANES:, LANES:]
    k = jnp.arange(outer, dtype=jnp.int32)
    angle = 2.0 * jnp.pi / outer * (k[:, None] * k[None, :] % outer).astype(jnp.float32)
    x = scan.reshape(lines, outer, LANES)
    re = jnp.einsum("lna,nk->lka", x, jnp.cos(angle), precision=precise)
    im = -jnp.einsum("lna,nk->lka", x, jnp.sin(angle), precision=precise)
    spec = jnp.concatenate([re * c + im * s, im * c - re * s], axis=-1)
    spec = jnp.einsum("lki,ij->lkj", spec, forward, precision=precise)
    split = LANES // outer
    weight = resp.reshape(lines, outer, split, outer).transpose(0, 3, 2, 1).reshape(lines, outer, LANES)
    spec = spec * jnp.concatenate([weight, weight], axis=-1)
    spec = jnp.einsum("lki,ji->lkj", spec, forward, precision=precise)
    ur, ui = spec[..., :LANES], spec[..., LANES:]
    out = jnp.einsum("lka,kn->lna", ur * c - ui * s, jnp.cos(angle), precision=precise)
    out = out - jnp.einsum("lka,kn->lna", ui * c + ur * s, jnp.sin(angle), precision=precise)
    return (out / length).reshape(lines, length)


def dense_path(table, mode_table, scan_lines, response, cycle_offset, column, order_slot, band_cycles, det_count):
    filtered = dense_filter(table, scan_lines, response)
    flat_index = (cycle_offset * NPHI + column).reshape(-1)
    empty = jnp.zeros((band_cycles * NPHI,), jnp.float32)
    partial_value = empty.at[flat_index].add(filtered.reshape(-1)).reshape(band_cycles, NPHI)
    counts = empty.at[flat_index].add(1.0).reshape(band_cycles, NPHI)
    summed = exchange_and_sum(partial_value, "det", det_count)
    hit_total = exchange_and_sum(counts, "det", det_count)
    sky_map = summed / jnp.maximum(hit_total, 1.0)
    count, half = order_slot.shape[0], NPHI // 2
    tables = jnp.sum(mode_table.astype(jnp.float32), axis=0)
    first, second = sky_map[:, :half], sky_map[:, half:]
    modes = jnp.concatenate([
        jnp.dot(first + second, tables[0], precision=precise),
        jnp.dot(first - second, tables[1], precision=precise),
    ], axis=1)
    part = jnp.arange(2, dtype=jnp.int32)[:, None] * (count // 2)
    modes = modes[:, (order_slot & 1) * count + part + (order_slot >> 1)].transpose(1, 0, 2)
    slots = order_slot.shape[0] // det_count
    groups = LANES // (2 * slots)
    blocks = modes.reshape(2, groups, -1, det_count, slots).transpose(3, 2, 1, 0, 4)
    blocks = blocks.reshape(det_count, -1, LANES)
    return sky_map, lax.all_to_all(blocks, "det", split_axis=0, concat_axis=0, tiled=True)


def swap_blocks(blocks, axis):
    count = len(blocks)
    out = list(blocks)
    for k in range(count - 1, 0, -1):
        out[k] = lax.ppermute(blocks[k], axis, [(i, i ^ k) for i in range(count)])
    return out


def local(scan_lines, response, cycle_offset, column, order_slot, legendre, *, det_count, band_count):
    slots, band_cycles, degrees = legendre.shape
    me = lax.axis_index("det").astype(jnp.int32).reshape(1)
    table = jnp.asarray(filter_tables(scan_lines.shape[1]))
    mode_table = jnp.asarray(mode_tables(order_slot.shape[0]))
    *send, mode_copy = filter_and_sort(
        me, table, mode_table, scan_lines, response, cycle_offset, column, det_count, band_cycles
    )
    recv = swap_blocks(send, "det")
    sky_map, modes, crowded = bin_and_modes(mode_copy, recv[::-1], order_slot, band_cycles)
    modes = lax.all_to_all(modes, "det", split_axis=0, concat_axis=0, tiled=True)
    sky_map, modes = lax.cond(
        crowded[0] > 0,
        lambda: dense_path(
            table, mode_table, scan_lines, response, cycle_offset, column, order_slot, band_cycles, det_count
        ),
        lambda: (sky_map, modes),
    )
    band = lax.axis_index("band").astype(jnp.int32)
    local_orders = lax.dynamic_slice_in_dim(order_slot, lax.axis_index("det") * slots, slots, 0)
    terms = swap_blocks(legendre_sums(band.reshape(1), local_orders, modes, legendre, band_count), "band")
    sums = functools.reduce(jnp.add, terms[::-1])
    width = degrees // band_count
    degree = band * width + jnp.arange(width, dtype=jnp.int32)
    keep = degree[None, None, :] >= local_orders[None, :, None]
    return jnp.where(keep, sums.reshape(2, slots, width), 0.0), sky_map


def solution(mesh):
    sizes = dict(mesh.shape)
    return jax.shard_map(
        functools.partial(local, det_count=sizes["det"], band_count=sizes["band"]),
        mesh=mesh,
        in_specs=(
            P(("det", "band"), None),
            P(("det", "band"), None),
            P(("det", "band"), None),
            P(("det", "band"), None),
            P(),
            P("det", "band", None),
        ),
        out_specs=(P(None, "det", "band"), P(("band", "det"), None)),
        check_vma=False,
    )
```

```python
import functools

import jax
import jax.numpy as jnp
import numpy as np
from jax import lax
from jax.experimental import pallas as pl
from jax.experimental.pallas import tpu as pltpu
from jax.sharding import PartitionSpec as P

NPHI = 2048
LANES = 128
SUB = 8
WINDOWS = 2
HEAD = 2
ROW = 256
PIECE, PIECES, STEP, TOP = jnp.float8_e4m3fn, 3, 32.0, 224.0
KEEP = 2.0**20 + 1.0

precise = lax.Precision.HIGHEST
NT = (((1,), (1,)), ((), ()))


def filter_tables(length):
    outer = length // LANES
    k1 = np.arange(outer)[:, None]
    n2 = np.arange(LANES)[None, :]
    turn = 2.0 * np.pi * ((k1 * n2) % length) / length
    twiddle = np.concatenate([np.cos(turn), np.sin(turn)], axis=1)
    a = np.arange(LANES)
    angle = 2.0 * np.pi * (np.outer(a, a) % LANES) / LANES
    c, s = np.cos(angle), np.sin(angle)
    order = (a % outer) * (LANES // outer) + a // outer
    c, s = c[:, order], s[:, order]
    forward = np.block([[c, -s], [s, c]])
    return np.concatenate([forward, twiddle]).astype(np.float32)


def mode_tables(count):
    half = NPHI // 2
    p = np.arange(half)[:, None]
    out = []
    for parity in (0, 1):
        m = 2 * np.arange(count // 2)[None, :] + parity
        angle = 2.0 * np.pi * ((p * m) % NPHI) / NPHI
        out.append(np.concatenate([np.cos(angle), -np.sin(angle)], axis=1))
    table = np.stack(out).astype(np.float32)
    high = table.astype(jnp.bfloat16)
    low = (table - high.astype(np.float32)).astype(jnp.bfloat16)
    return np.stack([high, low])


def small_fft(re, im, sign):
    count = len(re)
    if count == 1:
        return re, im
    even_re, even_im = small_fft(re[0::2], None if im is None else im[0::2], sign)
    odd_re, odd_im = small_fft(re[1::2], None if im is None else im[1::2], sign)
    half = count // 2
    out_re, out_im = [None] * count, [None] * count
    for k in range(half):
        wr = float(np.cos(2 * np.pi * k / count))
        wi = float(sign * np.sin(2 * np.pi * k / count))
        er, ei, orr, oi = even_re[k], even_im and even_im[k], odd_re[k], odd_im and odd_im[k]
        if k == 0:
            tr, ti = orr, oi
        elif 4 * k == count:
            tr = None if oi is None else -wi * oi
            ti = wi * orr
        elif oi is None:
            tr, ti = wr * orr, wi * orr
        else:
            tr, ti = wr * orr - wi * oi, wr * oi + wi * orr
        out_re[k] = er if tr is None else er + tr
        out_re[k + half] = er if tr is None else er - tr
        if ti is None:
            out_im[k] = out_im[k + half] = ei
        else:
            out_im[k] = ti if ei is None else ei + ti
            out_im[k + half] = -ti if ei is None else ei - ti
    if all(x is None for x in out_im):
        return out_re, None
    out_im = [jnp.zeros_like(out_re[0]) if x is None else x for x in out_im]
    return out_re, out_im


class Places:
    def __init__(self, tile_bits, total_bits):
        self.tile_bits, self.total_bits = tile_bits, total_bits
        self.of = list(range(total_bits))
        for level in range(tile_bits + 1, total_bits + 1):
            self.walk(level)
        held = [self.of.index(place) for place in range(total_bits)]
        self.of = held

    def swap(self, bit):
        other = self.of.index(0)
        self.of[bit], self.of[other] = 0, self.of[bit]

    def walk(self, level):
        for bit in range(level - 1, self.tile_bits - 1, -1):
            self.swap(bit)
        self.swap(0)

    def axis_distance(self, bit):
        place = self.of[bit] - self.tile_bits
        return (0, 1 << place) if place < 3 else (1, 1 << (place - 3))

    def mask(self, bit):
        axis, distance = self.axis_distance(bit)
        return (lax.broadcasted_iota(jnp.int32, (SUB, LANES), axis) & distance) != 0


def trade(low, high, upper, axis, distance):
    axis += low.ndim - 2
    size = low.shape[axis]
    return (
        jnp.where(upper, pltpu.roll(high, distance, axis=axis), low),
        jnp.where(upper, high, pltpu.roll(low, size - distance, axis=axis)),
    )


def exchange(keys, vals, a, b, down):
    if down:
        a, b = b, a
    swap = keys[a] > keys[b]
    keys[a], keys[b] = jnp.minimum(keys[a], keys[b]), jnp.maximum(keys[a], keys[b])
    vals[a], vals[b] = jnp.where(swap, vals[b], vals[a]), jnp.where(swap, vals[a], vals[b])


def sort_registers(keys, vals):
    tiles = len(keys)
    tile_bits = tiles.bit_length() - 1
    places = Places(tile_bits, tile_bits + 10)

    def flip(bit):
        return jnp.where(places.mask(bit), -1.0, 1.0)

    def trade_all(bit):
        upper, (axis, distance) = places.mask(bit), places.axis_distance(bit)
        places.swap(bit)
        for i in range(0, tiles, 2):
            keys[i], keys[i + 1] = trade(keys[i], keys[i + 1], upper, axis, distance)
            vals[i], vals[i + 1] = trade(vals[i], vals[i + 1], upper, axis, distance)

    for level in range(1, places.total_bits + 1):
        if level >= tile_bits:
            sign = 1.0
            if level > tile_bits:
                sign = flip(level - 1)
            if level < places.total_bits:
                sign = sign * flip(level)
            for i in range(tiles):
                keys[i] = keys[i] * sign
        for bit in range(level - 1, -1, -1):
            if bit >= tile_bits or (bit == 0 and level > tile_bits):
                trade_all(bit)
            step = 1 << bit if bit < tile_bits else 1
            for i in range(tiles):
                if not i & step:
                    exchange(keys, vals, i, i + step, level < tile_bits and (i >> level) & 1 == 1)
    assert places.of == list(range(places.total_bits))


def split2(x):
    high = x.astype(jnp.bfloat16)
    low = (x - high.astype(jnp.float32)).astype(jnp.bfloat16)
    return high, low


def three_products(left, right, dims):
    dot = functools.partial(lax.dot_general, dimension_numbers=dims, preferred_element_type=jnp.float32)
    return dot(left[0], right[0]) + (dot(left[1], right[0]) + dot(left[0], right[1]))


def sort_kernel(
    me_ref, scan_hbm, resp_hbm, cycle_hbm, column_hbm, table_hbm, modes_hbm, *refs,
    buckets, span, rows, windows,
):
    send_refs, refs = refs[:buckets // windows], refs[buckets // windows:]
    modes_ref, refs = refs[0], refs[1:]
    scan_ref, resp_ref, cycle_ref, column_ref, table_ref, arrived = refs[:6]
    key_ref, val_ref, spec_ref, key_rows, val_rows = refs[6:]
    lines, length = scan_ref.shape
    outer = length // LANES
    loads = [
        pltpu.make_async_copy(source, place, arrived.at[i])
        for i, (source, place) in enumerate([
            (scan_hbm, scan_ref), (table_hbm, table_ref), (resp_hbm, resp_ref),
            (cycle_hbm, cycle_ref), (column_hbm, column_ref), (modes_hbm, modes_ref),
        ])
    ]
    for load in loads:
        load.start()
    def twiddle_row(k):
        at = 2 * LANES + k
        return table_ref[at:at + 1, :LANES], table_ref[at:at + 1, LANES:]

    loads[0].wait()
    re, im = small_fft([scan_ref[:, n * LANES:(n + 1) * LANES] for n in range(outer)], None, -1)
    loads[1].wait()
    forward = table_ref[:2 * LANES, :]
    for k in range(outer):
        c, s = twiddle_row(k)
        here = pl.ds(k * lines, lines)
        spec_ref[here, :LANES] = re[k] * c + im[k] * s
        spec_ref[here, LANES:] = im[k] * c - re[k] * s
    for load in loads[2:-1]:
        load.wait()
    forward_pieces = split2(forward)
    spec = three_products(split2(spec_ref[...]), forward_pieces, (((1,), (0,)), ((), ())))
    resp = [resp_ref[:, n * LANES:(n + 1) * LANES] * (1.0 / length) for n in range(outer)]
    step = 1
    while step < outer:
        upper = (lax.broadcasted_iota(jnp.int32, (lines, LANES), 1) & step) != 0
        for n in range(outer):
            if not n & step:
                resp[n], resp[n + step] = trade(resp[n], resp[n + step], upper, 1, step)
        step *= 2
    resp = jnp.concatenate(resp, axis=0)
    spec = spec * jnp.concatenate([resp, resp], axis=1)
    spec_ref[...] = three_products(split2(spec), forward_pieces, NT)
    re, im = [], []
    for k in range(outer):
        c, s = twiddle_row(k)
        here = pl.ds(k * lines, lines)
        ur, ui = spec_ref[here, :LANES], spec_ref[here, LANES:]
        re.append(ur * c - ui * s)
        im.append(ui * c + ur * s)
    out, _ = small_fft(re, im, 1)
    keys = []
    for n in range(outer):
        cols = slice(n * LANES, (n + 1) * LANES)
        keys.append((cycle_ref[:, cols] * NPHI + column_ref[:, cols]).astype(jnp.float32))
    vals = list(out)
    sort_registers(keys, vals)
    row_len = outer * SUB
    last = functools.reduce(jnp.maximum, keys)
    first = functools.reduce(jnp.minimum, keys)
    last = jnp.max(last, axis=0, keepdims=True)
    first = jnp.min(first, axis=0, keepdims=True)
    for i in range(outer):
        key_ref[i * SUB:(i + 1) * SUB, :] = keys[i]
        val_ref[i * SUB:(i + 1) * SUB, :] = vals[i]
    key_rows[:LANES, :] = key_ref[...].T
    val_rows[:LANES, :] = val_ref[...].T
    reach = key_rows.shape[0] - LANES
    key_rows[LANES:, :] = jnp.full((reach, row_len), 2.0 * buckets * span, jnp.float32)
    val_rows[LANES:, :] = jnp.zeros((reach, row_len), jnp.float32)
    over = jnp.int32(0)
    for k, send_ref in enumerate(send_refs):
        for w in range(windows):
            bucket = (me_ref[0] ^ k) * windows + w
            low = (bucket * span).astype(jnp.float32)
            high = low + float(span)
            begin = jnp.sum((last < low).astype(jnp.float32)).astype(jnp.int32)
            end = jnp.sum((first < high).astype(jnp.float32)).astype(jnp.int32)
            over = over + (end - begin > rows).astype(jnp.int32)
            begin = jnp.minimum(begin, LANES)
            aligned = pl.multiple_of((begin // SUB) * SUB, SUB)
            back = lax.rem(reach - (begin - aligned), reach)
            here = pl.ds(aligned, reach)
            taken = pltpu.roll(key_rows[here, :], back, axis=0)[:rows]
            send_ref[w * rows:(w + 1) * rows, :] = taken - low
            at = (windows + w) * rows
            send_ref[at:at + rows, :] = pltpu.roll(val_rows[here, :], back, axis=0)[:rows]

    @pl.when(over > 0)
    def _():
        for send_ref in send_refs:
            send_ref[...] = jnp.full(send_ref.shape, jnp.nan, jnp.float32)

    loads[-1].wait()


def filter_and_sort(me, table, mode_table, scan, resp, cycle, column, det_count, band_cycles):
    lines, length = scan.shape
    tiles = length // LANES
    windows = WINDOWS
    buckets = det_count * windows
    span = band_cycles * NPHI // buckets
    row_len = tiles * SUB
    rows = LANES // buckets + 2
    reach = (rows + 2 * SUB - 2) // SUB * SUB
    operands = [scan, resp, cycle, column, table]
    body = functools.partial(sort_kernel, buckets=buckets, span=span, rows=rows, windows=windows)
    vmem = pl.BlockSpec(memory_space=pltpu.VMEM)
    return pl.pallas_call(
        body,
        out_shape=(jax.ShapeDtypeStruct((2 * windows * rows, row_len), jnp.float32),) * det_count
        + (jax.ShapeDtypeStruct(mode_table.shape, mode_table.dtype),),
        in_specs=[pl.BlockSpec(memory_space=pltpu.SMEM)]
        + [pl.BlockSpec(memory_space=pl.ANY)] * (len(operands) + 1),
        out_specs=(vmem,) * (det_count + 1),
        scratch_shapes=[pltpu.VMEM(x.shape, x.dtype) for x in operands] + [
            pltpu.SemaphoreType.DMA((len(operands) + 1,)),
            pltpu.VMEM((row_len, LANES), jnp.float32),
            pltpu.VMEM((row_len, LANES), jnp.float32),
            pltpu.VMEM((tiles * lines, 2 * LANES), jnp.float32),
            pltpu.VMEM((LANES + reach, row_len), jnp.float32),
            pltpu.VMEM((LANES + reach, row_len), jnp.float32),
        ],
        compiler_params=pltpu.CompilerParams(vmem_limit_bytes=24 * 1024 * 1024),
        name="filter_sort",
    )(me, *operands, mode_table)


def bin_kernel(
    *refs, sources, windows, rows, window_cycles
):
    recv_refs, (pick_ref, table_ref, leg_hbm, map_ref, send_ref, flag_ref, head_ref) = (
        refs[:sources], refs[sources:-7]
    )
    recv_ref, left_a, left_b, right_a, right_b, acc_ref, arrived = refs[-7:]
    head_load = pltpu.make_async_copy(leg_hbm.at[pl.ds(0, head_ref.shape[0])], head_ref, arrived)
    head_load.start()
    for e in range(sources):
        recv_ref[e] = recv_refs[e][...]
    left_refs, right_refs = (left_a, left_b), (right_a, right_b)
    row_len = recv_ref.shape[2]
    parts = NPHI // ROW
    area = parts * window_cycles
    a_iota = lax.broadcasted_iota(jnp.int32, (area, row_len), 0).astype(jnp.int8)
    b_iota = (lax.broadcasted_iota(jnp.int32, (ROW, row_len), 0) - ROW // 2).astype(jnp.int8)
    zero, one = jnp.zeros((), PIECE), jnp.ones((), PIECE)
    values = recv_ref[:, windows * rows:, :]
    largest = jnp.max(jnp.max(jnp.abs(values), axis=0), axis=(0, 1), keepdims=True)
    scale = jnp.where(largest > 0.0, TOP / largest, 1.0)

    def build(e, w, slot):
        left, right = left_refs[slot], right_refs[slot]
        for r in range(rows):
            q = recv_ref[e, w * rows + r:w * rows + r + 1, :].astype(jnp.int32)
            rest = recv_ref[e, (windows + w) * rows + r:(windows + w) * rows + r + 1, :] * scale
            cycle = q >> 11
            inside = (q >= 0) & (cycle < window_cycles)
            a = jnp.where(inside, ((q >> 8) & (parts - 1)) * window_cycles + cycle, -1).astype(jnp.int8)
            b = ((q & (ROW - 1)) - ROW // 2).astype(jnp.int8)
            cols = slice(r * row_len, (r + 1) * row_len)
            hit = a_iota == a
            for p in range(PIECES):
                spread = rest * KEEP
                piece = (spread - (spread - rest)).astype(PIECE)
                rest = (rest - piece.astype(jnp.float32)) * STEP
                left[p * area:(p + 1) * area, cols] = jnp.where(hit, piece, zero)
            left[PIECES * area:, cols] = jnp.where(hit, one, zero)
            right[:, cols] = jnp.where(b_iota == b, one, zero)

    def multiply(slot):
        acc_ref[...] += lax.dot_general(
            left_refs[slot][...], right_refs[slot][...], NT, preferred_element_type=jnp.float32
        )

    build(0, 0, 0)
    for w in range(windows):
        acc_ref[...] = jnp.zeros(acc_ref.shape, jnp.float32)

        def body(i, carry):
            build(2 * i + 1, w, 1)
            multiply(0)
            build(jnp.minimum(2 * i + 2, sources - 1), w, 0)
            multiply(1)
            return carry

        lax.fori_loop(0, sources // 2 - 1, body, 0)
        build(sources - 1, w, 1)
        multiply(0)
        if w + 1 < windows:
            build(0, w + 1, 0)
        multiply(1)
        acc = acc_ref[...]
        total = acc[(PIECES - 1) * area:PIECES * area]
        for p in range(PIECES - 2, -1, -1):
            total = acc[p * area:(p + 1) * area] + total * (1.0 / STEP)
        sky = total / scale / jnp.maximum(acc[PIECES * area:], 1.0)
        for c8 in range(parts):
            map_ref[w * window_cycles:(w + 1) * window_cycles, c8 * ROW:(c8 + 1) * ROW] = (
                sky[c8 * window_cycles:(c8 + 1) * window_cycles]
            )
    cycles = map_ref.shape[0]
    half = NPHI // 2
    modes = []
    for parity in (0, 1):
        a, b = map_ref[:, :half], map_ref[:, half:]
        high, low = split2(a + b if parity == 0 else a - b)
        first = jnp.dot(jnp.concatenate([high, low], axis=0), table_ref[0, parity], preferred_element_type=jnp.float32)
        second = jnp.dot(high, table_ref[1, parity], preferred_element_type=jnp.float32)
        modes.append(first[:cycles] + first[cycles:] + second)
    modes = jnp.concatenate(modes, axis=1)
    count = modes.shape[1]
    width = pick_ref.shape[1]
    high = modes.astype(jnp.bfloat16)
    rest = modes - high.astype(jnp.float32)
    middle = rest.astype(jnp.bfloat16)
    low = (rest - middle.astype(jnp.float32)).astype(jnp.bfloat16)
    pieces = jnp.concatenate([high, middle, low], axis=0)
    choose = (lax.broadcasted_iota(jnp.int32, (count, width), 0) == pick_ref[...])
    choose = jnp.where(choose, 1.0, 0.0).astype(jnp.bfloat16)
    moved = jnp.dot(pieces, choose, preferred_element_type=jnp.float32)
    moved = moved[:cycles] + moved[cycles:2 * cycles] + moved[2 * cycles:]
    owners, group_rows, lanes = send_ref.shape
    groups = cycles // group_rows
    lane_group = lax.broadcasted_iota(jnp.int32, (group_rows, lanes), 1) // (lanes // groups)
    flag_ref[0] = (jnp.max(jnp.where(values == values, 0.0, 1.0)) > 0.0).astype(jnp.int32)
    for d in range(owners):
        block = moved[:, d * lanes:(d + 1) * lanes]
        out = block[:group_rows]
        for h in range(1, groups):
            out = jnp.where(lane_group == h, block[h * group_rows:(h + 1) * group_rows], out)
        send_ref[d] = out
    head_load.wait()


def bin_and_modes(mode_table, legendre, recv, order_slot, band_cycles):
    sources = len(recv)
    lines, row_len = recv[0].shape
    windows = WINDOWS
    rows = lines // (2 * windows)
    cycles = band_cycles // sources
    count = order_slot.shape[0]
    slots = count // sources
    groups = LANES // (2 * slots)
    m = order_slot.reshape(sources, 1, 1, slots)
    part = jnp.arange(2, dtype=jnp.int32).reshape(1, 1, 2, 1)
    pick = (m & 1) * count + part * (count // 2) + (m >> 1)
    pick = jnp.broadcast_to(pick, (sources, groups, 2, slots)).reshape(1, sources * LANES)
    area = cycles // windows * (NPHI // ROW)
    depth = rows * row_len
    vmem = pl.BlockSpec(memory_space=pltpu.VMEM)
    return pl.pallas_call(
        functools.partial(bin_kernel, sources=sources, windows=windows, rows=rows, window_cycles=cycles // windows),
        out_shape=(
            jax.ShapeDtypeStruct((cycles, NPHI), jnp.float32),
            jax.ShapeDtypeStruct((sources, cycles // groups, LANES), jnp.float32),
            jax.ShapeDtypeStruct((1,), jnp.int32),
            jax.ShapeDtypeStruct((HEAD,) + legendre.shape[1:], jnp.float32),
        ),
        in_specs=[vmem] * (sources + 2) + [pl.BlockSpec(memory_space=pl.ANY)],
        out_specs=(vmem, vmem, pl.BlockSpec(memory_space=pltpu.SMEM), vmem),
        scratch_shapes=[
            pltpu.VMEM((sources, lines, row_len), jnp.float32),
            pltpu.VMEM(((PIECES + 1) * area, depth), PIECE),
            pltpu.VMEM(((PIECES + 1) * area, depth), PIECE),
            pltpu.VMEM((ROW, depth), PIECE),
            pltpu.VMEM((ROW, depth), PIECE),
            pltpu.VMEM(((PIECES + 1) * area, ROW), jnp.float32),
            pltpu.SemaphoreType.DMA,
        ],
        compiler_params=pltpu.CompilerParams(vmem_limit_bytes=40 * 1024 * 1024),
        name="bin_modes",
    )(*recv, pick, mode_table, legendre)


def legendre_kernel(me_ref, order_ref, recv_ref, head_ref, table_ref, *refs, owners):
    out_refs, (leg_ref, arrived, modes_ref, wide_ref, sums_ref) = refs[:owners], refs[owners:]
    slots, band_cycles, degrees = table_ref.shape

    def load(slot, act):
        skip = order_ref[slot] >= LANES

        @pl.when(skip)
        def _():
            upper = pl.ds(LANES, degrees - LANES)
            act(pltpu.make_async_copy(
                table_ref.at[slot, :, upper], leg_ref.at[slot, :, upper], arrived.at[slot]
            ))

        @pl.when(jnp.logical_not(skip))
        def _():
            act(pltpu.make_async_copy(table_ref.at[slot], leg_ref.at[slot], arrived.at[slot]))

    def start(slot, carry):
        load(slot, lambda copy: copy.start())
        return carry

    lax.fori_loop(HEAD, slots, start, 0)
    sources, group_rows, lanes = recv_ref.shape
    groups = lanes // (2 * slots)
    width = out_refs[0].shape[1]
    tiles = degrees // LANES
    for e in range(sources):
        block = recv_ref[e]
        for h in range(groups):
            at = (e * groups + h) * group_rows
            turned = block if h == 0 else pltpu.roll(block, lanes - h * 2 * slots, axis=1)
            modes_ref[at:at + group_rows, :] = turned

    def widen(slot, half):
        turned = pltpu.roll(modes_ref[...], lax.rem(lanes - slot, lanes), axis=1)
        for c in range(2):
            column = turned[:, c * slots:c * slots + 1]
            wide_ref[half, c] = jnp.broadcast_to(column, (band_cycles, lanes))

    widen(0, 0)

    def body(source_ref, slot, carry):
        half = slot & 1
        if source_ref is leg_ref:
            load(slot, lambda copy: copy.wait())
        sums = [[jnp.zeros((SUB, LANES), jnp.float32) for _ in range(tiles)] for _ in range(2)]
        for r in range(0, band_cycles, SUB):
            factor = [wide_ref[half, c, r:r + SUB, :] for c in range(2)]
            for t in range(tiles):
                block = source_ref[slot, r:r + SUB, t * LANES:(t + 1) * LANES]
                for c in range(2):
                    sums[c][t] = sums[c][t] + block * factor[c]
        widen(jnp.minimum(slot + 1, slots - 1), 1 - half)
        per_owner = width // LANES
        for c in range(2):
            lines = [jnp.sum(part, axis=0, keepdims=True) for part in sums[c]]
            for d in range(owners):
                line = jnp.concatenate(lines[d * per_owner:(d + 1) * per_owner], axis=1)
                sums_ref[d, pl.ds(c * slots + slot, 1), :] = line
        return carry

    lax.fori_loop(0, HEAD, functools.partial(body, head_ref), 0)
    lax.fori_loop(HEAD, slots, functools.partial(body, leg_ref), 0)
    for k in range(owners):
        out_refs[k][...] = sums_ref[me_ref[0] ^ k]


def legendre_sums(me, orders, recv, head, legendre, owners):
    slots, band_cycles, degrees = legendre.shape
    vmem = pl.BlockSpec(memory_space=pltpu.VMEM)
    return pl.pallas_call(
        functools.partial(legendre_kernel, owners=owners),
        out_shape=(jax.ShapeDtypeStruct((2 * slots, degrees // owners), jnp.float32),) * owners,
        in_specs=[pl.BlockSpec(memory_space=pltpu.SMEM)] * 2 + [vmem, vmem, pl.BlockSpec(memory_space=pl.ANY)],
        out_specs=(vmem,) * owners,
        scratch_shapes=[
            pltpu.VMEM(legendre.shape, jnp.float32),
            pltpu.SemaphoreType.DMA((slots,)),
            pltpu.VMEM((band_cycles, LANES), jnp.float32),
            pltpu.VMEM((2, 2, band_cycles, LANES), jnp.float32),
            pltpu.VMEM((owners, 2 * slots, degrees // owners), jnp.float32),
        ],
        compiler_params=pltpu.CompilerParams(vmem_limit_bytes=44 * 1024 * 1024),
        name="legendre_sums",
    )(me, orders, recv, head, legendre)


def exchange_and_sum(x, axis, count):
    parts = x.reshape(count, x.shape[0] // count, x.shape[1])
    return jnp.sum(lax.all_to_all(parts, axis, split_axis=0, concat_axis=0, tiled=True), axis=0)


def dense_filter(table, scan, resp):
    lines, length = scan.shape
    outer = length // LANES
    forward = table[:2 * LANES]
    c, s = table[2 * LANES:, :LANES], table[2 * LANES:, LANES:]
    k = jnp.arange(outer, dtype=jnp.int32)
    angle = 2.0 * jnp.pi / outer * (k[:, None] * k[None, :] % outer).astype(jnp.float32)
    x = scan.reshape(lines, outer, LANES)
    re = jnp.einsum("lna,nk->lka", x, jnp.cos(angle), precision=precise)
    im = -jnp.einsum("lna,nk->lka", x, jnp.sin(angle), precision=precise)
    spec = jnp.concatenate([re * c + im * s, im * c - re * s], axis=-1)
    spec = jnp.einsum("lki,ij->lkj", spec, forward, precision=precise)
    split = LANES // outer
    weight = resp.reshape(lines, outer, split, outer).transpose(0, 3, 2, 1).reshape(lines, outer, LANES)
    spec = spec * jnp.concatenate([weight, weight], axis=-1)
    spec = jnp.einsum("lki,ji->lkj", spec, forward, precision=precise)
    ur, ui = spec[..., :LANES], spec[..., LANES:]
    out = jnp.einsum("lka,kn->lna", ur * c - ui * s, jnp.cos(angle), precision=precise)
    out = out - jnp.einsum("lka,kn->lna", ui * c + ur * s, jnp.sin(angle), precision=precise)
    return (out / length).reshape(lines, length)


def dense_path(table, mode_table, scan_lines, response, cycle_offset, column, order_slot, band_cycles, det_count):
    filtered = dense_filter(table, scan_lines, response)
    flat_index = (cycle_offset * NPHI + column).reshape(-1)
    empty = jnp.zeros((band_cycles * NPHI,), jnp.float32)
    partial_value = empty.at[flat_index].add(filtered.reshape(-1)).reshape(band_cycles, NPHI)
    counts = empty.at[flat_index].add(1.0).reshape(band_cycles, NPHI)
    summed = exchange_and_sum(partial_value, "det", det_count)
    hit_total = exchange_and_sum(counts, "det", det_count)
    sky_map = summed / jnp.maximum(hit_total, 1.0)
    count, half = order_slot.shape[0], NPHI // 2
    tables = jnp.sum(mode_table.astype(jnp.float32), axis=0)
    first, second = sky_map[:, :half], sky_map[:, half:]
    modes = jnp.concatenate([
        jnp.dot(first + second, tables[0], precision=precise),
        jnp.dot(first - second, tables[1], precision=precise),
    ], axis=1)
    part = jnp.arange(2, dtype=jnp.int32)[:, None] * (count // 2)
    modes = modes[:, (order_slot & 1) * count + part + (order_slot >> 1)].transpose(1, 0, 2)
    slots = order_slot.shape[0] // det_count
    groups = LANES // (2 * slots)
    blocks = modes.reshape(2, groups, -1, det_count, slots).transpose(3, 2, 1, 0, 4)
    blocks = blocks.reshape(det_count, -1, LANES)
    return sky_map, lax.all_to_all(blocks, "det", split_axis=0, concat_axis=0, tiled=True)


def swap_blocks(blocks, axis):
    count = len(blocks)
    out = list(blocks)
    for k in range(count - 1, 0, -1):
        out[k] = lax.ppermute(blocks[k], axis, [(i, i ^ k) for i in range(count)])
    return out


def local(scan_lines, response, cycle_offset, column, order_slot, legendre, *, det_count, band_count):
    slots, band_cycles, degrees = legendre.shape
    me = lax.axis_index("det").astype(jnp.int32).reshape(1)
    table = jnp.asarray(filter_tables(scan_lines.shape[1]))
    mode_table = jnp.asarray(mode_tables(order_slot.shape[0]))
    *send, mode_copy = filter_and_sort(
        me, table, mode_table, scan_lines, response, cycle_offset, column, det_count, band_cycles
    )
    recv = swap_blocks(send, "det")
    sky_map, modes, crowded, head = bin_and_modes(mode_copy, legendre, recv[::-1], order_slot, band_cycles)
    modes = lax.all_to_all(modes, "det", split_axis=0, concat_axis=0, tiled=True)
    sky_map, modes = lax.cond(
        crowded[0] > 0,
        lambda: dense_path(
            table, mode_table, scan_lines, response, cycle_offset, column, order_slot, band_cycles, det_count
        ),
        lambda: (sky_map, modes),
    )
    band = lax.axis_index("band").astype(jnp.int32)
    local_orders = lax.dynamic_slice_in_dim(order_slot, lax.axis_index("det") * slots, slots, 0)
    terms = legendre_sums(band.reshape(1), local_orders, modes, head, legendre, band_count)
    terms = swap_blocks(terms, "band")
    sums = functools.reduce(jnp.add, terms[::-1])
    width = degrees // band_count
    degree = band * width + jnp.arange(width, dtype=jnp.int32)
    keep = degree[None, None, :] >= local_orders[None, :, None]
    return jnp.where(keep, sums.reshape(2, slots, width), 0.0), sky_map


def solution(mesh):
    sizes = dict(mesh.shape)
    return jax.shard_map(
        functools.partial(local, det_count=sizes["det"], band_count=sizes["band"]),
        mesh=mesh,
        in_specs=(
            P(("det", "band"), None),
            P(("det", "band"), None),
            P(("det", "band"), None),
            P(("det", "band"), None),
            P(),
            P("det", "band", None),
        ),
        out_specs=(P(None, "det", "band"), P(("band", "det"), None)),
        check_vma=False,
    )
```

```python
import functools

import jax
import jax.numpy as jnp
import numpy as np
from jax import lax
from jax.experimental import pallas as pl
from jax.experimental.pallas import tpu as pltpu
from jax.sharding import PartitionSpec as P

NPHI = 2048
LANES = 128
SUB = 8
WINDOWS = 2
ROW = 256
PIECE, PIECES, STEP, TOP = jnp.float8_e4m3fn, 3, 32.0, 224.0
KEEP = 2.0**20 + 1.0

precise = lax.Precision.HIGHEST
NT = (((1,), (1,)), ((), ()))


def filter_tables(length):
    outer = length // LANES
    k1 = np.arange(outer)[:, None]
    n2 = np.arange(LANES)[None, :]
    turn = 2.0 * np.pi * ((k1 * n2) % length) / length
    twiddle = np.concatenate([np.cos(turn), np.sin(turn)], axis=1)
    a = np.arange(LANES)
    angle = 2.0 * np.pi * (np.outer(a, a) % LANES) / LANES
    c, s = np.cos(angle), np.sin(angle)
    order = (a % outer) * (LANES // outer) + a // outer
    c, s = c[:, order], s[:, order]
    forward = np.block([[c, -s], [s, c]])
    return np.concatenate([forward, twiddle]).astype(np.float32)


def mode_tables(count):
    half = NPHI // 2
    p = np.arange(half)[:, None]
    out = []
    for parity in (0, 1):
        m = 2 * np.arange(count // 2)[None, :] + parity
        angle = 2.0 * np.pi * ((p * m) % NPHI) / NPHI
        out.append(np.concatenate([np.cos(angle), -np.sin(angle)], axis=1))
    table = np.stack(out).astype(np.float32)
    high = table.astype(jnp.bfloat16)
    low = (table - high.astype(np.float32)).astype(jnp.bfloat16)
    return np.stack([high, low])


def small_fft(re, im, sign):
    count = len(re)
    if count == 1:
        return re, im
    even_re, even_im = small_fft(re[0::2], None if im is None else im[0::2], sign)
    odd_re, odd_im = small_fft(re[1::2], None if im is None else im[1::2], sign)
    half = count // 2
    out_re, out_im = [None] * count, [None] * count
    for k in range(half):
        wr = float(np.cos(2 * np.pi * k / count))
        wi = float(sign * np.sin(2 * np.pi * k / count))
        er, ei, orr, oi = even_re[k], even_im and even_im[k], odd_re[k], odd_im and odd_im[k]
        if k == 0:
            tr, ti = orr, oi
        elif 4 * k == count:
            tr = None if oi is None else -wi * oi
            ti = wi * orr
        elif oi is None:
            tr, ti = wr * orr, wi * orr
        else:
            tr, ti = wr * orr - wi * oi, wr * oi + wi * orr
        out_re[k] = er if tr is None else er + tr
        out_re[k + half] = er if tr is None else er - tr
        if ti is None:
            out_im[k] = out_im[k + half] = ei
        else:
            out_im[k] = ti if ei is None else ei + ti
            out_im[k + half] = -ti if ei is None else ei - ti
    if all(x is None for x in out_im):
        return out_re, None
    out_im = [jnp.zeros_like(out_re[0]) if x is None else x for x in out_im]
    return out_re, out_im


class Places:
    def __init__(self, tile_bits, total_bits):
        self.tile_bits, self.total_bits = tile_bits, total_bits
        self.of = list(range(total_bits))
        for level in range(tile_bits + 1, total_bits + 1):
            self.walk(level)
        held = [self.of.index(place) for place in range(total_bits)]
        self.of = held

    def swap(self, bit):
        other = self.of.index(0)
        self.of[bit], self.of[other] = 0, self.of[bit]

    def walk(self, level):
        for bit in range(level - 1, self.tile_bits - 1, -1):
            self.swap(bit)
        self.swap(0)

    def axis_distance(self, bit):
        place = self.of[bit] - self.tile_bits
        return (0, 1 << place) if place < 3 else (1, 1 << (place - 3))

    def mask(self, bit):
        axis, distance = self.axis_distance(bit)
        return (lax.broadcasted_iota(jnp.int32, (SUB, LANES), axis) & distance) != 0


def trade(low, high, upper, axis, distance):
    axis += low.ndim - 2
    size = low.shape[axis]
    return (
        jnp.where(upper, pltpu.roll(high, distance, axis=axis), low),
        jnp.where(upper, high, pltpu.roll(low, size - distance, axis=axis)),
    )


def exchange(keys, vals, a, b, down):
    if down:
        a, b = b, a
    swap = keys[a] > keys[b]
    keys[a], keys[b] = jnp.minimum(keys[a], keys[b]), jnp.maximum(keys[a], keys[b])
    vals[a], vals[b] = jnp.where(swap, vals[b], vals[a]), jnp.where(swap, vals[a], vals[b])


def sort_registers(keys, vals):
    tiles = len(keys)
    tile_bits = tiles.bit_length() - 1
    places = Places(tile_bits, tile_bits + 10)

    def flip(bit):
        return jnp.where(places.mask(bit), -1.0, 1.0)

    def trade_all(bit):
        upper, (axis, distance) = places.mask(bit), places.axis_distance(bit)
        places.swap(bit)
        for i in range(0, tiles, 2):
            keys[i], keys[i + 1] = trade(keys[i], keys[i + 1], upper, axis, distance)
            vals[i], vals[i + 1] = trade(vals[i], vals[i + 1], upper, axis, distance)

    for level in range(1, places.total_bits + 1):
        if level >= tile_bits:
            sign = 1.0
            if level > tile_bits:
                sign = flip(level - 1)
            if level < places.total_bits:
                sign = sign * flip(level)
            for i in range(tiles):
                keys[i] = keys[i] * sign
        for bit in range(level - 1, -1, -1):
            if bit >= tile_bits or (bit == 0 and level > tile_bits):
                trade_all(bit)
            step = 1 << bit if bit < tile_bits else 1
            for i in range(tiles):
                if not i & step:
                    exchange(keys, vals, i, i + step, level < tile_bits and (i >> level) & 1 == 1)
    assert places.of == list(range(places.total_bits))


def split2(x):
    high = x.astype(jnp.bfloat16)
    low = (x - high.astype(jnp.float32)).astype(jnp.bfloat16)
    return high, low


def three_products(left, right, dims):
    dot = functools.partial(lax.dot_general, dimension_numbers=dims, preferred_element_type=jnp.float32)
    return dot(left[0], right[0]) + (dot(left[1], right[0]) + dot(left[0], right[1]))


def sort_kernel(
    me_ref, scan_hbm, resp_hbm, cycle_hbm, column_hbm, table_hbm, modes_hbm, *refs,
    buckets, span, rows, windows,
):
    send_refs, refs = refs[:buckets // windows], refs[buckets // windows:]
    modes_ref, refs = refs[0], refs[1:]
    scan_ref, resp_ref, cycle_ref, column_ref, table_ref, arrived = refs[:6]
    key_ref, val_ref, spec_ref, key_rows, val_rows = refs[6:]
    lines, length = scan_ref.shape
    outer = length // LANES
    loads = [
        pltpu.make_async_copy(source, place, arrived.at[i])
        for i, (source, place) in enumerate([
            (scan_hbm, scan_ref), (table_hbm, table_ref), (resp_hbm, resp_ref),
            (cycle_hbm, cycle_ref), (column_hbm, column_ref), (modes_hbm, modes_ref),
        ])
    ]
    for load in loads:
        load.start()
    def twiddle_row(k):
        at = 2 * LANES + k
        return table_ref[at:at + 1, :LANES], table_ref[at:at + 1, LANES:]

    loads[0].wait()
    re, im = small_fft([scan_ref[:, n * LANES:(n + 1) * LANES] for n in range(outer)], None, -1)
    loads[1].wait()
    forward = table_ref[:2 * LANES, :]
    for k in range(outer):
        c, s = twiddle_row(k)
        here = pl.ds(k * lines, lines)
        spec_ref[here, :LANES] = re[k] * c + im[k] * s
        spec_ref[here, LANES:] = im[k] * c - re[k] * s
    for load in loads[2:-1]:
        load.wait()
    forward_pieces = split2(forward)
    spec = three_products(split2(spec_ref[...]), forward_pieces, (((1,), (0,)), ((), ())))
    resp = [resp_ref[:, n * LANES:(n + 1) * LANES] * (1.0 / length) for n in range(outer)]
    step = 1
    while step < outer:
        upper = (lax.broadcasted_iota(jnp.int32, (lines, LANES), 1) & step) != 0
        for n in range(outer):
            if not n & step:
                resp[n], resp[n + step] = trade(resp[n], resp[n + step], upper, 1, step)
        step *= 2
    resp = jnp.concatenate(resp, axis=0)
    spec = spec * jnp.concatenate([resp, resp], axis=1)
    spec_ref[...] = three_products(split2(spec), forward_pieces, NT)
    re, im = [], []
    for k in range(outer):
        c, s = twiddle_row(k)
        here = pl.ds(k * lines, lines)
        ur, ui = spec_ref[here, :LANES], spec_ref[here, LANES:]
        re.append(ur * c - ui * s)
        im.append(ui * c + ur * s)
    out, _ = small_fft(re, im, 1)
    keys = []
    for n in range(outer):
        cols = slice(n * LANES, (n + 1) * LANES)
        keys.append((cycle_ref[:, cols] * NPHI + column_ref[:, cols]).astype(jnp.float32))
    vals = list(out)
    sort_registers(keys, vals)
    row_len = outer * SUB
    last = functools.reduce(jnp.maximum, keys)
    first = functools.reduce(jnp.minimum, keys)
    last = jnp.max(last, axis=0, keepdims=True)
    first = jnp.min(first, axis=0, keepdims=True)
    for i in range(outer):
        key_ref[i * SUB:(i + 1) * SUB, :] = keys[i]
        val_ref[i * SUB:(i + 1) * SUB, :] = vals[i]
    key_rows[:LANES, :] = key_ref[...].T
    val_rows[:LANES, :] = val_ref[...].T
    reach = key_rows.shape[0] - LANES
    key_rows[LANES:, :] = jnp.full((reach, row_len), 2.0 * buckets * span, jnp.float32)
    val_rows[LANES:, :] = jnp.zeros((reach, row_len), jnp.float32)
    over = jnp.int32(0)
    for k, send_ref in enumerate(send_refs):
        for w in range(windows):
            bucket = (me_ref[0] ^ k) * windows + w
            low = (bucket * span).astype(jnp.float32)
            high = low + float(span)
            begin = jnp.sum((last < low).astype(jnp.float32)).astype(jnp.int32)
            end = jnp.sum((first < high).astype(jnp.float32)).astype(jnp.int32)
            over = over + (end - begin > rows).astype(jnp.int32)
            begin = jnp.minimum(begin, LANES)
            aligned = pl.multiple_of((begin // SUB) * SUB, SUB)
            back = lax.rem(reach - (begin - aligned), reach)
            here = pl.ds(aligned, reach)
            taken = pltpu.roll(key_rows[here, :], back, axis=0)[:rows]
            send_ref[w * rows:(w + 1) * rows, :] = taken - low
            at = (windows + w) * rows
            send_ref[at:at + rows, :] = pltpu.roll(val_rows[here, :], back, axis=0)[:rows]

    @pl.when(over > 0)
    def _():
        for send_ref in send_refs:
            send_ref[...] = jnp.full(send_ref.shape, jnp.nan, jnp.float32)

    loads[-1].wait()


def filter_and_sort(me, table, mode_table, scan, resp, cycle, column, det_count, band_cycles):
    lines, length = scan.shape
    tiles = length // LANES
    windows = WINDOWS
    buckets = det_count * windows
    span = band_cycles * NPHI // buckets
    row_len = tiles * SUB
    rows = LANES // buckets + 2
    reach = (rows + 2 * SUB - 2) // SUB * SUB
    operands = [scan, resp, cycle, column, table]
    body = functools.partial(sort_kernel, buckets=buckets, span=span, rows=rows, windows=windows)
    vmem = pl.BlockSpec(memory_space=pltpu.VMEM)
    return pl.pallas_call(
        body,
        out_shape=(jax.ShapeDtypeStruct((2 * windows * rows, row_len), jnp.float32),) * det_count
        + (jax.ShapeDtypeStruct(mode_table.shape, mode_table.dtype),),
        in_specs=[pl.BlockSpec(memory_space=pltpu.SMEM)]
        + [pl.BlockSpec(memory_space=pl.ANY)] * (len(operands) + 1),
        out_specs=(vmem,) * (det_count + 1),
        scratch_shapes=[pltpu.VMEM(x.shape, x.dtype) for x in operands] + [
            pltpu.SemaphoreType.DMA((len(operands) + 1,)),
            pltpu.VMEM((row_len, LANES), jnp.float32),
            pltpu.VMEM((row_len, LANES), jnp.float32),
            pltpu.VMEM((tiles * lines, 2 * LANES), jnp.float32),
            pltpu.VMEM((LANES + reach, row_len), jnp.float32),
            pltpu.VMEM((LANES + reach, row_len), jnp.float32),
        ],
        compiler_params=pltpu.CompilerParams(vmem_limit_bytes=24 * 1024 * 1024),
        name="filter_sort",
    )(me, *operands, mode_table)


def bin_kernel(
    *refs, sources, windows, rows, window_cycles
):
    recv_refs, (pick_ref, table_ref, map_ref, send_ref, flag_ref) = refs[:sources], refs[sources:-6]
    recv_ref, left_a, left_b, right_a, right_b, acc_ref = refs[-6:]
    for e in range(sources):
        recv_ref[e] = recv_refs[e][...]
    left_refs, right_refs = (left_a, left_b), (right_a, right_b)
    row_len = recv_ref.shape[2]
    parts = NPHI // ROW
    area = parts * window_cycles
    a_iota = lax.broadcasted_iota(jnp.int32, (area, row_len), 0).astype(jnp.int8)
    b_iota = (lax.broadcasted_iota(jnp.int32, (ROW, row_len), 0) - ROW // 2).astype(jnp.int8)
    zero, one = jnp.zeros((), PIECE), jnp.ones((), PIECE)
    values = recv_ref[:, windows * rows:, :]
    largest = jnp.max(jnp.max(jnp.abs(values), axis=0), axis=(0, 1), keepdims=True)
    scale = jnp.where(largest > 0.0, TOP / largest, 1.0)

    def build(e, w, slot):
        left, right = left_refs[slot], right_refs[slot]
        for r in range(rows):
            q = recv_ref[e, w * rows + r:w * rows + r + 1, :].astype(jnp.int32)
            rest = recv_ref[e, (windows + w) * rows + r:(windows + w) * rows + r + 1, :] * scale
            cycle = q >> 11
            inside = (q >= 0) & (cycle < window_cycles)
            a = jnp.where(inside, ((q >> 8) & (parts - 1)) * window_cycles + cycle, -1).astype(jnp.int8)
            b = ((q & (ROW - 1)) - ROW // 2).astype(jnp.int8)
            cols = slice(r * row_len, (r + 1) * row_len)
            hit = a_iota == a
            for p in range(PIECES):
                spread = rest * KEEP
                piece = (spread - (spread - rest)).astype(PIECE)
                rest = (rest - piece.astype(jnp.float32)) * STEP
                left[p * area:(p + 1) * area, cols] = jnp.where(hit, piece, zero)
            left[PIECES * area:, cols] = jnp.where(hit, one, zero)
            right[:, cols] = jnp.where(b_iota == b, one, zero)

    def multiply(slot):
        acc_ref[...] += lax.dot_general(
            left_refs[slot][...], right_refs[slot][...], NT, preferred_element_type=jnp.float32
        )

    build(0, 0, 0)
    for w in range(windows):
        acc_ref[...] = jnp.zeros(acc_ref.shape, jnp.float32)

        def body(i, carry):
            build(2 * i + 1, w, 1)
            multiply(0)
            build(jnp.minimum(2 * i + 2, sources - 1), w, 0)
            multiply(1)
            return carry

        lax.fori_loop(0, sources // 2 - 1, body, 0)
        build(sources - 1, w, 1)
        multiply(0)
        if w + 1 < windows:
            build(0, w + 1, 0)
        multiply(1)
        acc = acc_ref[...]
        total = acc[(PIECES - 1) * area:PIECES * area]
        for p in range(PIECES - 2, -1, -1):
            total = acc[p * area:(p + 1) * area] + total * (1.0 / STEP)
        sky = total / scale / jnp.maximum(acc[PIECES * area:], 1.0)
        for c8 in range(parts):
            map_ref[w * window_cycles:(w + 1) * window_cycles, c8 * ROW:(c8 + 1) * ROW] = (
                sky[c8 * window_cycles:(c8 + 1) * window_cycles]
            )
    cycles = map_ref.shape[0]
    half = NPHI // 2
    modes = []
    for parity in (0, 1):
        a, b = map_ref[:, :half], map_ref[:, half:]
        high, low = split2(a + b if parity == 0 else a - b)
        first = jnp.dot(jnp.concatenate([high, low], axis=0), table_ref[0, parity], preferred_element_type=jnp.float32)
        second = jnp.dot(high, table_ref[1, parity], preferred_element_type=jnp.float32)
        modes.append(first[:cycles] + first[cycles:] + second)
    modes = jnp.concatenate(modes, axis=1)
    count = modes.shape[1]
    width = pick_ref.shape[1]
    high = modes.astype(jnp.bfloat16)
    rest = modes - high.astype(jnp.float32)
    middle = rest.astype(jnp.bfloat16)
    low = (rest - middle.astype(jnp.float32)).astype(jnp.bfloat16)
    pieces = jnp.concatenate([high, middle, low], axis=0)
    choose = (lax.broadcasted_iota(jnp.int32, (count, width), 0) == pick_ref[...])
    choose = jnp.where(choose, 1.0, 0.0).astype(jnp.bfloat16)
    moved = jnp.dot(pieces, choose, preferred_element_type=jnp.float32)
    moved = moved[:cycles] + moved[cycles:2 * cycles] + moved[2 * cycles:]
    owners, group_rows, lanes = send_ref.shape
    groups = cycles // group_rows
    lane_group = lax.broadcasted_iota(jnp.int32, (group_rows, lanes), 1) // (lanes // groups)
    flag_ref[0] = (jnp.max(jnp.where(values == values, 0.0, 1.0)) > 0.0).astype(jnp.int32)
    for d in range(owners):
        block = moved[:, d * lanes:(d + 1) * lanes]
        out = block[:group_rows]
        for h in range(1, groups):
            out = jnp.where(lane_group == h, block[h * group_rows:(h + 1) * group_rows], out)
        send_ref[d] = out


def bin_and_modes(mode_table, recv, order_slot, band_cycles):
    sources = len(recv)
    lines, row_len = recv[0].shape
    windows = WINDOWS
    rows = lines // (2 * windows)
    cycles = band_cycles // sources
    count = order_slot.shape[0]
    slots = count // sources
    groups = LANES // (2 * slots)
    m = order_slot.reshape(sources, 1, 1, slots)
    part = jnp.arange(2, dtype=jnp.int32).reshape(1, 1, 2, 1)
    pick = (m & 1) * count + part * (count // 2) + (m >> 1)
    pick = jnp.broadcast_to(pick, (sources, groups, 2, slots)).reshape(1, sources * LANES)
    area = cycles // windows * (NPHI // ROW)
    depth = rows * row_len
    vmem = pl.BlockSpec(memory_space=pltpu.VMEM)
    return pl.pallas_call(
        functools.partial(bin_kernel, sources=sources, windows=windows, rows=rows, window_cycles=cycles // windows),
        out_shape=(
            jax.ShapeDtypeStruct((cycles, NPHI), jnp.float32),
            jax.ShapeDtypeStruct((sources, cycles // groups, LANES), jnp.float32),
            jax.ShapeDtypeStruct((1,), jnp.int32),
        ),
        in_specs=[vmem] * (sources + 2),
        out_specs=(vmem, vmem, pl.BlockSpec(memory_space=pltpu.SMEM)),
        scratch_shapes=[
            pltpu.VMEM((sources, lines, row_len), jnp.float32),
            pltpu.VMEM(((PIECES + 1) * area, depth), PIECE),
            pltpu.VMEM(((PIECES + 1) * area, depth), PIECE),
            pltpu.VMEM((ROW, depth), PIECE),
            pltpu.VMEM((ROW, depth), PIECE),
            pltpu.VMEM(((PIECES + 1) * area, ROW), jnp.float32),
        ],
        compiler_params=pltpu.CompilerParams(vmem_limit_bytes=40 * 1024 * 1024),
        name="bin_modes",
    )(*recv, pick, mode_table)


def legendre_kernel(me_ref, order_ref, recv_ref, table_ref, *refs, owners):
    out_refs, (leg_ref, arrived, modes_ref, wide_ref, sums_ref) = refs[:owners], refs[owners:]
    slots, band_cycles, degrees = table_ref.shape

    def load(slot, act):
        skip = order_ref[slot] >= LANES

        @pl.when(skip)
        def _():
            upper = pl.ds(LANES, degrees - LANES)
            act(pltpu.make_async_copy(
                table_ref.at[slot, :, upper], leg_ref.at[slot, :, upper], arrived.at[slot]
            ))

        @pl.when(jnp.logical_not(skip))
        def _():
            act(pltpu.make_async_copy(table_ref.at[slot], leg_ref.at[slot], arrived.at[slot]))

    def start(slot, carry):
        load(slot, lambda copy: copy.start())
        return carry

    lax.fori_loop(0, slots, start, 0)
    sources, group_rows, lanes = recv_ref.shape
    groups = lanes // (2 * slots)
    width = out_refs[0].shape[1]
    tiles = degrees // LANES
    for e in range(sources):
        block = recv_ref[e]
        for h in range(groups):
            at = (e * groups + h) * group_rows
            turned = block if h == 0 else pltpu.roll(block, lanes - h * 2 * slots, axis=1)
            modes_ref[at:at + group_rows, :] = turned

    def widen(slot, half):
        turned = pltpu.roll(modes_ref[...], lax.rem(lanes - slot, lanes), axis=1)
        for c in range(2):
            column = turned[:, c * slots:c * slots + 1]
            wide_ref[half, c] = jnp.broadcast_to(column, (band_cycles, lanes))

    widen(0, 0)

    def body(slot, carry):
        half = slot & 1
        load(slot, lambda copy: copy.wait())
        sums = [[jnp.zeros((SUB, LANES), jnp.float32) for _ in range(tiles)] for _ in range(2)]
        for r in range(0, band_cycles, SUB):
            factor = [wide_ref[half, c, r:r + SUB, :] for c in range(2)]
            for t in range(tiles):
                block = leg_ref[slot, r:r + SUB, t * LANES:(t + 1) * LANES]
                for c in range(2):
                    sums[c][t] = sums[c][t] + block * factor[c]
        widen(jnp.minimum(slot + 1, slots - 1), 1 - half)
        per_owner = width // LANES
        for c in range(2):
            lines = [jnp.sum(part, axis=0, keepdims=True) for part in sums[c]]
            for d in range(owners):
                line = jnp.concatenate(lines[d * per_owner:(d + 1) * per_owner], axis=1)
                sums_ref[d, pl.ds(c * slots + slot, 1), :] = line
        return carry

    lax.fori_loop(0, slots, body, 0)
    for k in range(owners):
        out_refs[k][...] = sums_ref[me_ref[0] ^ k]


def legendre_sums(me, orders, recv, legendre, owners):
    slots, band_cycles, degrees = legendre.shape
    vmem = pl.BlockSpec(memory_space=pltpu.VMEM)
    return pl.pallas_call(
        functools.partial(legendre_kernel, owners=owners),
        out_shape=(jax.ShapeDtypeStruct((2 * slots, degrees // owners), jnp.float32),) * owners,
        in_specs=[pl.BlockSpec(memory_space=pltpu.SMEM)] * 2 + [vmem, pl.BlockSpec(memory_space=pl.ANY)],
        out_specs=(vmem,) * owners,
        scratch_shapes=[
            pltpu.VMEM(legendre.shape, jnp.float32),
            pltpu.SemaphoreType.DMA((slots,)),
            pltpu.VMEM((band_cycles, LANES), jnp.float32),
            pltpu.VMEM((2, 2, band_cycles, LANES), jnp.float32),
            pltpu.VMEM((owners, 2 * slots, degrees // owners), jnp.float32),
        ],
        compiler_params=pltpu.CompilerParams(vmem_limit_bytes=44 * 1024 * 1024),
        name="legendre_sums",
    )(me, orders, recv, legendre)


def exchange_and_sum(x, axis, count):
    parts = x.reshape(count, x.shape[0] // count, x.shape[1])
    return jnp.sum(lax.all_to_all(parts, axis, split_axis=0, concat_axis=0, tiled=True), axis=0)


def dense_filter(table, scan, resp):
    lines, length = scan.shape
    outer = length // LANES
    forward = table[:2 * LANES]
    c, s = table[2 * LANES:, :LANES], table[2 * LANES:, LANES:]
    k = jnp.arange(outer, dtype=jnp.int32)
    angle = 2.0 * jnp.pi / outer * (k[:, None] * k[None, :] % outer).astype(jnp.float32)
    x = scan.reshape(lines, outer, LANES)
    re = jnp.einsum("lna,nk->lka", x, jnp.cos(angle), precision=precise)
    im = -jnp.einsum("lna,nk->lka", x, jnp.sin(angle), precision=precise)
    spec = jnp.concatenate([re * c + im * s, im * c - re * s], axis=-1)
    spec = jnp.einsum("lki,ij->lkj", spec, forward, precision=precise)
    split = LANES // outer
    weight = resp.reshape(lines, outer, split, outer).transpose(0, 3, 2, 1).reshape(lines, outer, LANES)
    spec = spec * jnp.concatenate([weight, weight], axis=-1)
    spec = jnp.einsum("lki,ji->lkj", spec, forward, precision=precise)
    ur, ui = spec[..., :LANES], spec[..., LANES:]
    out = jnp.einsum("lka,kn->lna", ur * c - ui * s, jnp.cos(angle), precision=precise)
    out = out - jnp.einsum("lka,kn->lna", ui * c + ur * s, jnp.sin(angle), precision=precise)
    return (out / length).reshape(lines, length)


def dense_path(table, mode_table, scan_lines, response, cycle_offset, column, order_slot, band_cycles, det_count):
    filtered = dense_filter(table, scan_lines, response)
    flat_index = (cycle_offset * NPHI + column).reshape(-1)
    empty = jnp.zeros((band_cycles * NPHI,), jnp.float32)
    partial_value = empty.at[flat_index].add(filtered.reshape(-1)).reshape(band_cycles, NPHI)
    counts = empty.at[flat_index].add(1.0).reshape(band_cycles, NPHI)
    summed = exchange_and_sum(partial_value, "det", det_count)
    hit_total = exchange_and_sum(counts, "det", det_count)
    sky_map = summed / jnp.maximum(hit_total, 1.0)
    count, half = order_slot.shape[0], NPHI // 2
    tables = jnp.sum(mode_table.astype(jnp.float32), axis=0)
    first, second = sky_map[:, :half], sky_map[:, half:]
    modes = jnp.concatenate([
        jnp.dot(first + second, tables[0], precision=precise),
        jnp.dot(first - second, tables[1], precision=precise),
    ], axis=1)
    part = jnp.arange(2, dtype=jnp.int32)[:, None] * (count // 2)
    modes = modes[:, (order_slot & 1) * count + part + (order_slot >> 1)].transpose(1, 0, 2)
    slots = order_slot.shape[0] // det_count
    groups = LANES // (2 * slots)
    blocks = modes.reshape(2, groups, -1, det_count, slots).transpose(3, 2, 1, 0, 4)
    blocks = blocks.reshape(det_count, -1, LANES)
    return sky_map, lax.all_to_all(blocks, "det", split_axis=0, concat_axis=0, tiled=True)


def swap_blocks(blocks, axis):
    count = len(blocks)
    out = list(blocks)
    for k in range(count - 1, 0, -1):
        out[k] = lax.ppermute(blocks[k], axis, [(i, i ^ k) for i in range(count)])
    return out


def local(scan_lines, response, cycle_offset, column, order_slot, legendre, *, det_count, band_count):
    slots, band_cycles, degrees = legendre.shape
    me = lax.axis_index("det").astype(jnp.int32).reshape(1)
    table = jnp.asarray(filter_tables(scan_lines.shape[1]))
    mode_table = jnp.asarray(mode_tables(order_slot.shape[0]))
    *send, mode_copy = filter_and_sort(
        me, table, mode_table, scan_lines, response, cycle_offset, column, det_count, band_cycles
    )
    recv = swap_blocks(send, "det")
    sky_map, modes, crowded = bin_and_modes(mode_copy, recv[::-1], order_slot, band_cycles)
    modes = lax.all_to_all(modes, "det", split_axis=0, concat_axis=0, tiled=True)
    sky_map, modes = lax.cond(
        crowded[0] > 0,
        lambda: dense_path(
            table, mode_table, scan_lines, response, cycle_offset, column, order_slot, band_cycles, det_count
        ),
        lambda: (sky_map, modes),
    )
    band = lax.axis_index("band").astype(jnp.int32)
    local_orders = lax.dynamic_slice_in_dim(order_slot, lax.axis_index("det") * slots, slots, 0)
    terms = swap_blocks(legendre_sums(band.reshape(1), local_orders, modes, legendre, band_count), "band")
    sums = functools.reduce(jnp.add, terms[::-1])
    width = degrees // band_count
    degree = band * width + jnp.arange(width, dtype=jnp.int32)
    keep = degree[None, None, :] >= local_orders[None, :, None]
    return jnp.where(keep, sums.reshape(2, slots, width), 0.0), sky_map


def solution(mesh):
    sizes = dict(mesh.shape)
    return jax.shard_map(
        functools.partial(local, det_count=sizes["det"], band_count=sizes["band"]),
        mesh=mesh,
        in_specs=(
            P(("det", "band"), None),
            P(("det", "band"), None),
            P(("det", "band"), None),
            P(("det", "band"), None),
            P(),
            P("det", "band", None),
        ),
        out_specs=(P(None, "det", "band"), P(("band", "det"), None)),
        check_vma=False,
    )
```
